32 devices in a mesh: stream: 2 (over core), azim: 16 (over z, y, x).
Axes of the slice: x: 2, y: 2, z: 4, core: 2. Of those that a mesh axis runs over, the one named last changes fastest.
Arguments:
- surface_signal: bfloat16 [64, 65536], P(None, ('stream', 'azim')), may hold values from -6 to 6
- retarded_weights: bfloat16 [512, 64, 64], P(('stream', 'azim')), may hold values from -0.75 to 0.75
- radiation_weights: bfloat16 [1024, 65536], P(None, ('stream', 'azim')), may hold values from -0.046875 to 0.046875
- target_signal: float32 [64, 1024], replicated, may hold values from -6 to 6
- observer_weights: float32 [1024], replicated, may hold values from 0.5 to 2
- sample_weights: float32 [64], replicated, may hold values from 1 to 8
- host_element: int32 [65536], P(('stream', 'azim')), may hold values from 0 to 4095
- source_profile: float32 [320], replicated, may hold values from -6 to 6
- adjoint_state: bfloat16 [320, 8, 64, 256], P(None, 'stream', 'azim'), may hold values from -6 to 6
- volume_operator: bfloat16 [320, 320], replicated, may hold values from -0.3125 to 0.3125
- lift_operator: bfloat16 [320, 480], replicated, may hold values from -0.25 to 0.25
Outputs:
- obs_sens: float32 [64, 1024], P(None, 'azim')
- adjoint_next: float32 [320, 8, 64, 256], P(None, 'stream', 'azim')
The draws below stay inside these ranges and needn't reach their ends.
Inputs may be any that keep to these rules, and one draw needn't show every extreme that they name: host_element[i] numbers an element among the 4 x 4 x 256 elements of the device block that holds surface point i, as (x 4 + a) * 256 + r in that block.
All inputs are finite; a program needn't handle non-finite values.
Results may differ from the reference program's by a relative error of at most 0.0039.
Values may be sent and summed in bfloat16 or wider, within the bound.
No kernel may reach another device: no remote copies, remote signals or barrier semaphores. Data moves between devices by JAX's collectives and lax.ppermute only.
A program may use at most 64 MiB of HBM per device.

```python
import math
import jax
import jax.numpy as jnp
from jax import lax

OBS = 1024
TW = 64
NVAR = 5
NODE = 4
BLK = 128
SURF_DEV = 2048
EXD = 4
EAD = 4
ER = 256
COMP = 320
FACE = 80
SURF = 65536
NBLK = 512
NX = 8
NA = 64
N_AZIM = 16


def set_ends(entries, rng, least, top_value):
    index_at = [jax.random.randint(jax.random.fold_in(rng, axis), (), 0, length) for axis, length in enumerate(entries.shape)]
    widest = entries.shape.index(max(entries.shape))
    next_to = index_at[:widest] + [(index_at[widest] + 1) % entries.shape[widest]] + index_at[widest + 1:]
    return entries.at[tuple(index_at)].set(least).at[tuple(next_to)].set(top_value)


def spiked(values, key, source, target, blocks, factor):
    def block_of(dim):
        return (jnp.arange(values.shape[dim]) // (values.shape[dim] // blocks)).reshape((-1,) + (1,) * (values.ndim - 1 - dim))

    one_side = jax.random.permutation(key, blocks)[block_of(target)]
    second = (block_of(target) + blocks // 2) % blocks
    return jnp.where((block_of(source) == one_side) | (block_of(source) == second), factor * values, values)


def level_of(rng, shape, shards, smallest, top_value):
    loudness = 1.0
    for axis_at, blocks in shards:
        heights = jax.random.uniform(jax.random.fold_in(jax.random.fold_in(rng, 6), axis_at), (blocks,), jnp.float32, smallest / len(shards), top_value / len(shards))
        loudness = loudness * jnp.repeat(jnp.exp(heights), shape[axis_at] // blocks).reshape((-1,) + (1,) * (len(shape) - 1 - axis_at))
    return loudness


def gaussian(own_key, shape, scale, bound, cuts=(), kind=jnp.bfloat16):
    result = jax.random.normal(own_key, shape, jnp.float32) * scale
    if len(cuts) > 0:
        result = level_of(own_key, shape, cuts, -0.22, 0.18) * result
    return jnp.clip(result, min=-bound, max=bound).astype(kind)


def bell_draw_with(own_key, dims, scale, most, cuts, heavy, kind=jnp.bfloat16):
    entries = scale * jax.random.normal(own_key, dims, jnp.float32)
    if cuts:
        entries = entries * level_of(own_key, dims, cuts, -0.22, 0.18)
    return jnp.clip(spiked(entries, jax.random.fold_in(own_key, 3), *heavy), -most, most).astype(kind)


def setup_inputs(seed: int = 0) -> dict:
    keys = jax.random.split(jax.random.key(seed), 12)
    return {
        "surface_signal": gaussian(keys[0], (TW, SURF), 1.0, 6.0, ((1, 32),)),
        "retarded_weights": gaussian(keys[1], (NBLK, TW, TW), TW ** -0.5, 0.75, ((0, 32),)),
        "radiation_weights": bell_draw_with(keys[2], (OBS, SURF), SURF ** -0.5, 0.046875, ((1, 32),), (1, 0, 32, 2.75)),
        "target_signal": gaussian(keys[3], (TW, OBS), 1.0, 6.0, (), jnp.float32),
        "observer_weights": jnp.clip(jnp.exp(jax.random.uniform(keys[4], (OBS,), jnp.float32, math.log(0.5), math.log(2.0))), 0.5, 2.0),
        "sample_weights": jnp.clip(jnp.exp(jax.random.uniform(keys[5], (TW,), jnp.float32, math.log(1.0), math.log(8.0))), 1.0, 8.0),
        "host_element": set_ends(jax.random.randint(keys[6], (SURF,), 0, EXD * EAD * ER), jax.random.fold_in(keys[6], 1), 0, (EXD * EAD * ER) - 1).astype(jnp.int32),
        "source_profile": gaussian(keys[7], (COMP,), 1.0, 6.0, (), jnp.float32),
        "adjoint_state": gaussian(keys[8], (COMP, NX, NA, ER), 1.0, 6.0, ((1, 2), (2, 16))),
        "volume_operator": gaussian(keys[9], (COMP, COMP), COMP ** -0.5, 0.3125),
        "lift_operator": gaussian(keys[10], (COMP, 6 * FACE), (6 * FACE) ** -0.5, 0.25),
    }


def hann_taper(count):
    samples = jnp.arange(count, dtype=jnp.float32)
    return 0.5 - 0.5 * jnp.cos(2.0 * jnp.pi * (samples + 0.5) / count)


def plane_traces(plane):
    rest = plane.shape[1:]
    shaped = plane.reshape((NVAR, NODE, NODE, NODE) + rest)
    lower_axial = shaped[:, 0].reshape((FACE,) + rest)
    upper_axial = shaped[:, NODE - 1].reshape((FACE,) + rest)
    lower_sector = shaped[:, :, 0].reshape((FACE,) + rest)
    upper_sector = shaped[:, :, NODE - 1].reshape((FACE,) + rest)
    lower_radial = shaped[:, :, :, 0].reshape((FACE,) + rest)
    upper_radial = shaped[:, :, :, NODE - 1].reshape((FACE,) + rest)
    return lower_axial, upper_axial, lower_sector, upper_sector, lower_radial, upper_radial


def reference(surface_signal, retarded_weights, radiation_weights, target_signal, observer_weights, sample_weights, host_element, source_profile, adjoint_state, volume_operator, lift_operator):
    tapering = hann_taper(TW)
    blocked = surface_signal.reshape(TW, NBLK, BLK).astype(jnp.float32)
    delayed = jnp.einsum('bkt,kbs->tbs', retarded_weights.astype(jnp.float32), blocked)
    delayed_low = delayed.astype(jnp.bfloat16).reshape(TW, SURF)
    observer_signal = jnp.dot(delayed_low, radiation_weights.T, preferred_element_type=jnp.float32)
    obs_sens = observer_weights[None, :] * tapering[:, None] * (observer_signal - target_signal)
    sens_low = obs_sens.astype(jnp.bfloat16)
    spread = jnp.dot(sens_low, radiation_weights, preferred_element_type=jnp.float32)
    spread_low = spread.astype(jnp.bfloat16).reshape(TW, NBLK, BLK).astype(jnp.float32)
    source_time = jnp.einsum('bkt,tbs->kbs', retarded_weights.astype(jnp.float32), spread_low)
    strength = jnp.sum(source_time * sample_weights[:, None, None], axis=0).reshape(SURF)

    point_ids = jnp.arange(SURF, dtype=jnp.int32)
    device_ids = point_ids // SURF_DEV
    slab_ids = device_ids // N_AZIM
    sector_ids = device_ids % N_AZIM
    local_axial = host_element // (EAD * ER)
    local_sector = (host_element // ER) % EAD
    local_radial = host_element % ER
    flat_ids = ((slab_ids * EXD + local_axial) * NA + sector_ids * EAD + local_sector) * ER + local_radial
    element_source = jax.ops.segment_sum(strength, flat_ids.astype(jnp.int32), num_segments=NX * NA * ER)
    source_grid = element_source.reshape(NX, NA, ER)

    def plane_update(plane_index):
        current = lax.dynamic_index_in_dim(adjoint_state, plane_index, 1, keepdims=False)
        previous = lax.dynamic_index_in_dim(adjoint_state, jnp.maximum(plane_index - 1, 0), 1, keepdims=False)
        following = lax.dynamic_index_in_dim(adjoint_state, jnp.minimum(plane_index + 1, NX - 1), 1, keepdims=False)
        own_traces = plane_traces(current)
        from_lower_axial = jnp.where(plane_index > 0, plane_traces(previous)[1], jnp.zeros_like(own_traces[1]))
        from_upper_axial = jnp.where(plane_index < NX - 1, plane_traces(following)[0], jnp.zeros_like(own_traces[0]))
        from_lower_sector = jnp.roll(own_traces[3], 1, axis=1)
        from_upper_sector = jnp.roll(own_traces[2], -1, axis=1)
        zero_rim = jnp.zeros_like(own_traces[5][..., :1])
        from_lower_radial = jnp.concatenate([zero_rim, own_traces[5][..., :-1]], axis=2)
        from_upper_radial = jnp.concatenate([own_traces[4][..., 1:], zero_rim], axis=2)
        stacked = jnp.concatenate([from_lower_axial, from_upper_axial, from_lower_sector, from_upper_sector, from_lower_radial, from_upper_radial], axis=0).reshape(6 * FACE, NA * ER)
        flat_current = current.reshape(COMP, NA * ER)
        volume_term = jnp.dot(volume_operator, flat_current, preferred_element_type=jnp.float32)
        face_term = jnp.dot(lift_operator, stacked, preferred_element_type=jnp.float32)
        plane_source = lax.dynamic_index_in_dim(source_grid, plane_index, 0, keepdims=False).reshape(1, NA * ER)
        updated = flat_current.astype(jnp.float32) + volume_term + face_term + source_profile[:, None] * plane_source
        return updated.reshape(COMP, NA, ER)

    planes = lax.map(plane_update, jnp.arange(NX, dtype=jnp.int32))
    adjoint_next = jnp.transpose(planes, (1, 0, 2, 3))
    return obs_sens, adjoint_next
```

```python
import jax
import jax.numpy as jnp
import numpy as np
from jax import lax
from jax.experimental import pallas as pl
from jax.experimental.pallas import tpu as pltpu
from jax.sharding import PartitionSpec as P

NVAR = 5
NODE = 4
LANES = 128
F32 = jnp.float32
BF16 = jnp.bfloat16
MESH_AXES = ("stream", "azim")
VMEM = pl.BlockSpec(memory_space=pltpu.VMEM)
SMEM = pl.BlockSpec(memory_space=pltpu.SMEM)


def params(mib):
    return pltpu.CompilerParams(vmem_limit_bytes=mib * 2**20)


def cost(flops, nbytes):
    return pl.CostEstimate(flops=flops, bytes_accessed=nbytes, transcendentals=0)


def delay(weights_ref, signal_ref, delayed_ref):
    blocks = weights_ref.shape[0]
    width = signal_ref.shape[1] // blocks
    for b in range(blocks):
        columns = slice(b * width, (b + 1) * width)
        block = lax.dot_general(
            weights_ref[b],
            signal_ref[:, columns],
            (((0,), (0,)), ((), ())),
            preferred_element_type=F32,
        )
        delayed_ref[:, columns] = block.astype(BF16)


def project(delayed_ref, radiation_ref, out_ref):
    out_ref[...] = lax.dot_general(
        delayed_ref[...],
        radiation_ref[...],
        (((1,), (1,)), ((), ())),
        preferred_element_type=F32,
    )


def first_half_kernel(half_ref, signal_ref, weights_ref, radiation_ref, out_ref, delayed_ref):
    @pl.when(pl.program_id(0) == 0)
    def _():
        delay(weights_ref, signal_ref, delayed_ref)

    project(delayed_ref, radiation_ref, out_ref)


def second_half_kernel(half_ref, delayed_ref, radiation_ref, out_ref):
    project(delayed_ref, radiation_ref, out_ref)


def observer_half(kernel, half, operands, radiation, delayed_shape=None):
    observers, points = radiation.shape
    window = operands[0].shape[0]
    steps = 2
    rows = observers // 2 // steps
    whole = [pl.BlockSpec(x.shape, lambda i, h, n=x.ndim: (0,) * n) for x in operands]
    out_specs = [pl.BlockSpec((window, rows), lambda i, h: (0, i))]
    out_shape = [jax.ShapeDtypeStruct((window, observers // 2), F32)]
    if delayed_shape is not None:
        out_specs.append(pl.BlockSpec(delayed_shape, lambda i, h: (0, 0)))
        out_shape.append(jax.ShapeDtypeStruct(delayed_shape, BF16))
    return pl.pallas_call(
        kernel,
        grid_spec=pltpu.PrefetchScalarGridSpec(
            num_scalar_prefetch=1,
            grid=(steps,),
            in_specs=whole
            + [pl.BlockSpec((rows, points), lambda i, h: (h[0] * steps + i, 0))],
            out_specs=out_specs,
        ),
        out_shape=out_shape,
        compiler_params=params(24),
        cost_estimate=cost(window * observers * points, observers * points),
    )(half, *operands, radiation)


def flatten_kernel(sectors, state_ref, flat_ref, lo_ref, hi_ref, azlo_ref, azhi_ref, plane_ref):
    comps, planes, rows, lanes = state_ref.shape
    tiles = rows // sectors
    width = sectors * tiles * lanes
    for x in range(planes):
        plane_ref[...] = state_ref[:, x].astype(F32).reshape(comps * rows, lanes)
        for k in range(rows):
            j, a = divmod(k, sectors)
            first = x * width + (a * tiles + j) * lanes
            flat_ref[:, first : first + lanes] = plane_ref[
                pl.ds(k, comps, stride=rows), :
            ].astype(BF16)
    group = NODE * NODE
    for v in range(NVAR):
        low = v * NODE * group
        top = low + (NODE - 1) * group
        lo_ref[v * group : (v + 1) * group, :] = flat_ref[low : low + group, :width]
        hi_ref[v * group : (v + 1) * group, :] = flat_ref[
            top : top + group, (planes - 1) * width :
        ]
    faces = NVAR * group
    face = lax.broadcasted_iota(jnp.int32, (faces, comps), 0)
    comp = lax.broadcasted_iota(jnp.int32, (faces, comps), 1)
    base = (face // NODE) * group + face % NODE
    pick_low = (comp == base).astype(F32).astype(BF16)
    pick_top = (comp == base + (NODE - 1) * NODE).astype(F32).astype(BF16)
    block = tiles * lanes
    for x in range(planes):
        first = x * width
        last = first + (sectors - 1) * block
        azlo_ref[:, x * block : (x + 1) * block] = jnp.dot(
            pick_low, flat_ref[:, first : first + block], preferred_element_type=F32
        ).astype(BF16)
        azhi_ref[:, x * block : (x + 1) * block] = jnp.dot(
            pick_top, flat_ref[:, last : last + block], preferred_element_type=F32
        ).astype(BF16)


def operator_kernel(volume_ref, lift_ref, weights_ref, samples_ref, host_ref, op_ref, v_ref, hot_ref):
    comps = volume_ref.shape[0]
    group = NODE * NODE
    faces = NVAR * group
    op_ref[:, :comps] = volume_ref[...]
    op_ref[:, comps : comps + 2 * faces] = lift_ref[:, : 2 * faces]
    face = lax.broadcasted_iota(jnp.int32, (2 * faces, comps), 0)
    comp = lax.broadcasted_iota(jnp.int32, (2 * faces, comps), 1)
    upper = (face < faces).astype(jnp.int32) * (NODE - 1)
    row = face % faces
    sector_at = (row // NODE) * group + row % NODE + upper * NODE
    radial_at = row * NODE + upper
    first = comps + 2 * faces
    for at, start in ((sector_at, 2 * faces), (radial_at, 4 * faces)):
        spread = (comp == at).astype(F32).astype(BF16)
        op_ref[:, first : first + comps] = jnp.dot(
            lift_ref[:, start : start + 2 * faces], spread, preferred_element_type=F32
        ).astype(BF16)
        first += comps
    op_ref[:, first : first + 2 * faces] = lift_ref[:, 2 * faces : 4 * faces]
    v_ref[...] = jnp.sum(weights_ref[...].astype(F32) * samples_ref[...][None], axis=1)
    lanes, points = hot_ref.shape
    within = lax.broadcasted_iota(jnp.int32, (lanes, points), 0)
    hot_ref[...] = (within == host_ref[...] % lanes).astype(F32).astype(BF16)


def plane_kernel(x, planes, flat_ref, op_ref, axlo_ref, axhi_ref, azlo_ref, azhi_ref, out_ref, stack_ref):
    comps = flat_ref.shape[0]
    width = flat_ref.shape[1] // planes
    block = azlo_ref.shape[1] // planes
    sectors = width // block
    tiles = block // LANES
    rows = sectors * tiles
    group = NODE * NODE
    faces = NVAR * group
    here = x * width
    own = flat_ref[:, here : here + width]
    stack_ref[:comps, :] = own
    for v in range(NVAR):
        low = v * NODE * group
        top = low + (NODE - 1) * group
        at = comps + v * group
        if x > 0:
            stack_ref[at : at + group, :] = flat_ref[top : top + group, here - width : here]
        else:
            stack_ref[at : at + group, :] = axlo_ref[v * group : (v + 1) * group, :]
        at += faces
        if x < planes - 1:
            stack_ref[at : at + group, :] = flat_ref[
                low : low + group, here + width : here + 2 * width
            ]
        else:
            stack_ref[at : at + group, :] = axhi_ref[v * group : (v + 1) * group, :]
    comp = lax.broadcasted_iota(jnp.int32, (comps, block), 0)
    lane = lax.broadcasted_iota(jnp.int32, (comps, block), 1)
    q = (comp // NODE) % NODE
    w = comp % NODE
    q_top = (q == NODE - 1).astype(F32).astype(BF16)
    q_low = (q == 0).astype(F32).astype(BF16)
    w_top = ((w == NODE - 1) & (lane > 0)).astype(F32).astype(BF16)
    w_low = ((w == 0) & (lane < block - 1)).astype(F32).astype(BF16)
    mix = comps + 2 * faces
    zeros = jnp.zeros((faces, block), BF16)
    for a in range(sectors):
        first = a * block
        columns = slice(first, first + block)
        part = flat_ref[:, here + first : here + first + block]
        sector = None
        if a > 0:
            sector = q_top * flat_ref[:, here + first - block : here + first]
        if a < sectors - 1:
            right = q_low * flat_ref[:, here + first + block : here + first + 2 * block]
            sector = right if sector is None else sector + right
        if sector is None:
            sector = jnp.zeros((comps, block), BF16)
        stack_ref[mix : mix + comps, columns] = sector
        stack_ref[mix + comps : mix + 2 * comps, columns] = w_top * pltpu.roll(
            part, 1, 1
        ) + w_low * pltpu.roll(part, block - 1, 1)
        halo = mix + 2 * comps
        stack_ref[halo : halo + faces, columns] = (
            azlo_ref[:, x * block : (x + 1) * block] if a == 0 else zeros
        )
        stack_ref[halo + faces : halo + 2 * faces, columns] = (
            azhi_ref[:, x * block : (x + 1) * block] if a == sectors - 1 else zeros
        )
    result = jnp.dot(op_ref[...], stack_ref[...], preferred_element_type=F32)
    for k in range(rows):
        j, a = divmod(k, sectors)
        first = (a * tiles + j) * LANES
        out_ref[pl.ds(k, comps, stride=rows), :] = result[:, first : first + LANES] + own[
            :, first : first + LANES
        ].astype(F32)


def strength_part(v_ref, sens, radiation_ref):
    blocks = v_ref.shape[0]
    points = radiation_ref.shape[1]
    combined = jnp.dot(
        v_ref[...], sens, preferred_element_type=F32, precision=lax.Precision.HIGHEST
    )
    high = combined.astype(BF16)
    low = (combined - high.astype(F32)).astype(BF16)
    both = jnp.concatenate([high, low], axis=0)
    product = jnp.dot(both, radiation_ref[...], preferred_element_type=F32)
    product = product[:blocks] + product[blocks:]
    block = lax.broadcasted_iota(jnp.int32, (blocks, points), 0)
    point = lax.broadcasted_iota(jnp.int32, (blocks, points), 1)
    return jnp.sum(
        jnp.where(block == point // (points // blocks), product, 0.0), axis=0, keepdims=True
    )


def sensitivity(sums, half, taper_ref, weights_ref, target_ref):
    width = sums.shape[1]
    columns = pl.ds(pl.multiple_of(half * width, width), width)
    return weights_ref[:, columns] * taper_ref[...] * (sums - target_ref[:, columns])


def own_half_kernel(half_ref, sums_ref, taper_ref, weights_ref, target_ref, v_ref, radiation_ref, out_ref):
    sens = sensitivity(sums_ref[...], half_ref[0], taper_ref, weights_ref, target_ref)
    out_ref[...] = strength_part(v_ref, sens, radiation_ref)


def final_kernel(
    tiles,
    half_ref,
    sector_ref,
    own_ref,
    other_ref,
    taper_ref,
    weights_ref,
    target_ref,
    v_ref,
    radiation_ref,
    part_ref,
    host_ref,
    hot_ref,
    profile_ref,
    *rest,
):
    planes = len(rest) - 4
    base_refs = rest[:planes]
    sens_ref, out_ref, source_ref, all_ref = rest[planes:]
    rows = out_ref.shape[2]
    lanes = out_ref.shape[3]

    @pl.when(pl.program_id(0) == 0)
    def _():
        other = half_ref[0]
        width = own_ref.shape[1]
        own_sens = sensitivity(own_ref[...], 1 - other, taper_ref, weights_ref, target_ref)
        sens = sensitivity(other_ref[...], other, taper_ref, weights_ref, target_ref)
        all_ref[:, pl.ds(pl.multiple_of(other * width, width), width)] = sens
        all_ref[:, pl.ds(pl.multiple_of((1 - other) * width, width), width)] = own_sens
        strength = part_ref[...] + strength_part(v_ref, sens, radiation_ref)
        host = host_ref[...]
        sectors = rows // tiles
        per_plane = rows * lanes
        row = (
            (host // per_plane) * rows
            + ((host // lanes) % tiles) * sectors
            + (host // (lanes * tiles)) % sectors
        )
        at = lax.broadcasted_iota(jnp.int32, (planes * rows, host.shape[1]), 0)
        placed = jnp.where(at == row, strength, 0.0)
        high = placed.astype(BF16)
        low = (placed - high.astype(F32)).astype(BF16)
        gathered = lax.dot_general(
            jnp.concatenate([high, low], axis=0),
            hot_ref[...],
            (((1,), (1,)), ((), ())),
            preferred_element_type=F32,
        )
        source_ref[...] = gathered[: planes * rows] + gathered[planes * rows :]
        count = sens_ref.shape[1]
        start = sector_ref[0] * count
        aligned = pl.multiple_of((start // LANES) * LANES, LANES)
        window = all_ref[:, pl.ds(aligned, LANES)]
        turned = pltpu.roll(window, lax.rem(LANES - (start - aligned), LANES), 1)
        sens_ref[...] = turned[:, :count]

    profile = profile_ref[...]
    for x in range(planes):
        source = source_ref[x * rows : (x + 1) * rows, :]
        count = profile.shape[0]
        out_ref[:, x] = base_refs[x][...].reshape(count, rows, lanes) + profile.reshape(
            count, 1, 1
        ) * source.reshape(1, rows, lanes)


def exchange(value, mask, devices):
    return lax.ppermute(value, MESH_AXES, [(i, i ^ mask) for i in range(devices)])


def body(
    surface_signal,
    retarded_weights,
    radiation_weights,
    target_signal,
    observer_weights,
    sample_weights,
    host_element,
    source_profile,
    adjoint_state,
    volume_operator,
    lift_operator,
):
    streams = lax.axis_size("stream")
    sectors_all = lax.axis_size("azim")
    devices = streams * sectors_all
    stream = lax.axis_index("stream")
    sector = lax.axis_index("azim")
    window, points = surface_signal.shape
    observers = radiation_weights.shape[0]
    blocks = retarded_weights.shape[0]
    comps, planes, sectors, radial = adjoint_state.shape
    tiles = radial // LANES
    rows = sectors * tiles
    width = sectors * radial
    faces = NVAR * NODE * NODE

    mine = lax.rem(stream, 2).astype(jnp.int32).reshape(1)
    other = 1 - mine

    send, delayed = observer_half(
        first_half_kernel,
        other,
        (surface_signal, retarded_weights),
        radiation_weights,
        (window, points),
    )
    received = exchange(send, sectors_all, devices)
    (own,) = observer_half(second_half_kernel, mine, (delayed,), radiation_weights)
    sums = own + received

    view = (
        adjoint_state.reshape(comps, planes, sectors, tiles, LANES)
        .transpose(0, 1, 3, 2, 4)
        .reshape(comps, planes, rows, LANES)
    )
    flat, low_plane, top_plane, low_sector, top_sector = pl.pallas_call(
        lambda *refs: flatten_kernel(sectors, *refs),
        out_shape=[
            jax.ShapeDtypeStruct((comps, planes * width), BF16),
            jax.ShapeDtypeStruct((faces, width), BF16),
            jax.ShapeDtypeStruct((faces, width), BF16),
            jax.ShapeDtypeStruct((faces, planes * radial), BF16),
            jax.ShapeDtypeStruct((faces, planes * radial), BF16),
        ],
        scratch_shapes=[pltpu.VMEM((comps * rows, LANES), F32)],
        compiler_params=params(24),
        cost_estimate=cost(0, 10 * 2**20),
    )(view)
    ring = [(i, (i + 1) % sectors_all) for i in range(sectors_all)]
    back = [(target, source) for source, target in ring]
    azlo = lax.ppermute(top_sector, "azim", ring)
    azhi = lax.ppermute(low_sector, "azim", back)
    if streams == 2:
        swapped = lax.ppermute(
            jnp.where(stream == 0, top_plane, low_plane), "stream", [(0, 1), (1, 0)]
        )
        axlo = jnp.where(stream == 1, swapped, jnp.zeros_like(swapped))
        axhi = jnp.where(stream == 0, swapped, jnp.zeros_like(swapped))
    else:
        up = [(i, i + 1) for i in range(streams - 1)]
        axlo = lax.ppermute(top_plane, "stream", up)
        axhi = lax.ppermute(low_plane, "stream", [(b, a) for a, b in up])

    operator, v, hot = pl.pallas_call(
        operator_kernel,
        out_shape=[
            jax.ShapeDtypeStruct((comps, 3 * comps + 4 * faces), BF16),
            jax.ShapeDtypeStruct((blocks, window), F32),
            jax.ShapeDtypeStruct((LANES, points), BF16),
        ],
        compiler_params=params(16),
        cost_estimate=cost(0, 4 * 2**20),
    )(
        volume_operator,
        lift_operator,
        retarded_weights,
        sample_weights.reshape(window, 1),
        host_element.reshape(1, points),
    )

    bases = []
    for x in range(planes):
        bases.append(
            pl.pallas_call(
                lambda *refs, x=x: plane_kernel(x, planes, *refs),
                out_shape=jax.ShapeDtypeStruct((comps * rows, LANES), F32),
                scratch_shapes=[pltpu.VMEM((operator.shape[1], width), BF16)],
                compiler_params=params(24),
                cost_estimate=cost(2 * comps * operator.shape[1] * width, 2 * 2**20),
            )(flat, operator, axlo, axhi, azlo, azhi)
        )

    bits = [1 << n for n in range((sectors_all - 1).bit_length())]
    bits += [sectors_all << n for n in range(1, (streams - 1).bit_length())]
    for first in range(0, len(bits), 2):
        pair = bits[first : first + 2]
        masks = pair + ([pair[0] | pair[1]] if len(pair) == 2 else [])
        low = sums.astype(BF16)
        parts = [exchange(low, mask, devices) for mask in masks]
        total = low.astype(F32) + parts[0].astype(F32)
        if len(parts) == 3:
            total = total + (parts[1].astype(F32) + parts[2].astype(F32))
        sums = total

    remote = exchange(sums, sectors_all, devices)
    taper = np.arange(window, dtype=np.float64)
    taper = (0.5 - 0.5 * np.cos(2.0 * np.pi * (taper + 0.5) / window)).astype(np.float32)
    taper = jnp.asarray(taper).reshape(window, 1)
    weights = observer_weights.reshape(1, observers)
    half_rows = observers // 2
    half_spec = pl.BlockSpec((half_rows, points), lambda i, h, *_: (h[0], 0))

    def whole(x):
        return pl.BlockSpec(x.shape, lambda i, *_: (0,) * x.ndim)

    operands = (sums, taper, weights, target_signal, v)
    part = pl.pallas_call(
        own_half_kernel,
        grid_spec=pltpu.PrefetchScalarGridSpec(
            num_scalar_prefetch=1,
            grid=(1,),
            in_specs=[whole(x) for x in operands] + [half_spec],
            out_specs=pl.BlockSpec((1, points), lambda i, h: (0, 0)),
        ),
        out_shape=jax.ShapeDtypeStruct((1, points), F32),
        compiler_params=params(24),
        cost_estimate=cost(2 * 2 * blocks * half_rows * points, half_rows * points * 2),
    )(mine, *operands, radiation_weights)

    steps = 5
    chunk = comps // steps
    head = (sums, remote, taper, weights, target_signal, v)
    tail = (part, host_element.reshape(1, points), hot)
    own_width = observers // sectors_all
    sens, updated = pl.pallas_call(
        lambda *refs: final_kernel(tiles, *refs),
        grid_spec=pltpu.PrefetchScalarGridSpec(
            num_scalar_prefetch=2,
            grid=(steps,),
            in_specs=[whole(x) for x in head]
            + [half_spec]
            + [whole(x) for x in tail]
            + [pl.BlockSpec((chunk, 1), lambda i, *_: (i, 0))]
            + [pl.BlockSpec((chunk * rows, LANES), lambda i, *_: (i, 0))] * planes,
            out_specs=[
                pl.BlockSpec((window, own_width), lambda i, *_: (0, 0)),
                pl.BlockSpec((chunk, planes, rows, LANES), lambda i, *_: (i, 0, 0, 0)),
            ],
            scratch_shapes=[
                pltpu.VMEM((planes * rows, LANES), F32),
                pltpu.VMEM((window, observers), F32),
            ],
        ),
        out_shape=[
            jax.ShapeDtypeStruct((window, own_width), F32),
            jax.ShapeDtypeStruct((comps, planes, rows, LANES), F32),
        ],
        compiler_params=params(32),
        cost_estimate=cost(0, 12 * 2**20),
    )(
        other,
        sector.astype(jnp.int32).reshape(1),
        *head,
        radiation_weights,
        *tail,
        source_profile.reshape(comps, 1),
        *bases,
    )
    updated = (
        updated.reshape(comps, planes, tiles, sectors, LANES)
        .transpose(0, 1, 3, 2, 4)
        .reshape(adjoint_state.shape)
    )
    return sens, updated


def solution(mesh):
    return jax.shard_map(
        body,
        mesh=mesh,
        in_specs=(
            P(None, ("stream", "azim")),
            P(("stream", "azim"), None, None),
            P(None, ("stream", "azim")),
            P(),
            P(),
            P(),
            P(("stream", "azim")),
            P(),
            P(None, "stream", "azim", None),
            P(),
            P(),
        ),
        out_specs=(P(None, "azim"), P(None, "stream", "azim", None)),
        check_vma=False,
    )
```

```python
import jax
import jax.numpy as jnp
import numpy as np
from jax import lax
from jax.experimental import pallas as pl
from jax.experimental.pallas import tpu as pltpu
from jax.sharding import PartitionSpec as P

NVAR = 5
NODE = 4
LANES = 128
F32 = jnp.float32
BF16 = jnp.bfloat16
MESH_AXES = ("stream", "azim")
VMEM = pl.BlockSpec(memory_space=pltpu.VMEM)
HBM = pl.BlockSpec(memory_space=pl.ANY)


def vmem(shape, dtype):
    return pltpu.VMEM(shape, dtype)


def in_hbm(x):
    return pltpu.with_memory_space_constraint(x, pltpu.HBM)


def call(kernel, ins, outs, args, scratch=(), mib=16, flops=0, nbytes=0, out_specs=None):
    return pl.pallas_call(
        kernel,
        in_specs=ins,
        out_specs=out_specs or [VMEM] * len(outs),
        out_shape=outs,
        scratch_shapes=list(scratch),
        compiler_params=pltpu.CompilerParams(vmem_limit_bytes=mib * 2**20),
        cost_estimate=pl.CostEstimate(flops=flops, bytes_accessed=nbytes, transcendentals=0),
    )(*args)


def core_of():
    return lax.rem(lax.axis_index("stream"), 2)


def mine_is_top():
    return core_of() == lax.rem(lax.axis_index("azim"), 2)


def project(delayed, radiation):
    return lax.dot_general(
        delayed, radiation, (((1,), (1,)), ((), ())), preferred_element_type=F32
    )


def start_kernel(
    sectors,
    signal_hbm,
    weights_hbm,
    radiation_hbm,
    state_hbm,
    send_ref,
    delayed_ref,
    radiation_ref,
    state_ref,
    weights_ref,
    swap_ref,
    mine_ref,
    second_ref,
    signal_ref,
    rows_ref,
    sems,
):
    comps, planes, rows, lanes = state_ref.shape
    tiles = rows // sectors
    block = tiles * lanes
    group = NODE * NODE
    faces = NVAR * group
    observers = radiation_ref.shape[0]
    half = observers // 2
    chunk = half // 2
    core = core_of()
    far = pl.multiple_of((1 - core) * half, half)
    near = pl.multiple_of(core * half, half)
    pieces = [
        (signal_hbm, signal_ref),
        (weights_hbm, weights_ref),
        (radiation_hbm.at[pl.ds(far, chunk)], radiation_ref.at[pl.ds(far, chunk)]),
        (
            radiation_hbm.at[pl.ds(far + chunk, chunk)],
            radiation_ref.at[pl.ds(far + chunk, chunk)],
        ),
        (state_hbm, state_ref),
        (radiation_hbm.at[pl.ds(near, half)], radiation_ref.at[pl.ds(near, half)]),
    ]
    copies = [
        pltpu.make_async_copy(source, target, sems.at[n])
        for n, (source, target) in enumerate(pieces)
    ]
    for copy in copies:
        copy.start()
    copies[0].wait()
    copies[1].wait()
    blocks = weights_ref.shape[0]
    width = signal_ref.shape[1] // blocks
    for b in range(blocks):
        columns = slice(b * width, (b + 1) * width)
        delayed_ref[:, columns] = lax.dot_general(
            weights_ref[b],
            signal_ref[:, columns],
            (((0,), (0,)), ((), ())),
            preferred_element_type=F32,
        ).astype(BF16)
    copies[2].wait()
    send_ref[:, :chunk] = project(delayed_ref[...], radiation_ref[pl.ds(far, chunk), :])
    copies[3].wait()
    send_ref[:, chunk:] = project(
        delayed_ref[...], radiation_ref[pl.ds(far + chunk, chunk), :]
    )
    copies[4].wait()

    def gather(x, offsets, count):
        for n, offset in enumerate(offsets):
            rows_ref[n * count * rows : (n + 1) * count * rows, :] = (
                state_ref[pl.ds(offset, count), x].astype(F32).reshape(count * rows, lanes)
            )

    def picked(k):
        return rows_ref[pl.ds(k, faces, stride=rows), :].astype(BF16)

    top = mine_is_top()
    for at_top in (0, 1):
        mine_here = top if at_top else jnp.logical_not(top)
        offset = at_top * (NODE - 1) * NODE
        a = at_top * (sectors - 1)
        for x in range(planes):
            gather(x, [n * group + offset for n in range(NVAR * NODE)], NODE)
            for j in range(tiles):
                columns = slice(x * block + j * lanes, x * block + (j + 1) * lanes)
                value = picked(j * sectors + a)

                @pl.when(mine_here)
                def _():
                    mine_ref[:, columns] = value

                @pl.when(jnp.logical_not(mine_here))
                def _():
                    swap_ref[:faces, columns] = value

    def plane_face(at_top, put):
        x = at_top * (planes - 1)
        first = at_top * ((NODE - 1) * group)
        gather(x, [v * NODE * group + first for v in range(NVAR)], group)
        for k in range(rows):
            j, a = divmod(k, sectors)
            first_lane = (a * tiles + j) * lanes
            put(slice(first_lane, first_lane + lanes), picked(k))

    def put_swap(columns, value):
        swap_ref[faces:, columns] = value

    def put_second(columns, value):
        second_ref[:, columns] = value

    plane_face(1 - core, put_swap)
    if second_ref.shape[0] == faces:
        plane_face(core, put_second)
    else:
        second_ref[...] = jnp.zeros(second_ref.shape, BF16)
    copies[5].wait()


def near_kernel(count, delayed_ref, radiation_ref, *refs):
    sources = refs[:count]
    own_ref = refs[count]
    targets = refs[count + 1 : 2 * count + 1]
    sems = refs[2 * count + 1]
    copies = [
        pltpu.make_async_copy(source, target, sems.at[n])
        for n, (source, target) in enumerate(zip(sources, targets))
    ]
    for copy in copies:
        copy.start()
    half = radiation_ref.shape[0] // 2
    near = pl.multiple_of(core_of() * half, half)
    own_ref[...] = project(delayed_ref[...], radiation_ref[pl.ds(near, half), :])
    for copy in copies:
        copy.wait()


def join_kernel(own_ref, received_ref, mine_ref, swapped_ref, low_ref, pay_ref):
    faces = mine_ref.shape[0]
    low_ref[...] = (own_ref[...] + received_ref[...]).astype(BF16)
    pay_ref[:faces, :] = mine_ref[...]
    pay_ref[faces:, :] = swapped_ref[:faces, :]


def split(x):
    high = x.astype(BF16)
    return high, (x - high.astype(F32)).astype(BF16)


def prepare_kernel(
    sectors,
    state_ref,
    volume_ref,
    lift_ref,
    weights_ref,
    samples_ref,
    host_ref,
    profile_ref,
    flat_ref,
    op_ref,
    v_ref,
    hot_ref,
    spread_ref,
    plane_ref,
):
    comps, planes, rows, lanes = state_ref.shape
    tiles = rows // sectors
    width = sectors * tiles * lanes
    group = NODE * NODE
    faces = NVAR * group
    for x in range(planes):
        plane_ref[x] = state_ref[:, x].astype(F32).reshape(comps * rows, lanes)
        for k in range(rows):
            j, a = divmod(k, sectors)
            first = x * width + (a * tiles + j) * lanes
            flat_ref[:, first : first + lanes] = plane_ref[
                x, pl.ds(k, comps, stride=rows), :
            ].astype(BF16)
    op_ref[:, :comps] = volume_ref[...]
    op_ref[:, comps : comps + 2 * faces] = lift_ref[:, : 2 * faces]
    face = lax.broadcasted_iota(jnp.int32, (2 * faces, comps), 0)
    comp = lax.broadcasted_iota(jnp.int32, (2 * faces, comps), 1)
    upper = (face < faces).astype(jnp.int32) * (NODE - 1)
    row = face % faces
    sector_at = (row // NODE) * group + row % NODE + upper * NODE
    radial_at = row * NODE + upper
    first = comps + 2 * faces
    for at, start in ((sector_at, 2 * faces), (radial_at, 4 * faces)):
        place = (comp == at).astype(F32).astype(BF16)
        op_ref[:, first : first + comps] = jnp.dot(
            lift_ref[:, start : start + 2 * faces], place, preferred_element_type=F32
        ).astype(BF16)
        first += comps
    op_ref[:, first : first + 2 * faces] = lift_ref[:, 2 * faces : 4 * faces]

    blocks, window, _ = weights_ref.shape
    samples = jnp.concatenate([samples_ref[...]] * blocks, axis=1)
    owner = lax.broadcasted_iota(jnp.int32, (blocks, blocks * window), 0)
    entry = lax.broadcasted_iota(jnp.int32, (blocks, blocks * window), 1)
    chosen = jnp.where(owner == entry // window, samples, 0.0)
    stacked = weights_ref[...].reshape(blocks * window, window)
    v_ref[...] = sum(
        jnp.dot(part, stacked, preferred_element_type=F32) for part in split(chosen)
    )
    points = hot_ref.shape[1]
    within = lax.broadcasted_iota(jnp.int32, (lanes, points), 0)
    hot_ref[...] = (within == host_ref[...] % lanes).astype(F32).astype(BF16)

    line = lax.broadcasted_iota(jnp.int32, (comps, comps), 0)
    cross = lax.broadcasted_iota(jnp.int32, (comps, comps), 1)
    diagonal = jnp.where(line == cross, profile_ref[...], 0.0)
    ones = jnp.ones((comps, lanes), BF16)
    high, low = split(diagonal)
    lowest = (diagonal - high.astype(F32) - low.astype(F32)).astype(BF16)
    column = sum(
        jnp.dot(part, ones, preferred_element_type=F32) for part in (high, low, lowest)
    )
    for k in range(rows):
        spread_ref[pl.ds(k, comps, stride=rows), :] = column


def planes_kernel(
    first_plane,
    planes,
    flat_ref,
    op_ref,
    crossed_ref,
    back_ref,
    swapped_ref,
    second_ref,
    *refs,
):
    out_refs = refs[:-1]
    stack_ref = refs[-1]
    comps = flat_ref.shape[0]
    width = flat_ref.shape[1] // planes
    group = NODE * NODE
    faces = NVAR * group
    block = back_ref.shape[1] // planes
    sectors = width // block
    tiles = block // LANES
    rows = sectors * tiles
    comp = lax.broadcasted_iota(jnp.int32, (comps, block), 0)
    lane = lax.broadcasted_iota(jnp.int32, (comps, block), 1)
    q = (comp // NODE) % NODE
    w = comp % NODE
    q_top = (q == NODE - 1).astype(F32).astype(BF16)
    q_low = (q == 0).astype(F32).astype(BF16)
    w_top = ((w == NODE - 1) & (lane > 0)).astype(F32).astype(BF16)
    w_low = ((w == 0) & (lane < block - 1)).astype(F32).astype(BF16)
    zeros = jnp.zeros((faces, block), BF16)
    top = mine_is_top()
    odd = core_of() == 1

    def second(v):
        if second_ref.shape[0] == faces:
            return second_ref[v * group : (v + 1) * group, :]
        return jnp.zeros((group, width), BF16)

    def first(v):
        return swapped_ref[faces + v * group : faces + (v + 1) * group, :]

    for n, out_ref in enumerate(out_refs):
        x = first_plane + n
        here = x * width
        own = flat_ref[:, here : here + width]
        stack_ref[n, :comps, :] = own
        for v in range(NVAR):
            low_row = v * NODE * group
            top_row = low_row + (NODE - 1) * group
            at = comps + v * group
            if x > 0:
                value = flat_ref[top_row : top_row + group, here - width : here]
            else:
                value = jnp.where(odd, first(v), second(v))
            stack_ref[n, at : at + group, :] = value
            at += faces
            if x < planes - 1:
                value = flat_ref[low_row : low_row + group, here + width : here + 2 * width]
            else:
                value = jnp.where(odd, second(v), first(v))
            stack_ref[n, at : at + group, :] = value
        mix = comps + 2 * faces
        halo = mix + 2 * comps
        crossed = crossed_ref[:faces, x * block : (x + 1) * block]
        back = back_ref[:, x * block : (x + 1) * block]
        for a in range(sectors):
            at = a * block
            columns = slice(at, at + block)
            part = flat_ref[:, here + at : here + at + block]
            sector = None
            if a > 0:
                sector = q_top * flat_ref[:, here + at - block : here + at]
            if a < sectors - 1:
                right = q_low * flat_ref[:, here + at + block : here + at + 2 * block]
                sector = right if sector is None else sector + right
            if sector is None:
                sector = jnp.zeros((comps, block), BF16)
            stack_ref[n, mix : mix + comps, columns] = sector
            stack_ref[n, mix + comps : halo, columns] = w_top * pltpu.roll(
                part, 1, 1
            ) + w_low * pltpu.roll(part, block - 1, 1)
            stack_ref[n, halo : halo + faces, columns] = (
                jnp.where(top, back, crossed) if a == 0 else zeros
            )
            stack_ref[n, halo + faces : halo + 2 * faces, columns] = (
                jnp.where(top, crossed, back) if a == sectors - 1 else zeros
            )
        result = jnp.dot(op_ref[...], stack_ref[n], preferred_element_type=F32)
        for k in range(rows):
            j, a = divmod(k, sectors)
            at = (a * tiles + j) * LANES
            out_ref[pl.ds(k, comps, stride=rows), :] = result[:, at : at + LANES] + own[
                :, at : at + LANES
            ].astype(F32)


def strength_part(v_ref, sens, radiation):
    blocks = v_ref.shape[0]
    points = radiation.shape[1]
    combined = jnp.dot(
        v_ref[...], sens, preferred_element_type=F32, precision=lax.Precision.HIGHEST
    )
    both = jnp.concatenate(split(combined), axis=0)
    product = jnp.dot(both, radiation, preferred_element_type=F32)
    product = product[:blocks] + product[blocks:]
    block = lax.broadcasted_iota(jnp.int32, (blocks, points), 0)
    point = lax.broadcasted_iota(jnp.int32, (blocks, points), 1)
    return jnp.sum(
        jnp.where(block == point // (points // blocks), product, 0.0), axis=0, keepdims=True
    )


def sensitivity(sums, half, taper_ref, weights_ref, target_ref):
    width = sums.shape[1]
    columns = pl.ds(pl.multiple_of(half * width, width), width)
    return weights_ref[:, columns] * taper_ref[...] * (sums - target_ref[:, columns])


def own_kernel(sums_ref, taper_ref, weights_ref, target_ref, v_ref, radiation_ref, part_ref, sens_ref):
    core = core_of()
    half = radiation_ref.shape[0] // 2
    sens = sensitivity(sums_ref[...], core, taper_ref, weights_ref, target_ref)
    sens_ref[...] = sens
    part_ref[...] = strength_part(
        v_ref, sens, radiation_ref[pl.ds(pl.multiple_of(core * half, half), half), :]
    )


def final_kernel(
    tiles,
    chunks,
    other_ref,
    own_sens_ref,
    taper_ref,
    weights_ref,
    target_ref,
    v_ref,
    radiation_ref,
    part_ref,
    host_ref,
    hot_ref,
    spread_ref,
    *rest,
):
    planes = len(rest) - 5
    base_refs = rest[:planes]
    sens_ref, out_hbm, all_ref, buffer_ref, sems = rest[planes:]
    comps, _, rows, lanes = out_hbm.shape
    far = 1 - core_of()
    half = radiation_ref.shape[0] // 2
    start = pl.multiple_of(far * half, half)
    sens = sensitivity(other_ref[...], far, taper_ref, weights_ref, target_ref)
    strength = part_ref[...] + strength_part(v_ref, sens, radiation_ref[pl.ds(start, half), :])
    host = host_ref[...]
    sectors = rows // tiles
    per_plane = rows * lanes
    row = (
        (host // per_plane) * rows
        + ((host // lanes) % tiles) * sectors
        + (host // (lanes * tiles)) % sectors
    )
    at = lax.broadcasted_iota(jnp.int32, (planes * rows, host.shape[1]), 0)
    placed = jnp.where(at == row, strength, 0.0)
    gathered = lax.dot_general(
        jnp.concatenate(split(placed), axis=0),
        hot_ref[...],
        (((1,), (1,)), ((), ())),
        preferred_element_type=F32,
    )
    source = gathered[: planes * rows] + gathered[planes * rows :]
    chunk = comps // chunks
    copies = []
    for n in range(chunks):
        part = slice(n * chunk, (n + 1) * chunk)
        lines = slice(n * chunk * rows, (n + 1) * chunk * rows)
        spread = spread_ref[lines, :].reshape(chunk, rows, lanes)
        for x in range(planes):
            buffer_ref[part, x] = (
                base_refs[x][lines, :].reshape(chunk, rows, lanes)
                + spread * source[x * rows : (x + 1) * rows][None]
            )
        copy = pltpu.make_async_copy(buffer_ref.at[part], out_hbm.at[part], sems.at[n])
        copy.start()
        copies.append(copy)

    all_ref[:, pl.ds(start, half)] = sens
    all_ref[:, pl.ds(pl.multiple_of((1 - far) * half, half), half)] = own_sens_ref[...]
    count = sens_ref.shape[1]
    first = lax.axis_index("azim") * count
    aligned = pl.multiple_of((first // LANES) * LANES, LANES)
    window = all_ref[:, pl.ds(aligned, LANES)]
    turned = pltpu.roll(window, lax.rem(LANES - (first - aligned), LANES), 1)
    sens_ref[...] = turned[:, :count]
    for copy in copies:
        copy.wait()


def exchange(value, mask, devices):
    return lax.ppermute(value, MESH_AXES, [(i, i ^ mask) for i in range(devices)])


def body(
    surface_signal,
    retarded_weights,
    radiation_weights,
    target_signal,
    observer_weights,
    sample_weights,
    host_element,
    source_profile,
    adjoint_state,
    volume_operator,
    lift_operator,
):
    streams = lax.axis_size("stream")
    around = lax.axis_size("azim")
    devices = streams * around
    window, points = surface_signal.shape
    observers = radiation_weights.shape[0]
    half = observers // 2
    blocks = retarded_weights.shape[0]
    comps, planes, sectors, radial = adjoint_state.shape
    tiles = radial // LANES
    rows = sectors * tiles
    width = sectors * radial
    faces = NVAR * NODE * NODE
    depth = 3 * comps + 4 * faces
    barrier = lax.optimization_barrier

    view = (
        adjoint_state.reshape(comps, planes, sectors, tiles, LANES)
        .transpose(0, 1, 3, 2, 4)
        .reshape(comps, planes, rows, LANES)
    )
    send, delayed, radiation, state, retarded, swap, mine, second = call(
        lambda *refs: start_kernel(sectors, *refs),
        [HBM] * 4,
        [
            vmem((window, half), F32),
            vmem((window, points), BF16),
            vmem(radiation_weights.shape, BF16),
            vmem(view.shape, BF16),
            vmem(retarded_weights.shape, BF16),
            vmem((2 * faces, width), BF16),
            vmem((faces, planes * radial), BF16),
            vmem((faces if streams > 2 else 16, width), BF16),
        ],
        [in_hbm(x) for x in (surface_signal, retarded_weights, radiation_weights, view)],
        [
            pltpu.VMEM((window, points), BF16),
            pltpu.VMEM((faces * rows, LANES), F32),
            pltpu.SemaphoreType.DMA((6,)),
        ],
    )
    received = exchange(send, around, devices)
    swapped = exchange(swap, around, devices)
    small = [
        target_signal,
        observer_weights.reshape(1, observers),
        sample_weights.reshape(1, window),
        host_element.reshape(1, points),
        source_profile.reshape(1, comps),
        volume_operator,
        lift_operator,
    ]
    own, target, weights, samples, host, profile, volume, lift = call(
        lambda *refs: near_kernel(len(small), *refs),
        [VMEM, VMEM] + [HBM] * len(small),
        [vmem((window, half), F32)] + [vmem(x.shape, x.dtype) for x in small],
        [delayed, radiation] + [in_hbm(x) for x in small],
        [pltpu.SemaphoreType.DMA((len(small),))],
    )
    low, pay = call(
        join_kernel,
        [VMEM] * 4,
        [vmem((window, half), BF16), vmem((2 * faces, planes * radial), BF16)],
        [own, received, mine, swapped],
    )

    bits = [1 << n for n in range((around - 1).bit_length())]
    bits += [around << n for n in range(1, (streams - 1).bit_length())]
    stages = []
    for first in range(0, len(bits), 2):
        pair = bits[first : first + 2]
        stages.append(pair + ([pair[0] | pair[1]] if len(pair) == 2 else []))

    low, pay, state = barrier((low, pay, state))
    parts = [exchange(low, mask, devices) for mask in stages[0]]
    inner = [(i, i ^ 1) for i in range(around)]
    outer = [(i, (i + 1 if i % 2 else i - 1) % around) for i in range(around)]
    pairs = []
    for s in range(streams):
        pairs += [(s * around + i, s * around + j) for i, j in (outer if s % 2 else inner)]
    crossed = lax.ppermute(pay, MESH_AXES, pairs)
    if streams > 2:
        links = [(s, s + 1) for s in range(1, streams - 1, 2)]
        second = lax.ppermute(second, "stream", links + [(b, a) for a, b in links])
    flat, operator, v, hot, spread = call(
        lambda *refs: prepare_kernel(sectors, *refs),
        [VMEM] * 7,
        [
            vmem((comps, planes * width), BF16),
            vmem((comps, depth), BF16),
            vmem((blocks, window), F32),
            vmem((LANES, points), BF16),
            vmem((comps * rows, LANES), F32),
        ],
        [state, volume, lift, retarded, samples, host, profile],
        [pltpu.VMEM((planes, comps * rows, LANES), F32)],
        nbytes=12 * 2**20,
    )

    def combine(low, parts):
        total = low.astype(F32) + parts[0].astype(F32)
        if len(parts) == 3:
            total = total + (parts[1].astype(F32) + parts[2].astype(F32))
        return total

    parts, flat = barrier((parts, flat))
    sums = combine(low, parts)
    low = sums.astype(BF16)
    low, crossed = barrier((low, crossed))
    back = exchange(crossed[faces:], around, devices)

    def run_planes(first, count):
        return call(
            lambda *refs: planes_kernel(first, planes, *refs),
            [VMEM] * 6,
            [vmem((comps * rows, LANES), F32)] * count,
            [flat, operator, crossed, back, swapped, second],
            [pltpu.VMEM((count, depth, width), BF16)],
            flops=2 * comps * depth * width * count,
            nbytes=count * 4 * 2**20,
        )

    bases = []
    for masks in stages[1:]:
        parts = [exchange(low, mask, devices) for mask in masks]
        if not bases:
            bases = list(run_planes(0, planes // 2)) + list(run_planes(planes // 2, planes // 2))
            parts, bases = barrier((parts, bases))
        sums = combine(low, parts)
        low = sums.astype(BF16)

    remote = exchange(sums, around, devices)
    taper = np.arange(window, dtype=np.float64)
    taper = (0.5 - 0.5 * np.cos(2.0 * np.pi * (taper + 0.5) / window)).astype(np.float32)
    taper = jnp.asarray(taper).reshape(window, 1)
    part, own_sens = call(
        own_kernel,
        [VMEM] * 6,
        [vmem((1, points), F32), vmem((window, half), F32)],
        [sums, taper, weights, target, v, radiation],
        flops=2 * 2 * blocks * half * points,
        nbytes=half * points * 2,
    )
    chunks = 8
    sens, updated = call(
        lambda *refs: final_kernel(tiles, chunks, *refs),
        [VMEM] * (11 + planes),
        [
            jax.ShapeDtypeStruct((window, observers // around), F32),
            jax.ShapeDtypeStruct(view.shape, F32),
        ],
        [remote, own_sens, taper, weights, target, v, radiation, part, host, hot, spread]
        + list(bases),
        [
            pltpu.VMEM((window, observers), F32),
            pltpu.VMEM(view.shape, F32),
            pltpu.SemaphoreType.DMA((chunks,)),
        ],
        nbytes=12 * 2**20,
        out_specs=[VMEM, HBM],
    )
    updated = (
        updated.reshape(comps, planes, tiles, sectors, LANES)
        .transpose(0, 1, 3, 2, 4)
        .reshape(adjoint_state.shape)
    )
    return sens, updated


def solution(mesh):
    return jax.shard_map(
        body,
        mesh=mesh,
        in_specs=(
            P(None, ("stream", "azim")),
            P(("stream", "azim"), None, None),
            P(None, ("stream", "azim")),
            P(),
            P(),
            P(),
            P(("stream", "azim")),
            P(),
            P(None, "stream", "azim", None),
            P(),
            P(),
        ),
        out_specs=(P(None, "azim"), P(None, "stream", "azim", None)),
        check_vma=False,
    )
```

```python
import jax
import jax.numpy as jnp
import numpy as np
from jax import lax
from jax.experimental import pallas as pl
from jax.experimental.pallas import tpu as pltpu
from jax.sharding import PartitionSpec as P

NVAR = 5
NODE = 4
LANES = 128
F32 = jnp.float32
BF16 = jnp.bfloat16
MESH_AXES = ("stream", "azim")
VMEM = pl.BlockSpec(memory_space=pltpu.VMEM)
HBM = pl.BlockSpec(memory_space=pl.ANY)


def vmem(shape, dtype):
    return pltpu.VMEM(shape, dtype)


def in_hbm(x):
    return pltpu.with_memory_space_constraint(x, pltpu.HBM)


def call(kernel, ins, outs, args, scratch=(), mib=16, flops=0, nbytes=0, out_specs=None, aliases=None):
    return pl.pallas_call(
        kernel,
        in_specs=ins,
        out_specs=out_specs or [VMEM] * len(outs),
        out_shape=outs,
        scratch_shapes=list(scratch),
        input_output_aliases=aliases or {},
        compiler_params=pltpu.CompilerParams(vmem_limit_bytes=mib * 2**20),
        cost_estimate=pl.CostEstimate(flops=flops, bytes_accessed=nbytes, transcendentals=0),
    )(*args)


def core_of():
    return lax.rem(lax.axis_index("stream"), 2)


def mine_is_top():
    return core_of() == lax.rem(lax.axis_index("azim"), 2)


def project(delayed, radiation):
    return lax.dot_general(
        delayed, radiation, (((1,), (1,)), ((), ())), preferred_element_type=F32
    )


def started(pairs, sems):
    copies = [
        pltpu.make_async_copy(source, target, sems.at[n])
        for n, (source, target) in enumerate(pairs)
    ]
    for copy in copies:
        copy.start()
    return copies


def start_kernel(
    sectors,
    signal_hbm,
    weights_hbm,
    radiation_hbm,
    state_hbm,
    send_ref,
    delayed_ref,
    radiation_ref,
    state_ref,
    weights_ref,
    swap_ref,
    mine_ref,
    second_ref,
    signal_ref,
    rows_ref,
    sems,
):
    comps, planes, rows, lanes = state_ref.shape
    tiles = rows // sectors
    block = tiles * lanes
    group = NODE * NODE
    faces = NVAR * group
    half = radiation_ref.shape[0]
    chunk = half // 2
    core = core_of()
    far = pl.multiple_of((1 - core) * half, half)
    pairs = [(signal_hbm, signal_ref), (weights_hbm, weights_ref)]
    for first in (0, chunk):
        pairs.append(
            (radiation_hbm.at[pl.ds(far + first, chunk)], radiation_ref.at[pl.ds(first, chunk)])
        )
    quarter = comps // NODE
    for first in range(0, comps, quarter):
        part = pl.ds(first, quarter)
        pairs.append((state_hbm.at[part], state_ref.at[part]))
    copies = started(pairs, sems)
    copies[0].wait()
    copies[1].wait()
    blocks = weights_ref.shape[0]
    width = signal_ref.shape[1] // blocks
    for b in range(blocks):
        columns = slice(b * width, (b + 1) * width)
        delayed_ref[:, columns] = lax.dot_general(
            weights_ref[b],
            signal_ref[:, columns],
            (((0,), (0,)), ((), ())),
            preferred_element_type=F32,
        ).astype(BF16)
    copies[2].wait()
    send_ref[:, :chunk] = project(delayed_ref[...], radiation_ref[:chunk, :])
    copies[3].wait()
    send_ref[:, chunk:] = project(delayed_ref[...], radiation_ref[chunk:, :])
    for copy in copies[4:]:
        copy.wait()

    def gather(x, offsets, count):
        for n, offset in enumerate(offsets):
            rows_ref[n * count * rows : (n + 1) * count * rows, :] = (
                state_ref[pl.ds(offset, count), x].astype(F32).reshape(count * rows, lanes)
            )

    def picked(k):
        return rows_ref[pl.ds(k, faces, stride=rows), :].astype(BF16)

    top = mine_is_top()
    for at_top in (0, 1):
        mine_here = top if at_top else jnp.logical_not(top)
        offset = at_top * (NODE - 1) * NODE
        a = at_top * (sectors - 1)
        for x in range(planes):
            gather(x, [n * group + offset for n in range(NVAR * NODE)], NODE)
            for j in range(tiles):
                columns = slice(x * block + j * lanes, x * block + (j + 1) * lanes)
                value = picked(j * sectors + a)

                @pl.when(mine_here)
                def _():
                    mine_ref[:, columns] = value

                @pl.when(jnp.logical_not(mine_here))
                def _():
                    swap_ref[:faces, columns] = value

    def plane_face(at_top, put):
        x = at_top * (planes - 1)
        first = at_top * ((NODE - 1) * group)
        gather(x, [v * NODE * group + first for v in range(NVAR)], group)
        for k in range(rows):
            j, a = divmod(k, sectors)
            first_lane = (a * tiles + j) * lanes
            put(slice(first_lane, first_lane + lanes), picked(k))

    def put_swap(columns, value):
        swap_ref[faces:, columns] = value

    def put_second(columns, value):
        second_ref[:, columns] = value

    plane_face(1 - core, put_swap)
    if second_ref.shape[0] == faces:
        plane_face(core, put_second)
    else:
        second_ref[...] = jnp.zeros(second_ref.shape, BF16)


def near_kernel(count, delayed_ref, radiation_hbm, *refs):
    own_ref, radiation_ref = refs[count : count + 2]
    half = radiation_ref.shape[0]
    chunk = half // 2
    near = pl.multiple_of(core_of() * half, half)
    pairs = [
        (radiation_hbm.at[pl.ds(near + first, chunk)], radiation_ref.at[pl.ds(first, chunk)])
        for first in (0, chunk)
    ]
    pairs += zip(refs[:count], refs[count + 2 : 2 * count + 2])
    copies = started(pairs, refs[2 * count + 2])
    copies[0].wait()
    own_ref[:, :chunk] = project(delayed_ref[...], radiation_ref[:chunk, :])
    copies[1].wait()
    own_ref[:, chunk:] = project(delayed_ref[...], radiation_ref[chunk:, :])
    for copy in copies[2:]:
        copy.wait()


def pack_kernel(mine_ref, swapped_ref, pay_ref):
    faces = mine_ref.shape[0]
    pay_ref[:faces, :] = mine_ref[...]
    pay_ref[faces:, :] = swapped_ref[:faces, :]


def split(x):
    high = x.astype(BF16)
    return high, (x - high.astype(F32)).astype(BF16)


def prepare_kernel(
    sectors,
    state_ref,
    volume_ref,
    lift_ref,
    weights_ref,
    samples_ref,
    host_ref,
    profile_ref,
    flat_ref,
    op_ref,
    edge_ref,
    v_ref,
    hot_ref,
    spread_ref,
    plane_ref,
):
    comps, planes, rows, lanes = state_ref.shape
    tiles = rows // sectors
    width = sectors * tiles * lanes
    group = NODE * NODE
    faces = NVAR * group
    for x in range(planes):
        plane_ref[x] = state_ref[:, x].astype(F32).reshape(comps * rows, lanes)
        for k in range(rows):
            j, a = divmod(k, sectors)
            first = x * width + (a * tiles + j) * lanes
            flat_ref[:, first : first + lanes] = plane_ref[
                x, pl.ds(k, comps, stride=rows), :
            ].astype(BF16)
    op_ref[:, :comps] = volume_ref[...]
    op_ref[:, comps : comps + 2 * faces] = lift_ref[:, : 2 * faces]
    face = lax.broadcasted_iota(jnp.int32, (2 * faces, comps), 0)
    comp = lax.broadcasted_iota(jnp.int32, (2 * faces, comps), 1)
    upper = (face < faces).astype(jnp.int32) * (NODE - 1)
    row = face % faces
    sector_at = (row // NODE) * group + row % NODE + upper * NODE
    radial_at = row * NODE + upper
    first = comps + 2 * faces
    for at, start in ((sector_at, 2 * faces), (radial_at, 4 * faces)):
        place = (comp == at).astype(F32).astype(BF16)
        op_ref[:, first : first + comps] = jnp.dot(
            lift_ref[:, start : start + 2 * faces], place, preferred_element_type=F32
        ).astype(BF16)
        first += comps
    edge_ref[:, :faces] = lift_ref[:, 2 * faces : 3 * faces]
    edge_ref[:, LANES : LANES + faces] = lift_ref[:, 3 * faces : 4 * faces]

    blocks, window, _ = weights_ref.shape
    samples = jnp.concatenate([samples_ref[...]] * blocks, axis=1)
    owner = lax.broadcasted_iota(jnp.int32, (blocks, blocks * window), 0)
    entry = lax.broadcasted_iota(jnp.int32, (blocks, blocks * window), 1)
    chosen = jnp.where(owner == entry // window, samples, 0.0)
    stacked = weights_ref[...].reshape(blocks * window, window)
    v_ref[...] = sum(
        jnp.dot(part, stacked, preferred_element_type=F32) for part in split(chosen)
    )
    points = hot_ref.shape[1]
    within = lax.broadcasted_iota(jnp.int32, (lanes, points), 0)
    hot_ref[...] = (within == host_ref[...] % lanes).astype(F32).astype(BF16)

    line = lax.broadcasted_iota(jnp.int32, (comps, comps), 0)
    cross = lax.broadcasted_iota(jnp.int32, (comps, comps), 1)
    diagonal = jnp.where(line == cross, profile_ref[...].reshape(1, comps), 0.0)
    ones = jnp.ones((comps, lanes), BF16)
    high, low = split(diagonal)
    lowest = (diagonal - high.astype(F32) - low.astype(F32)).astype(BF16)
    column = sum(
        jnp.dot(part, ones, preferred_element_type=F32) for part in (high, low, lowest)
    )
    for k in range(rows):
        spread_ref[pl.ds(k, comps, stride=rows), :] = column


def planes_kernel(
    first_plane,
    planes,
    sectors,
    flat_ref,
    op_ref,
    swapped_ref,
    second_ref,
    *refs,
):
    out_refs = refs[:-1]
    stack_ref = refs[-1]
    comps = flat_ref.shape[0]
    width = flat_ref.shape[1] // planes
    group = NODE * NODE
    faces = NVAR * group
    block = width // sectors
    tiles = block // LANES
    rows = sectors * tiles
    comp = lax.broadcasted_iota(jnp.int32, (comps, block), 0)
    lane = lax.broadcasted_iota(jnp.int32, (comps, block), 1)
    q = (comp // NODE) % NODE
    w = comp % NODE
    q_top = (q == NODE - 1).astype(F32).astype(BF16)
    q_low = (q == 0).astype(F32).astype(BF16)
    w_top = ((w == NODE - 1) & (lane > 0)).astype(F32).astype(BF16)
    w_low = ((w == 0) & (lane < block - 1)).astype(F32).astype(BF16)
    odd = core_of() == 1

    def second(v):
        if second_ref.shape[0] == faces:
            return second_ref[v * group : (v + 1) * group, :]
        return jnp.zeros((group, width), BF16)

    def first(v):
        return swapped_ref[faces + v * group : faces + (v + 1) * group, :]

    for n, out_ref in enumerate(out_refs):
        x = first_plane + n
        here = x * width
        own = flat_ref[:, here : here + width]
        stack_ref[n, :comps, :] = own
        for v in range(NVAR):
            low_row = v * NODE * group
            top_row = low_row + (NODE - 1) * group
            at = comps + v * group
            if x > 0:
                value = flat_ref[top_row : top_row + group, here - width : here]
            else:
                value = jnp.where(odd, first(v), second(v))
            stack_ref[n, at : at + group, :] = value
            at += faces
            if x < planes - 1:
                value = flat_ref[low_row : low_row + group, here + width : here + 2 * width]
            else:
                value = jnp.where(odd, second(v), first(v))
            stack_ref[n, at : at + group, :] = value
        mix = comps + 2 * faces
        for a in range(sectors):
            at = a * block
            columns = slice(at, at + block)
            part = flat_ref[:, here + at : here + at + block]
            sector = None
            if a > 0:
                sector = q_top * flat_ref[:, here + at - block : here + at]
            if a < sectors - 1:
                right = q_low * flat_ref[:, here + at + block : here + at + 2 * block]
                sector = right if sector is None else sector + right
            if sector is None:
                sector = jnp.zeros((comps, block), BF16)
            stack_ref[n, mix : mix + comps, columns] = sector
            stack_ref[n, mix + comps :, columns] = w_top * pltpu.roll(
                part, 1, 1
            ) + w_low * pltpu.roll(part, block - 1, 1)
        result = jnp.dot(op_ref[...], stack_ref[n], preferred_element_type=F32)
        for k in range(rows):
            j, a = divmod(k, sectors)
            at = (a * tiles + j) * LANES
            out_ref[pl.ds(k, comps, stride=rows), :] = result[:, at : at + LANES] + own[
                :, at : at + LANES
            ].astype(F32)


def edge_kernel(planes, sectors, edge_ref, crossed_ref, back_ref, *refs):
    base_refs, out_refs = refs[:planes], refs[planes:]
    faces = back_ref.shape[0]
    block = back_ref.shape[1] // planes
    tiles = block // LANES
    rows = sectors * tiles
    comps = edge_ref.shape[0]
    top = mine_is_top()
    for x in range(planes):
        columns = slice(x * block, (x + 1) * block)
        crossed = crossed_ref[:faces, columns]
        back = back_ref[:, columns]
        for side, a in ((0, 0), (1, sectors - 1)):
            halo = jnp.where(top, crossed, back) if side else jnp.where(top, back, crossed)
            term = jnp.dot(
                edge_ref[:, side * LANES : side * LANES + faces],
                halo,
                preferred_element_type=F32,
            )
            for j in range(tiles):
                place = pl.ds(j * sectors + a, comps, stride=rows)
                out_refs[x][place, :] = (
                    base_refs[x][place, :] + term[:, j * LANES : (j + 1) * LANES]
                )


def strength_part(v_ref, sens, radiation):
    blocks = v_ref.shape[0]
    points = radiation.shape[1]
    combined = jnp.dot(
        v_ref[...], sens, preferred_element_type=F32, precision=lax.Precision.HIGHEST
    )
    both = jnp.concatenate(split(combined), axis=0)
    product = jnp.dot(both, radiation, preferred_element_type=F32)
    product = product[:blocks] + product[blocks:]
    block = lax.broadcasted_iota(jnp.int32, (blocks, points), 0)
    point = lax.broadcasted_iota(jnp.int32, (blocks, points), 1)
    return jnp.sum(
        jnp.where(block == point // (points // blocks), product, 0.0), axis=0, keepdims=True
    )


def sensitivity(sums, half, taper_ref, weights_ref, target_ref):
    width = sums.shape[1]
    columns = pl.ds(pl.multiple_of(half * width, width), width)
    return weights_ref[:, columns] * taper_ref[...] * (sums - target_ref[:, columns])


def own_kernel(sums_ref, taper_ref, weights_ref, target_ref, v_ref, radiation_ref, part_ref, sens_ref):
    sens = sensitivity(sums_ref[...], core_of(), taper_ref, weights_ref, target_ref)
    sens_ref[...] = sens
    part_ref[...] = strength_part(v_ref, sens, radiation_ref[...])


def final_kernel(
    tiles,
    chunks,
    other_ref,
    own_sens_ref,
    taper_ref,
    weights_ref,
    target_ref,
    v_ref,
    radiation_ref,
    part_ref,
    host_ref,
    hot_ref,
    spread_ref,
    *rest,
):
    planes = len(rest) - 5
    base_refs = rest[:planes]
    sens_ref, out_hbm, all_ref, buffer_ref, sems = rest[planes:]
    comps, _, rows, lanes = out_hbm.shape
    far = 1 - core_of()
    half = radiation_ref.shape[0]
    start = pl.multiple_of(far * half, half)
    sens = sensitivity(other_ref[...], far, taper_ref, weights_ref, target_ref)
    strength = part_ref[...] + strength_part(v_ref, sens, radiation_ref[...])
    host = host_ref[...]
    sectors = rows // tiles
    per_plane = rows * lanes
    row = (
        (host // per_plane) * rows
        + ((host // lanes) % tiles) * sectors
        + (host // (lanes * tiles)) % sectors
    )
    at = lax.broadcasted_iota(jnp.int32, (planes * rows, host.shape[1]), 0)
    placed = jnp.where(at == row, strength, 0.0)
    gathered = lax.dot_general(
        jnp.concatenate(split(placed), axis=0),
        hot_ref[...],
        (((1,), (1,)), ((), ())),
        preferred_element_type=F32,
    )
    source = gathered[: planes * rows] + gathered[planes * rows :]
    chunk = comps // chunks
    copies = []
    for n in range(chunks):
        part = slice(n * chunk, (n + 1) * chunk)
        lines = slice(n * chunk * rows, (n + 1) * chunk * rows)
        spread = spread_ref[lines, :].reshape(chunk, rows, lanes)
        for x in range(planes):
            buffer_ref[part, x] = (
                base_refs[x][lines, :].reshape(chunk, rows, lanes)
                + spread * source[x * rows : (x + 1) * rows][None]
            )
        copy = pltpu.make_async_copy(buffer_ref.at[part], out_hbm.at[part], sems.at[n])
        copy.start()
        copies.append(copy)

    all_ref[:, pl.ds(start, half)] = sens
    all_ref[:, pl.ds(pl.multiple_of((1 - far) * half, half), half)] = own_sens_ref[...]
    count = sens_ref.shape[1]
    first = lax.axis_index("azim") * count
    aligned = pl.multiple_of((first // LANES) * LANES, LANES)
    window = all_ref[:, pl.ds(aligned, LANES)]
    turned = pltpu.roll(window, lax.rem(LANES - (first - aligned), LANES), 1)
    sens_ref[...] = turned[:, :count]
    for copy in copies:
        copy.wait()


def exchange(value, mask, devices):
    return lax.ppermute(value, MESH_AXES, [(i, i ^ mask) for i in range(devices)])


def body(
    surface_signal,
    retarded_weights,
    radiation_weights,
    target_signal,
    observer_weights,
    sample_weights,
    host_element,
    source_profile,
    adjoint_state,
    volume_operator,
    lift_operator,
):
    streams = lax.axis_size("stream")
    around = lax.axis_size("azim")
    devices = streams * around
    window, points = surface_signal.shape
    observers = radiation_weights.shape[0]
    half = observers // 2
    blocks = retarded_weights.shape[0]
    comps, planes, sectors, radial = adjoint_state.shape
    tiles = radial // LANES
    rows = sectors * tiles
    width = sectors * radial
    faces = NVAR * NODE * NODE
    barrier = lax.optimization_barrier
    depth = 3 * comps + 2 * faces

    view = (
        adjoint_state.reshape(comps, planes, sectors, tiles, LANES)
        .transpose(0, 1, 3, 2, 4)
        .reshape(comps, planes, rows, LANES)
    )
    send, delayed, far, state, retarded, swap, mine, second = call(
        lambda *refs: start_kernel(sectors, *refs),
        [HBM] * 4,
        [
            vmem((window, half), F32),
            vmem((window, points), BF16),
            vmem((half, points), BF16),
            vmem(view.shape, BF16),
            vmem(retarded_weights.shape, BF16),
            vmem((2 * faces, width), BF16),
            vmem((faces, planes * radial), BF16),
            vmem((faces if streams > 2 else 16, width), BF16),
        ],
        [in_hbm(x) for x in (surface_signal, retarded_weights, radiation_weights, view)],
        [
            pltpu.VMEM((window, points), BF16),
            pltpu.VMEM((faces * rows, LANES), F32),
            pltpu.SemaphoreType.DMA((4 + NODE,)),
        ],
    )
    received = exchange(send, around, devices)
    swapped = exchange(swap, around, devices)
    small = [
        target_signal,
        observer_weights.reshape(1, observers),
        sample_weights.reshape(1, window),
        host_element.reshape(1, points),
        source_profile,
        volume_operator,
        lift_operator,
    ]
    own, near, target, weights, samples, host, profile, volume, lift = call(
        lambda *refs: near_kernel(len(small), *refs),
        [VMEM] + [HBM] * (1 + len(small)),
        [vmem((window, half), F32), vmem((half, points), BF16)]
        + [vmem(x.shape, x.dtype) for x in small],
        [delayed] + [in_hbm(x) for x in [radiation_weights] + small],
        [pltpu.SemaphoreType.DMA((2 + len(small),))],
    )
    low = (own + received).astype(BF16)
    low, state = barrier((low, state))

    bits = [1 << n for n in range((around - 1).bit_length())]
    bits += [around << n for n in range(1, (streams - 1).bit_length())]
    stages = []
    for first in range(0, len(bits), 2):
        pair = bits[first : first + 2]
        stages.append(pair + ([pair[0] | pair[1]] if len(pair) == 2 else []))

    inner = [(i, i ^ 1) for i in range(around)]
    outer = [(i, (i + 1 if i % 2 else i - 1) % around) for i in range(around)]
    pairs = []
    for s in range(streams):
        pairs += [(s * around + i, s * around + j) for i, j in (outer if s % 2 else inner)]
    pay = call(
        pack_kernel, [VMEM] * 2, [vmem((2 * faces, planes * radial), BF16)], [mine, swapped]
    )[0]
    crossed = lax.ppermute(pay, MESH_AXES, pairs)
    parts = [exchange(low, mask, devices) for mask in stages[0]]
    if streams > 2:
        links = [(s, s + 1) for s in range(1, streams - 1, 2)]
        second = lax.ppermute(second, "stream", links + [(b, a) for a, b in links])
    flat, operator, edge, v, hot, spread = call(
        lambda *refs: prepare_kernel(sectors, *refs),
        [VMEM] * 7,
        [
            vmem((comps, planes * width), BF16),
            vmem((comps, depth), BF16),
            vmem((comps, 2 * LANES), BF16),
            vmem((blocks, window), F32),
            vmem((LANES, points), BF16),
            vmem((comps * rows, LANES), F32),
        ],
        [state, volume, lift, retarded, samples, host, profile],
        [pltpu.VMEM((planes, comps * rows, LANES), F32)],
        nbytes=12 * 2**20,
    )

    def combine(low, parts):
        total = low.astype(F32) + parts[0].astype(F32)
        if len(parts) == 3:
            total = total + (parts[1].astype(F32) + parts[2].astype(F32))
        return total

    parts, flat = barrier((parts, flat))
    sums = combine(low, parts)
    low = sums.astype(BF16)

    def run_planes(first, count):
        return call(
            lambda *refs: planes_kernel(first, planes, sectors, *refs),
            [VMEM] * 4,
            [vmem((comps * rows, LANES), F32)] * count,
            [flat, operator, swapped, second],
            [pltpu.VMEM((count, depth, width), BF16)],
            flops=2 * comps * depth * width * count,
            nbytes=count * 4 * 2**20,
        )

    bases = []
    for masks in stages[1:]:
        parts = [exchange(low, mask, devices) for mask in masks]
        if not bases:
            bases = run_planes(0, planes // 2)
            parts, bases = barrier((parts, bases))
            bases = list(bases) + list(run_planes(planes // 2, planes // 2))
        sums = combine(low, parts)
        low = sums.astype(BF16)

    remote = exchange(sums, around, devices)
    taper = np.arange(window, dtype=np.float64)
    taper = (0.5 - 0.5 * np.cos(2.0 * np.pi * (taper + 0.5) / window)).astype(np.float32)
    taper = jnp.asarray(taper).reshape(window, 1)
    part, own_sens = call(
        own_kernel,
        [VMEM] * 6,
        [vmem((1, points), F32), vmem((window, half), F32)],
        [sums, taper, weights, target, v, near],
        flops=2 * 2 * blocks * half * points,
        nbytes=half * points * 2,
    )
    crossed, remote = barrier((crossed, remote))
    back = exchange(crossed[faces:], around, devices)
    bases = call(
        lambda *refs: edge_kernel(planes, sectors, *refs),
        [VMEM] * (3 + planes),
        [vmem(x.shape, F32) for x in bases],
        [edge, crossed, back] + list(bases),
        nbytes=4 * 2**20,
        aliases={3 + n: n for n in range(planes)},
    )
    chunks = 8
    sens, updated = call(
        lambda *refs: final_kernel(tiles, chunks, *refs),
        [VMEM] * (11 + planes),
        [
            jax.ShapeDtypeStruct((window, observers // around), F32),
            jax.ShapeDtypeStruct(view.shape, F32),
        ],
        [remote, own_sens, taper, weights, target, v, far, part, host, hot, spread]
        + list(bases),
        [
            pltpu.VMEM((window, observers), F32),
            pltpu.VMEM(view.shape, F32),
            pltpu.SemaphoreType.DMA((chunks,)),
        ],
        nbytes=12 * 2**20,
        out_specs=[VMEM, HBM],
    )
    updated = (
        updated.reshape(comps, planes, tiles, sectors, LANES)
        .transpose(0, 1, 3, 2, 4)
        .reshape(adjoint_state.shape)
    )
    return sens, updated


def solution(mesh):
    return jax.shard_map(
        body,
        mesh=mesh,
        in_specs=(
            P(None, ("stream", "azim")),
            P(("stream", "azim"), None, None),
            P(None, ("stream", "azim")),
            P(),
            P(),
            P(),
            P(("stream", "azim")),
            P(),
            P(None, "stream", "azim", None),
            P(),
            P(),
        ),
        out_specs=(P(None, "azim"), P(None, "stream", "azim", None)),
        check_vma=False,
    )
```

```python
import jax
import jax.numpy as jnp
import numpy as np
from jax import lax
from jax.experimental import pallas as pl
from jax.experimental.pallas import tpu as pltpu
from jax.sharding import PartitionSpec as P

NVAR = 5
NODE = 4
LANES = 128
F32 = jnp.float32
BF16 = jnp.bfloat16
MESH_AXES = ("stream", "azim")
VMEM = pl.BlockSpec(memory_space=pltpu.VMEM)
HBM = pl.BlockSpec(memory_space=pl.ANY)


def vmem(shape, dtype):
    return pltpu.VMEM(shape, dtype)


def in_hbm(x):
    return pltpu.with_memory_space_constraint(x, pltpu.HBM)


def call(kernel, ins, outs, args, scratch=(), mib=16, flops=0, nbytes=0, out_specs=None, aliases=None):
    return pl.pallas_call(
        kernel,
        in_specs=ins,
        out_specs=out_specs or [VMEM] * len(outs),
        out_shape=outs,
        scratch_shapes=list(scratch),
        input_output_aliases=aliases or {},
        compiler_params=pltpu.CompilerParams(vmem_limit_bytes=mib * 2**20),
        cost_estimate=pl.CostEstimate(flops=flops, bytes_accessed=nbytes, transcendentals=0),
    )(*args)


def core_of():
    return lax.rem(lax.axis_index("stream"), 2)


def mine_is_top():
    return core_of() == lax.rem(lax.axis_index("azim"), 2)


def quotient(x, n):
    return x >> (n.bit_length() - 1) if n & (n - 1) == 0 else x // n


def remainder(x, n):
    return x & (n - 1) if n & (n - 1) == 0 else x % n


def split(x):
    high = x.astype(BF16)
    return high, (x - high.astype(F32)).astype(BF16)


def project(delayed, radiation):
    return lax.dot_general(
        delayed, radiation, (((1,), (1,)), ((), ())), preferred_element_type=F32
    )


def started(pairs, sems):
    copies = [
        pltpu.make_async_copy(source, target, sems.at[n])
        for n, (source, target) in enumerate(pairs)
    ]
    for copy in copies:
        copy.start()
    return copies


def start_kernel(sectors, count, signal_hbm, weights_hbm, radiation_hbm, state_hbm, *refs):
    small_hbm, refs = refs[:count], refs[count:]
    send_ref, delayed_ref, far_ref, near_ref, state_ref, weights_ref, *refs = refs
    swap_ref, mine_ref, second_ref, *refs = refs
    small_ref, (signal_ref, rows_ref, sems) = refs[:count], refs[count:]
    comps, planes, rows, lanes = state_ref.shape
    tiles = rows // sectors
    block = tiles * lanes
    group = NODE * NODE
    faces = NVAR * group
    half = far_ref.shape[0]
    chunk = half // 2
    core = core_of()
    far = pl.multiple_of((1 - core) * half, half)
    near = pl.multiple_of(core * half, half)
    pairs = [(signal_hbm, signal_ref), (weights_hbm, weights_ref)]
    for first in (0, chunk):
        pairs.append(
            (radiation_hbm.at[pl.ds(far + first, chunk)], far_ref.at[pl.ds(first, chunk)])
        )
    quarter = comps // NODE
    for first in range(0, comps, quarter):
        part = pl.ds(first, quarter)
        pairs.append((state_hbm.at[part], state_ref.at[part]))
    ready = len(pairs)
    pairs.append((radiation_hbm.at[pl.ds(near, half)], near_ref))
    pairs += zip(small_hbm, small_ref)
    copies = started(pairs, sems)
    copies[0].wait()
    copies[1].wait()
    blocks = weights_ref.shape[0]
    width = signal_ref.shape[1] // blocks
    for b in range(blocks):
        columns = slice(b * width, (b + 1) * width)
        delayed_ref[:, columns] = lax.dot_general(
            weights_ref[b],
            signal_ref[:, columns],
            (((0,), (0,)), ((), ())),
            preferred_element_type=F32,
        ).astype(BF16)
    copies[2].wait()
    send_ref[:, :chunk] = project(delayed_ref[...], far_ref[:chunk, :])
    copies[3].wait()
    send_ref[:, chunk:] = project(delayed_ref[...], far_ref[chunk:, :])
    for copy in copies[4:ready]:
        copy.wait()

    def gather(x, offsets, count):
        for n, offset in enumerate(offsets):
            rows_ref[n * count * rows : (n + 1) * count * rows, :] = (
                state_ref[pl.ds(offset, count), x].astype(F32).reshape(count * rows, lanes)
            )

    def picked(k):
        return rows_ref[pl.ds(k, faces, stride=rows), :].astype(BF16)

    top = mine_is_top()
    for at_top in (0, 1):
        mine_here = top if at_top else jnp.logical_not(top)
        offset = at_top * (NODE - 1) * NODE
        a = at_top * (sectors - 1)
        for x in range(planes):
            gather(x, [n * group + offset for n in range(NVAR * NODE)], NODE)
            for j in range(tiles):
                columns = slice(x * block + j * lanes, x * block + (j + 1) * lanes)
                value = picked(j * sectors + a)

                @pl.when(mine_here)
                def _():
                    mine_ref[:, columns] = value

                @pl.when(jnp.logical_not(mine_here))
                def _():
                    swap_ref[:faces, columns] = value

    def plane_face(at_top, put):
        x = at_top * (planes - 1)
        first = at_top * ((NODE - 1) * group)
        gather(x, [v * NODE * group + first for v in range(NVAR)], group)
        for k in range(rows):
            j, a = divmod(k, sectors)
            first_lane = (a * tiles + j) * lanes
            put(slice(first_lane, first_lane + lanes), picked(k))

    def put_swap(columns, value):
        swap_ref[faces:, columns] = value

    def put_second(columns, value):
        second_ref[:, columns] = value

    plane_face(1 - core, put_swap)
    if second_ref.shape[0] == faces:
        plane_face(core, put_second)
    else:
        second_ref[...] = jnp.zeros(second_ref.shape, BF16)
    for copy in copies[ready:]:
        copy.wait()


def near_kernel(delayed_ref, near_ref, own_ref):
    own_ref[...] = project(delayed_ref[...], near_ref[...])


def pack_kernel(mine_ref, swapped_ref, pay_ref):
    faces = mine_ref.shape[0]
    pay_ref[:faces, :] = mine_ref[...]
    pay_ref[faces:, :] = swapped_ref[:faces, :]


def prepare_kernel(
    sectors,
    state_ref,
    volume_ref,
    lift_ref,
    weights_ref,
    samples_ref,
    host_ref,
    profile_ref,
    flat_ref,
    op_ref,
    edge_ref,
    v_ref,
    hot_ref,
    row_ref,
    spread_ref,
    plane_ref,
):
    comps, planes, rows, lanes = state_ref.shape
    tiles = rows // sectors
    width = sectors * tiles * lanes
    group = NODE * NODE
    faces = NVAR * group
    for x in range(planes):
        plane_ref[x] = state_ref[:, x].astype(F32).reshape(comps * rows, lanes)
        for k in range(rows):
            j, a = divmod(k, sectors)
            first = x * width + (a * tiles + j) * lanes
            flat_ref[:, first : first + lanes] = plane_ref[
                x, pl.ds(k, comps, stride=rows), :
            ].astype(BF16)
    op_ref[:, :comps] = volume_ref[...]
    op_ref[:, comps : comps + 2 * faces] = lift_ref[:, : 2 * faces]
    face = lax.broadcasted_iota(jnp.int32, (2 * faces, comps), 0)
    comp = lax.broadcasted_iota(jnp.int32, (2 * faces, comps), 1)
    upper = (face < faces).astype(jnp.int32) * (NODE - 1)
    row = jnp.where(face < faces, face, face - faces)
    sector_at = quotient(row, NODE) * group + remainder(row, NODE) + upper * NODE
    radial_at = row * NODE + upper
    first = comps + 2 * faces
    for at, start in ((sector_at, 2 * faces), (radial_at, 4 * faces)):
        place = (comp == at).astype(F32).astype(BF16)
        op_ref[:, first : first + comps] = jnp.dot(
            lift_ref[:, start : start + 2 * faces], place, preferred_element_type=F32
        ).astype(BF16)
        first += comps
    edge_ref[:, :faces] = lift_ref[:, 2 * faces : 3 * faces]
    edge_ref[:, LANES : LANES + faces] = lift_ref[:, 3 * faces : 4 * faces]

    blocks, window, _ = weights_ref.shape
    samples = jnp.concatenate([samples_ref[...]] * blocks, axis=1)
    owner = lax.broadcasted_iota(jnp.int32, (blocks, blocks * window), 0)
    entry = lax.broadcasted_iota(jnp.int32, (blocks, blocks * window), 1)
    chosen = jnp.where(owner == quotient(entry, window), samples, 0.0)
    stacked = weights_ref[...].reshape(blocks * window, window)
    v_ref[...] = sum(
        jnp.dot(part, stacked, preferred_element_type=F32) for part in split(chosen)
    )
    points = hot_ref.shape[1]
    within = lax.broadcasted_iota(jnp.int32, (lanes, points), 0)
    host = host_ref[...]
    hot_ref[...] = (within == remainder(host, lanes)).astype(F32).astype(BF16)
    row_ref[...] = (
        quotient(host, rows * lanes) * rows
        + remainder(quotient(host, lanes), tiles) * sectors
        + remainder(quotient(host, lanes * tiles), sectors)
    )

    line = lax.broadcasted_iota(jnp.int32, (comps, comps), 0)
    cross = lax.broadcasted_iota(jnp.int32, (comps, comps), 1)
    diagonal = jnp.where(line == cross, profile_ref[...].reshape(1, comps), 0.0)
    ones = jnp.ones((comps, lanes), BF16)
    high, low = split(diagonal)
    lowest = (diagonal - high.astype(F32) - low.astype(F32)).astype(BF16)
    column = sum(
        jnp.dot(part, ones, preferred_element_type=F32) for part in (high, low, lowest)
    )
    for k in range(rows):
        spread_ref[pl.ds(k, comps, stride=rows), :] = column


def planes_kernel(
    first_plane,
    planes,
    sectors,
    flat_ref,
    op_ref,
    swapped_ref,
    second_ref,
    *refs,
):
    out_refs = refs[:-1]
    stack_ref = refs[-1]
    comps = flat_ref.shape[0]
    width = flat_ref.shape[1] // planes
    group = NODE * NODE
    faces = NVAR * group
    block = width // sectors
    tiles = block // LANES
    rows = sectors * tiles
    comp = lax.broadcasted_iota(jnp.int32, (comps, block), 0)
    lane = lax.broadcasted_iota(jnp.int32, (comps, block), 1)
    q = remainder(quotient(comp, NODE), NODE)
    w = remainder(comp, NODE)
    q_top = (q == NODE - 1).astype(F32).astype(BF16)
    q_low = (q == 0).astype(F32).astype(BF16)
    w_top = ((w == NODE - 1) & (lane > 0)).astype(F32).astype(BF16)
    w_low = ((w == 0) & (lane < block - 1)).astype(F32).astype(BF16)
    odd = core_of() == 1

    def second(v):
        if second_ref.shape[0] == faces:
            return second_ref[v * group : (v + 1) * group, :]
        return jnp.zeros((group, width), BF16)

    def first(v):
        return swapped_ref[faces + v * group : faces + (v + 1) * group, :]

    for n, out_ref in enumerate(out_refs):
        x = first_plane + n
        here = x * width
        own = flat_ref[:, here : here + width]
        stack_ref[n, :comps, :] = own
        for v in range(NVAR):
            low_row = v * NODE * group
            top_row = low_row + (NODE - 1) * group
            at = comps + v * group
            if x > 0:
                value = flat_ref[top_row : top_row + group, here - width : here]
            else:
                value = jnp.where(odd, first(v), second(v))
            stack_ref[n, at : at + group, :] = value
            at += faces
            if x < planes - 1:
                value = flat_ref[low_row : low_row + group, here + width : here + 2 * width]
            else:
                value = jnp.where(odd, second(v), first(v))
            stack_ref[n, at : at + group, :] = value
        mix = comps + 2 * faces
        for a in range(sectors):
            at = a * block
            columns = slice(at, at + block)
            part = flat_ref[:, here + at : here + at + block]
            sector = None
            if a > 0:
                sector = q_top * flat_ref[:, here + at - block : here + at]
            if a < sectors - 1:
                right = q_low * flat_ref[:, here + at + block : here + at + 2 * block]
                sector = right if sector is None else sector + right
            if sector is None:
                sector = jnp.zeros((comps, block), BF16)
            stack_ref[n, mix : mix + comps, columns] = sector
            stack_ref[n, mix + comps :, columns] = w_top * pltpu.roll(
                part, 1, 1
            ) + w_low * pltpu.roll(part, block - 1, 1)
        result = jnp.dot(op_ref[...], stack_ref[n], preferred_element_type=F32)
        for k in range(rows):
            j, a = divmod(k, sectors)
            at = (a * tiles + j) * LANES
            out_ref[pl.ds(k, comps, stride=rows), :] = result[:, at : at + LANES] + own[
                :, at : at + LANES
            ].astype(F32)


def strength_part(v_ref, sens, radiation):
    blocks = v_ref.shape[0]
    points = radiation.shape[1]
    v_high, v_low = split(v_ref[...])
    s_high, s_low = split(sens)
    combined = jnp.dot(
        jnp.concatenate([v_high, v_low, v_high], axis=1),
        jnp.concatenate([s_high, s_high, s_low], axis=0),
        preferred_element_type=F32,
    )
    both = jnp.concatenate(split(combined), axis=0)
    product = jnp.dot(both, radiation, preferred_element_type=F32)
    product = product[:blocks] + product[blocks:]
    block = lax.broadcasted_iota(jnp.int32, (blocks, points), 0)
    point = lax.broadcasted_iota(jnp.int32, (blocks, points), 1)
    chosen = block == quotient(point, points // blocks)
    return jnp.sum(jnp.where(chosen, product, 0.0), axis=0, keepdims=True)


def sensitivity(sums, half, taper_ref, weights_ref, target_ref):
    width = sums.shape[1]
    columns = pl.ds(pl.multiple_of(half * width, width), width)
    return weights_ref[:, columns] * taper_ref[...] * (sums - target_ref[:, columns])


def own_kernel(sums_ref, taper_ref, weights_ref, target_ref, v_ref, radiation_ref, part_ref, sens_ref):
    sens = sensitivity(sums_ref[...], core_of(), taper_ref, weights_ref, target_ref)
    sens_ref[...] = sens
    part_ref[...] = strength_part(v_ref, sens, radiation_ref[...])


def final_kernel(
    sectors,
    chunks,
    other_ref,
    own_sens_ref,
    taper_ref,
    weights_ref,
    target_ref,
    v_ref,
    far_ref,
    part_ref,
    row_ref,
    hot_ref,
    spread_ref,
    edge_ref,
    crossed_ref,
    back_ref,
    *rest,
):
    planes = len(rest) - 5
    base_refs = rest[:planes]
    sens_ref, out_hbm, all_ref, buffer_ref, sems = rest[planes:]
    comps, _, rows, lanes = out_hbm.shape
    tiles = rows // sectors
    block = tiles * lanes
    other_core = 1 - core_of()
    half = far_ref.shape[0]
    start = pl.multiple_of(other_core * half, half)
    sens = sensitivity(other_ref[...], other_core, taper_ref, weights_ref, target_ref)
    strength = part_ref[...] + strength_part(v_ref, sens, far_ref[...])
    at = lax.broadcasted_iota(jnp.int32, (planes * rows, strength.shape[1]), 0)
    placed = jnp.where(at == row_ref[...], strength, 0.0)
    gathered = lax.dot_general(
        jnp.concatenate(split(placed), axis=0),
        hot_ref[...],
        (((1,), (1,)), ((), ())),
        preferred_element_type=F32,
    )
    source = gathered[: planes * rows] + gathered[planes * rows :]
    faces = crossed_ref.shape[0] // 2
    top = mine_is_top()
    crossed = crossed_ref[:faces, :]
    back = back_ref[faces:, :]
    halos = (jnp.where(top, back, crossed), jnp.where(top, crossed, back))
    chunk = comps // chunks
    flat_ref = buffer_ref.reshape(comps * planes * rows, lanes)
    copies = []
    for n in range(chunks):
        part = slice(n * chunk, (n + 1) * chunk)
        lines = slice(n * chunk * rows, (n + 1) * chunk * rows)
        spread = spread_ref[lines, :].reshape(chunk, rows, lanes)
        for x in range(planes):
            buffer_ref[part, x] = (
                base_refs[x][lines, :].reshape(chunk, rows, lanes)
                + spread * source[x * rows : (x + 1) * rows][None]
            )
        for side, a in ((0, 0), (1, sectors - 1)):
            term = jnp.dot(
                edge_ref[part, side * LANES : side * LANES + faces],
                halos[side],
                preferred_element_type=F32,
            )
            for x in range(planes):
                for j in range(tiles):
                    first = (n * chunk * planes + x) * rows + j * sectors + a
                    place = pl.ds(first, chunk, stride=planes * rows)
                    column = x * block + j * lanes
                    flat_ref[place, :] = flat_ref[place, :] + term[:, column : column + lanes]
        copy = pltpu.make_async_copy(buffer_ref.at[part], out_hbm.at[part], sems.at[n])
        copy.start()
        copies.append(copy)

    all_ref[:, pl.ds(start, half)] = sens
    all_ref[:, pl.ds(pl.multiple_of((1 - other_core) * half, half), half)] = own_sens_ref[...]
    count = sens_ref.shape[1]
    first = lax.axis_index("azim") * count
    aligned = pl.multiple_of((first // LANES) * LANES, LANES)
    window = all_ref[:, pl.ds(aligned, LANES)]
    turned = pltpu.roll(window, lax.rem(LANES - (first - aligned), LANES), 1)
    sens_ref[...] = turned[:, :count]
    for copy in copies:
        copy.wait()


def exchange(value, mask, devices):
    return lax.ppermute(value, MESH_AXES, [(i, i ^ mask) for i in range(devices)])


def body(
    surface_signal,
    retarded_weights,
    radiation_weights,
    target_signal,
    observer_weights,
    sample_weights,
    host_element,
    source_profile,
    adjoint_state,
    volume_operator,
    lift_operator,
):
    streams = lax.axis_size("stream")
    around = lax.axis_size("azim")
    devices = streams * around
    window, points = surface_signal.shape
    observers = radiation_weights.shape[0]
    half = observers // 2
    blocks = retarded_weights.shape[0]
    comps, planes, sectors, radial = adjoint_state.shape
    tiles = radial // LANES
    rows = sectors * tiles
    width = sectors * radial
    faces = NVAR * NODE * NODE
    barrier = lax.optimization_barrier
    depth = 3 * comps + 2 * faces

    view = (
        adjoint_state.reshape(comps, planes, sectors, tiles, LANES)
        .transpose(0, 1, 3, 2, 4)
        .reshape(comps, planes, rows, LANES)
    )
    small = [
        target_signal,
        observer_weights.reshape(1, observers),
        sample_weights.reshape(1, window),
        host_element.reshape(1, points),
        source_profile,
        volume_operator,
        lift_operator,
    ]
    large = [surface_signal, retarded_weights, radiation_weights, view]
    send, delayed, far, near, state, retarded, swap, mine, second, *small = call(
        lambda *refs: start_kernel(sectors, len(small), *refs),
        [HBM] * len(large + small),
        [
            vmem((window, half), F32),
            vmem((window, points), BF16),
            vmem((half, points), BF16),
            vmem((half, points), BF16),
            vmem(view.shape, BF16),
            vmem(retarded_weights.shape, BF16),
            vmem((2 * faces, width), BF16),
            vmem((faces, planes * radial), BF16),
            vmem((faces if streams > 2 else 16, width), BF16),
        ]
        + [vmem(x.shape, x.dtype) for x in small],
        [in_hbm(x) for x in large + small],
        [
            pltpu.VMEM((window, points), BF16),
            pltpu.VMEM((faces * rows, LANES), F32),
            pltpu.SemaphoreType.DMA((5 + NODE + len(small),)),
        ],
    )
    target, weights, samples, host, profile, volume, lift = small
    received = exchange(send, around, devices)
    swapped = exchange(swap, around, devices)
    own = call(near_kernel, [VMEM] * 2, [vmem((window, half), F32)], [delayed, near])[0]
    low = (own + received).astype(BF16)
    low, state = barrier((low, state))

    bits = [1 << n for n in range((around - 1).bit_length())]
    bits += [around << n for n in range(1, (streams - 1).bit_length())]
    stages = []
    for first in range(0, len(bits), 2):
        pair = bits[first : first + 2]
        stages.append(([pair[0] | pair[1]] if len(pair) == 2 else []) + pair[::-1])

    inner = [(i, i ^ 1) for i in range(around)]
    outer = [(i, (i + 1 if i % 2 else i - 1) % around) for i in range(around)]
    pairs = []
    for s in range(streams):
        pairs += [(s * around + i, s * around + j) for i, j in (outer if s % 2 else inner)]
    pay = call(
        pack_kernel, [VMEM] * 2, [vmem((2 * faces, planes * radial), BF16)], [mine, swapped]
    )[0]
    crossed = lax.ppermute(pay, MESH_AXES, pairs)
    parts = [exchange(low, mask, devices) for mask in stages[0]]
    if streams > 2:
        links = [(s, s + 1) for s in range(1, streams - 1, 2)]
        second = lax.ppermute(second, "stream", links + [(b, a) for a, b in links])
    flat, operator, edge, v, hot, row, spread = call(
        lambda *refs: prepare_kernel(sectors, *refs),
        [VMEM] * 7,
        [
            vmem((comps, planes * width), BF16),
            vmem((comps, depth), BF16),
            vmem((comps, 2 * LANES), BF16),
            vmem((blocks, window), F32),
            vmem((LANES, points), BF16),
            vmem((1, points), jnp.int32),
            vmem((comps * rows, LANES), F32),
        ],
        [state, volume, lift, retarded, samples, host, profile],
        [pltpu.VMEM((planes, comps * rows, LANES), F32)],
        nbytes=12 * 2**20,
    )

    def combine(low, parts):
        total = low.astype(F32) + parts[0].astype(F32)
        if len(parts) == 3:
            total = total + (parts[1].astype(F32) + parts[2].astype(F32))
        return total

    parts, flat = barrier((parts, flat))
    sums = combine(low, parts)
    low = sums.astype(BF16)

    def run_planes(first, count):
        return call(
            lambda *refs: planes_kernel(first, planes, sectors, *refs),
            [VMEM] * 4,
            [vmem((comps * rows, LANES), F32)] * count,
            [flat, operator, swapped, second],
            [pltpu.VMEM((count, depth, width), BF16)],
            flops=2 * comps * depth * width * count,
            nbytes=count * 4 * 2**20,
        )

    bases = []
    for masks in stages[1:]:
        parts = [exchange(low, mask, devices) for mask in masks]
        if not bases:
            bases = list(run_planes(0, planes // 2)) + list(run_planes(planes // 2, planes // 2))
            parts, bases = barrier((parts, bases))
        sums = combine(low, parts)
        low = sums.astype(BF16)

    remote = exchange(sums, around, devices)
    crossed, bases = barrier((crossed, bases))
    back = exchange(crossed, around, devices)
    taper = np.arange(window, dtype=np.float64)
    taper = (0.5 - 0.5 * np.cos(2.0 * np.pi * (taper + 0.5) / window)).astype(np.float32)
    taper = jnp.asarray(taper).reshape(window, 1)
    part, own_sens = call(
        own_kernel,
        [VMEM] * 6,
        [vmem((1, points), F32), vmem((window, half), F32)],
        [sums, taper, weights, target, v, near],
        flops=2 * 2 * blocks * half * points,
        nbytes=half * points * 2,
    )
    chunks = 5
    sens, updated = call(
        lambda *refs: final_kernel(sectors, chunks, *refs),
        [VMEM] * (14 + planes),
        [
            jax.ShapeDtypeStruct((window, observers // around), F32),
            jax.ShapeDtypeStruct(view.shape, F32),
        ],
        [remote, own_sens, taper, weights, target, v, far, part, row, hot, spread]
        + [edge, crossed, back]
        + list(bases),
        [
            pltpu.VMEM((window, observers), F32),
            pltpu.VMEM(view.shape, F32),
            pltpu.SemaphoreType.DMA((chunks,)),
        ],
        nbytes=12 * 2**20,
        out_specs=[VMEM, HBM],
    )
    updated = (
        updated.reshape(comps, planes, tiles, sectors, LANES)
        .transpose(0, 1, 3, 2, 4)
        .reshape(adjoint_state.shape)
    )
    return sens, updated


def solution(mesh):
    return jax.shard_map(
        body,
        mesh=mesh,
        in_specs=(
            P(None, ("stream", "azim")),
            P(("stream", "azim"), None, None),
            P(None, ("stream", "azim")),
            P(),
            P(),
            P(),
            P(("stream", "azim")),
            P(),
            P(None, "stream", "azim", None),
            P(),
            P(),
        ),
        out_specs=(P(None, "azim"), P(None, "stream", "azim", None)),
        check_vma=False,
    )
```

```python
import jax
import jax.numpy as jnp
import numpy as np
from jax import lax
from jax.experimental import pallas as pl
from jax.experimental.pallas import tpu as pltpu
from jax.sharding import PartitionSpec as P

NVAR = 5
NODE = 4
LANES = 128
F32 = jnp.float32
BF16 = jnp.bfloat16
MESH_AXES = ("stream", "azim")
VMEM = pl.BlockSpec(memory_space=pltpu.VMEM)
HBM = pl.BlockSpec(memory_space=pl.ANY)


def vmem(shape, dtype):
    return pltpu.VMEM(shape, dtype)


def in_hbm(x):
    return pltpu.with_memory_space_constraint(x, pltpu.HBM)


def call(kernel, ins, outs, args, scratch=(), mib=16, flops=0, nbytes=0, out_specs=None, aliases=None):
    return pl.pallas_call(
        kernel,
        in_specs=ins,
        out_specs=out_specs or [VMEM] * len(outs),
        out_shape=outs,
        scratch_shapes=list(scratch),
        input_output_aliases=aliases or {},
        compiler_params=pltpu.CompilerParams(vmem_limit_bytes=mib * 2**20),
        cost_estimate=pl.CostEstimate(flops=flops, bytes_accessed=nbytes, transcendentals=0),
    )(*args)


def core_of():
    return lax.rem(lax.axis_index("stream"), 2)


def mine_is_top():
    return core_of() == lax.rem(lax.axis_index("azim"), 2)


def quotient(x, n):
    return x >> (n.bit_length() - 1) if n & (n - 1) == 0 else x // n


def remainder(x, n):
    return x & (n - 1) if n & (n - 1) == 0 else x % n


def split(x):
    high = x.astype(BF16)
    return high, (x - high.astype(F32)).astype(BF16)


def project(delayed, radiation):
    return lax.dot_general(
        delayed, radiation, (((1,), (1,)), ((), ())), preferred_element_type=F32
    )


def started(pairs, sems):
    copies = [
        pltpu.make_async_copy(source, target, sems.at[n])
        for n, (source, target) in enumerate(pairs)
    ]
    for copy in copies:
        copy.start()
    return copies


def start_kernel(sectors, count, signal_hbm, weights_hbm, radiation_hbm, state_hbm, *refs):
    small_hbm, refs = refs[:count], refs[count:]
    send_ref, delayed_ref, far_ref, near_ref, state_ref, weights_ref, *refs = refs
    swap_ref, mine_ref, second_ref, *refs = refs
    small_ref, (signal_ref, rows_ref, sems) = refs[:count], refs[count:]
    comps, planes, rows, lanes = state_ref.shape
    tiles = rows // sectors
    block = tiles * lanes
    group = NODE * NODE
    faces = NVAR * group
    half = far_ref.shape[0]
    chunk = half // 2
    core = core_of()
    far = pl.multiple_of((1 - core) * half, half)
    near = pl.multiple_of(core * half, half)
    pairs = [(signal_hbm, signal_ref), (weights_hbm, weights_ref)]
    for first in (0, chunk):
        pairs.append(
            (radiation_hbm.at[pl.ds(far + first, chunk)], far_ref.at[pl.ds(first, chunk)])
        )
    quarter = comps // NODE
    for first in range(0, comps, quarter):
        part = pl.ds(first, quarter)
        pairs.append((state_hbm.at[part], state_ref.at[part]))
    ready = len(pairs)
    pairs.append((radiation_hbm.at[pl.ds(near, half)], near_ref))
    pairs += zip(small_hbm, small_ref)
    copies = started(pairs, sems)
    copies[0].wait()
    copies[1].wait()
    blocks = weights_ref.shape[0]
    width = signal_ref.shape[1] // blocks
    for b in range(blocks):
        columns = slice(b * width, (b + 1) * width)
        delayed_ref[:, columns] = lax.dot_general(
            weights_ref[b],
            signal_ref[:, columns],
            (((0,), (0,)), ((), ())),
            preferred_element_type=F32,
        ).astype(BF16)
    copies[2].wait()
    send_ref[:, :chunk] = project(delayed_ref[...], far_ref[:chunk, :])
    copies[3].wait()
    send_ref[:, chunk:] = project(delayed_ref[...], far_ref[chunk:, :])
    for copy in copies[4:ready]:
        copy.wait()

    def gather(x, offsets, count):
        for n, offset in enumerate(offsets):
            rows_ref[n * count * rows : (n + 1) * count * rows, :] = (
                state_ref[pl.ds(offset, count), x].astype(F32).reshape(count * rows, lanes)
            )

    def picked(k):
        return rows_ref[pl.ds(k, faces, stride=rows), :].astype(BF16)

    top = mine_is_top()
    for at_top in (0, 1):
        mine_here = top if at_top else jnp.logical_not(top)
        offset = at_top * (NODE - 1) * NODE
        a = at_top * (sectors - 1)
        for x in range(planes):
            gather(x, [n * group + offset for n in range(NVAR * NODE)], NODE)
            for j in range(tiles):
                columns = slice(x * block + j * lanes, x * block + (j + 1) * lanes)
                value = picked(j * sectors + a)

                @pl.when(mine_here)
                def _():
                    mine_ref[:, columns] = value

                @pl.when(jnp.logical_not(mine_here))
                def _():
                    swap_ref[:faces, columns] = value

    def plane_face(at_top, put):
        x = at_top * (planes - 1)
        first = at_top * ((NODE - 1) * group)
        gather(x, [v * NODE * group + first for v in range(NVAR)], group)
        for k in range(rows):
            j, a = divmod(k, sectors)
            first_lane = (a * tiles + j) * lanes
            put(slice(first_lane, first_lane + lanes), picked(k))

    def put_swap(columns, value):
        swap_ref[faces:, columns] = value

    def put_second(columns, value):
        second_ref[:, columns] = value

    plane_face(1 - core, put_swap)
    if second_ref.shape[0] == faces:
        plane_face(core, put_second)
    else:
        second_ref[...] = jnp.zeros(second_ref.shape, BF16)
    for copy in copies[ready:]:
        copy.wait()


def near_kernel(delayed_ref, near_ref, own_ref):
    own_ref[...] = project(delayed_ref[...], near_ref[...])


def join_kernel(own_ref, received_ref, mine_ref, swapped_ref, low_ref, pay_ref):
    faces = mine_ref.shape[0]
    low_ref[...] = (own_ref[...] + received_ref[...]).astype(BF16)
    pay_ref[:faces, :] = mine_ref[...]
    pay_ref[faces:, :] = swapped_ref[:faces, :]


def prepare_kernel(
    sectors,
    state_ref,
    volume_ref,
    lift_ref,
    weights_ref,
    samples_ref,
    host_ref,
    profile_ref,
    flat_ref,
    op_ref,
    edge_ref,
    v_ref,
    hot_ref,
    row_ref,
    spread_ref,
    plane_ref,
):
    comps, planes, rows, lanes = state_ref.shape
    tiles = rows // sectors
    width = sectors * tiles * lanes
    group = NODE * NODE
    faces = NVAR * group
    for x in range(planes):
        plane_ref[x] = state_ref[:, x].astype(F32).reshape(comps * rows, lanes)
        for k in range(rows):
            j, a = divmod(k, sectors)
            first = x * width + (a * tiles + j) * lanes
            flat_ref[:, first : first + lanes] = plane_ref[
                x, pl.ds(k, comps, stride=rows), :
            ].astype(BF16)
    op_ref[:, :comps] = volume_ref[...]
    op_ref[:, comps : comps + 2 * faces] = lift_ref[:, : 2 * faces]
    face = lax.broadcasted_iota(jnp.int32, (2 * faces, comps), 0)
    comp = lax.broadcasted_iota(jnp.int32, (2 * faces, comps), 1)
    upper = (face < faces).astype(jnp.int32) * (NODE - 1)
    row = jnp.where(face < faces, face, face - faces)
    sector_at = quotient(row, NODE) * group + remainder(row, NODE) + upper * NODE
    radial_at = row * NODE + upper
    first = comps + 2 * faces
    for at, start in ((sector_at, 2 * faces), (radial_at, 4 * faces)):
        place = (comp == at).astype(F32).astype(BF16)
        op_ref[:, first : first + comps] = jnp.dot(
            lift_ref[:, start : start + 2 * faces], place, preferred_element_type=F32
        ).astype(BF16)
        first += comps
    edge_ref[:, :faces] = lift_ref[:, 2 * faces : 3 * faces]
    edge_ref[:, LANES : LANES + faces] = lift_ref[:, 3 * faces : 4 * faces]

    blocks, window, _ = weights_ref.shape
    samples = jnp.concatenate([samples_ref[...]] * blocks, axis=1)
    owner = lax.broadcasted_iota(jnp.int32, (blocks, blocks * window), 0)
    entry = lax.broadcasted_iota(jnp.int32, (blocks, blocks * window), 1)
    chosen = jnp.where(owner == quotient(entry, window), samples, 0.0)
    stacked = weights_ref[...].reshape(blocks * window, window)
    v_ref[...] = sum(
        jnp.dot(part, stacked, preferred_element_type=F32) for part in split(chosen)
    )
    points = hot_ref.shape[1]
    within = lax.broadcasted_iota(jnp.int32, (lanes, points), 0)
    host = host_ref[...]
    hot_ref[...] = (within == remainder(host, lanes)).astype(F32).astype(BF16)
    row_ref[...] = (
        quotient(host, rows * lanes) * rows
        + remainder(quotient(host, lanes), tiles) * sectors
        + remainder(quotient(host, lanes * tiles), sectors)
    )

    line = lax.broadcasted_iota(jnp.int32, (comps, comps), 0)
    cross = lax.broadcasted_iota(jnp.int32, (comps, comps), 1)
    diagonal = jnp.where(line == cross, profile_ref[...].reshape(1, comps), 0.0)
    ones = jnp.ones((comps, lanes), BF16)
    high, low = split(diagonal)
    lowest = (diagonal - high.astype(F32) - low.astype(F32)).astype(BF16)
    column = sum(
        jnp.dot(part, ones, preferred_element_type=F32) for part in (high, low, lowest)
    )
    for k in range(rows):
        spread_ref[pl.ds(k, comps, stride=rows), :] = column


def planes_kernel(
    first_plane,
    planes,
    sectors,
    flat_ref,
    op_ref,
    swapped_ref,
    second_ref,
    *refs,
):
    out_refs = refs[:-1]
    stack_ref = refs[-1]
    comps = flat_ref.shape[0]
    width = flat_ref.shape[1] // planes
    group = NODE * NODE
    faces = NVAR * group
    block = width // sectors
    tiles = block // LANES
    rows = sectors * tiles
    comp = lax.broadcasted_iota(jnp.int32, (comps, block), 0)
    lane = lax.broadcasted_iota(jnp.int32, (comps, block), 1)
    q = remainder(quotient(comp, NODE), NODE)
    w = remainder(comp, NODE)
    q_top = (q == NODE - 1).astype(F32).astype(BF16)
    q_low = (q == 0).astype(F32).astype(BF16)
    w_top = ((w == NODE - 1) & (lane > 0)).astype(F32).astype(BF16)
    w_low = ((w == 0) & (lane < block - 1)).astype(F32).astype(BF16)
    odd = core_of() == 1

    def second(v):
        if second_ref.shape[0] == faces:
            return second_ref[v * group : (v + 1) * group, :]
        return jnp.zeros((group, width), BF16)

    def first(v):
        return swapped_ref[faces + v * group : faces + (v + 1) * group, :]

    for n, out_ref in enumerate(out_refs):
        x = first_plane + n
        here = x * width
        own = flat_ref[:, here : here + width]
        stack_ref[n, :comps, :] = own
        for v in range(NVAR):
            low_row = v * NODE * group
            top_row = low_row + (NODE - 1) * group
            at = comps + v * group
            if x > 0:
                value = flat_ref[top_row : top_row + group, here - width : here]
            else:
                value = jnp.where(odd, first(v), second(v))
            stack_ref[n, at : at + group, :] = value
            at += faces
            if x < planes - 1:
                value = flat_ref[low_row : low_row + group, here + width : here + 2 * width]
            else:
                value = jnp.where(odd, second(v), first(v))
            stack_ref[n, at : at + group, :] = value
        mix = comps + 2 * faces
        for a in range(sectors):
            at = a * block
            columns = slice(at, at + block)
            part = flat_ref[:, here + at : here + at + block]
            sector = None
            if a > 0:
                sector = q_top * flat_ref[:, here + at - block : here + at]
            if a < sectors - 1:
                right = q_low * flat_ref[:, here + at + block : here + at + 2 * block]
                sector = right if sector is None else sector + right
            if sector is None:
                sector = jnp.zeros((comps, block), BF16)
            stack_ref[n, mix : mix + comps, columns] = sector
            stack_ref[n, mix + comps :, columns] = w_top * pltpu.roll(
                part, 1, 1
            ) + w_low * pltpu.roll(part, block - 1, 1)
        result = jnp.dot(op_ref[...], stack_ref[n], preferred_element_type=F32)
        for k in range(rows):
            j, a = divmod(k, sectors)
            at = (a * tiles + j) * LANES
            out_ref[pl.ds(k, comps, stride=rows), :] = result[:, at : at + LANES] + own[
                :, at : at + LANES
            ].astype(F32)


def strength_part(v_ref, sens, radiation):
    blocks = v_ref.shape[0]
    points = radiation.shape[1]
    v_high, v_low = split(v_ref[...])
    s_high, s_low = split(sens)
    combined = jnp.dot(
        jnp.concatenate([v_high, v_low, v_high], axis=1),
        jnp.concatenate([s_high, s_high, s_low], axis=0),
        preferred_element_type=F32,
    )
    both = jnp.concatenate(split(combined), axis=0)
    product = jnp.dot(both, radiation, preferred_element_type=F32)
    product = product[:blocks] + product[blocks:]
    block = lax.broadcasted_iota(jnp.int32, (blocks, points), 0)
    point = lax.broadcasted_iota(jnp.int32, (blocks, points), 1)
    chosen = block == quotient(point, points // blocks)
    return jnp.sum(jnp.where(chosen, product, 0.0), axis=0, keepdims=True)


def sensitivity(sums, half, taper_ref, weights_ref, target_ref):
    width = sums.shape[1]
    columns = pl.ds(pl.multiple_of(half * width, width), width)
    return weights_ref[:, columns] * taper_ref[...] * (sums - target_ref[:, columns])


def own_kernel(sums_ref, taper_ref, weights_ref, target_ref, v_ref, radiation_ref, part_ref, sens_ref):
    sens = sensitivity(sums_ref[...], core_of(), taper_ref, weights_ref, target_ref)
    sens_ref[...] = sens
    part_ref[...] = strength_part(v_ref, sens, radiation_ref[...])


def final_kernel(
    sectors,
    chunks,
    other_ref,
    own_sens_ref,
    taper_ref,
    weights_ref,
    target_ref,
    v_ref,
    far_ref,
    part_ref,
    row_ref,
    hot_ref,
    spread_ref,
    edge_ref,
    crossed_ref,
    back_ref,
    *rest,
):
    planes = len(rest) - 5
    base_refs = rest[:planes]
    sens_ref, out_hbm, all_ref, buffer_ref, sems = rest[planes:]
    comps, _, rows, lanes = out_hbm.shape
    tiles = rows // sectors
    block = tiles * lanes
    other_core = 1 - core_of()
    half = far_ref.shape[0]
    start = pl.multiple_of(other_core * half, half)
    sens = sensitivity(other_ref[...], other_core, taper_ref, weights_ref, target_ref)
    strength = part_ref[...] + strength_part(v_ref, sens, far_ref[...])
    at = lax.broadcasted_iota(jnp.int32, (planes * rows, strength.shape[1]), 0)
    placed = jnp.where(at == row_ref[...], strength, 0.0)
    gathered = lax.dot_general(
        jnp.concatenate(split(placed), axis=0),
        hot_ref[...],
        (((1,), (1,)), ((), ())),
        preferred_element_type=F32,
    )
    source = gathered[: planes * rows] + gathered[planes * rows :]
    faces = crossed_ref.shape[0] // 2
    top = mine_is_top()
    crossed = crossed_ref[:faces, :]
    back = back_ref[faces:, :]
    halos = (jnp.where(top, back, crossed), jnp.where(top, crossed, back))
    chunk = comps // chunks
    copies = []
    for n in range(chunks):
        part = slice(n * chunk, (n + 1) * chunk)
        lines = slice(n * chunk * rows, (n + 1) * chunk * rows)
        spread = spread_ref[lines, :].reshape(chunk, rows, lanes)
        for x in range(planes):
            buffer_ref[x, part] = (
                base_refs[x][lines, :].reshape(chunk, rows, lanes)
                + spread * source[x * rows : (x + 1) * rows][None]
            )
        for side, a in ((0, 0), (1, sectors - 1)):
            term = jnp.dot(
                edge_ref[part, side * LANES : side * LANES + faces],
                halos[side],
                preferred_element_type=F32,
            )
            for x in range(planes):
                flat_ref = buffer_ref.at[x].reshape(comps * rows, lanes)
                for j in range(tiles):
                    place = pl.ds(n * chunk * rows + j * sectors + a, chunk, stride=rows)
                    column = x * block + j * lanes
                    flat_ref[place, :] = flat_ref[place, :] + term[:, column : column + lanes]
        for x in range(planes):
            copy = pltpu.make_async_copy(
                buffer_ref.at[x, part], out_hbm.at[part, x], sems.at[n * planes + x]
            )
            copy.start()
            copies.append(copy)

    all_ref[:, pl.ds(start, half)] = sens
    all_ref[:, pl.ds(pl.multiple_of((1 - other_core) * half, half), half)] = own_sens_ref[...]
    count = sens_ref.shape[1]
    first = lax.axis_index("azim") * count
    aligned = pl.multiple_of((first // LANES) * LANES, LANES)
    window = all_ref[:, pl.ds(aligned, LANES)]
    turned = pltpu.roll(window, lax.rem(LANES - (first - aligned), LANES), 1)
    sens_ref[...] = turned[:, :count]
    for copy in copies:
        copy.wait()


def exchange(value, mask, devices):
    return lax.ppermute(value, MESH_AXES, [(i, i ^ mask) for i in range(devices)])


def body(
    surface_signal,
    retarded_weights,
    radiation_weights,
    target_signal,
    observer_weights,
    sample_weights,
    host_element,
    source_profile,
    adjoint_state,
    volume_operator,
    lift_operator,
):
    streams = lax.axis_size("stream")
    around = lax.axis_size("azim")
    devices = streams * around
    window, points = surface_signal.shape
    observers = radiation_weights.shape[0]
    half = observers // 2
    blocks = retarded_weights.shape[0]
    comps, planes, sectors, radial = adjoint_state.shape
    tiles = radial // LANES
    rows = sectors * tiles
    width = sectors * radial
    faces = NVAR * NODE * NODE
    barrier = lax.optimization_barrier
    depth = 3 * comps + 2 * faces

    view = (
        adjoint_state.reshape(comps, planes, sectors, tiles, LANES)
        .transpose(0, 1, 3, 2, 4)
        .reshape(comps, planes, rows, LANES)
    )
    small = [
        target_signal,
        observer_weights.reshape(1, observers),
        sample_weights.reshape(1, window),
        host_element.reshape(1, points),
        source_profile,
        volume_operator,
        lift_operator,
    ]
    large = [surface_signal, retarded_weights, radiation_weights, view]
    send, delayed, far, near, state, retarded, swap, mine, second, *small = call(
        lambda *refs: start_kernel(sectors, len(small), *refs),
        [HBM] * len(large + small),
        [
            vmem((window, half), F32),
            vmem((window, points), BF16),
            vmem((half, points), BF16),
            vmem((half, points), BF16),
            vmem(view.shape, BF16),
            vmem(retarded_weights.shape, BF16),
            vmem((2 * faces, width), BF16),
            vmem((faces, planes * radial), BF16),
            vmem((faces if streams > 2 else 16, width), BF16),
        ]
        + [vmem(x.shape, x.dtype) for x in small],
        [in_hbm(x) for x in large + small],
        [
            pltpu.VMEM((window, points), BF16),
            pltpu.VMEM((faces * rows, LANES), F32),
            pltpu.SemaphoreType.DMA((5 + NODE + len(small),)),
        ],
    )
    target, weights, samples, host, profile, volume, lift = small
    received = exchange(send, around, devices)
    swapped = exchange(swap, around, devices)
    own = call(near_kernel, [VMEM] * 2, [vmem((window, half), F32)], [delayed, near])[0]
    low, pay = call(
        join_kernel,
        [VMEM] * 4,
        [vmem((window, half), BF16), vmem((2 * faces, planes * radial), BF16)],
        [own, received, mine, swapped],
    )
    low, pay, state = barrier((low, pay, state))

    bits = [1 << n for n in range((around - 1).bit_length())]
    bits += [around << n for n in range(1, (streams - 1).bit_length())]
    stages = []
    for first in range(0, len(bits), 2):
        pair = bits[first : first + 2]
        stages.append(pair + ([pair[0] | pair[1]] if len(pair) == 2 else []))

    inner = [(i, i ^ 1) for i in range(around)]
    outer = [(i, (i + 1 if i % 2 else i - 1) % around) for i in range(around)]
    pairs = []
    for s in range(streams):
        pairs += [(s * around + i, s * around + j) for i, j in (outer if s % 2 else inner)]
    crossed = lax.ppermute(pay, MESH_AXES, pairs)
    parts = [exchange(low, mask, devices) for mask in stages[0]]
    if streams > 2:
        links = [(s, s + 1) for s in range(1, streams - 1, 2)]
        second = lax.ppermute(second, "stream", links + [(b, a) for a, b in links])
    flat, operator, edge, v, hot, row, spread = call(
        lambda *refs: prepare_kernel(sectors, *refs),
        [VMEM] * 7,
        [
            vmem((comps, planes * width), BF16),
            vmem((comps, depth), BF16),
            vmem((comps, 2 * LANES), BF16),
            vmem((blocks, window), F32),
            vmem((LANES, points), BF16),
            vmem((1, points), jnp.int32),
            vmem((comps * rows, LANES), F32),
        ],
        [state, volume, lift, retarded, samples, host, profile],
        [pltpu.VMEM((planes, comps * rows, LANES), F32)],
        nbytes=12 * 2**20,
    )

    def combine(low, parts):
        total = low.astype(F32) + parts[0].astype(F32)
        if len(parts) == 3:
            total = total + (parts[1].astype(F32) + parts[2].astype(F32))
        return total

    parts, flat = barrier((parts, flat))
    sums = combine(low, parts)
    low = sums.astype(BF16)

    def run_planes(first, count):
        return call(
            lambda *refs: planes_kernel(first, planes, sectors, *refs),
            [VMEM] * 4,
            [vmem((comps * rows, LANES), F32)] * count,
            [flat, operator, swapped, second],
            [pltpu.VMEM((count, depth, width), BF16)],
            flops=2 * comps * depth * width * count,
            nbytes=count * 4 * 2**20,
        )

    bases = []
    for masks in stages[1:]:
        parts = [exchange(low, mask, devices) for mask in masks]
        if not bases:
            bases = list(run_planes(0, planes // 2)) + list(run_planes(planes // 2, planes // 2))
            parts, bases = barrier((parts, bases))
        sums = combine(low, parts)
        low = sums.astype(BF16)

    remote = exchange(sums, around, devices)
    crossed, bases = barrier((crossed, bases))
    back = exchange(crossed, around, devices)
    taper = np.arange(window, dtype=np.float64)
    taper = (0.5 - 0.5 * np.cos(2.0 * np.pi * (taper + 0.5) / window)).astype(np.float32)
    taper = jnp.asarray(taper).reshape(window, 1)
    part, own_sens = call(
        own_kernel,
        [VMEM] * 6,
        [vmem((1, points), F32), vmem((window, half), F32)],
        [sums, taper, weights, target, v, near],
        flops=2 * 2 * blocks * half * points,
        nbytes=half * points * 2,
    )
    chunks = 5
    sens, updated = call(
        lambda *refs: final_kernel(sectors, chunks, *refs),
        [VMEM] * (14 + planes),
        [
            jax.ShapeDtypeStruct((window, observers // around), F32),
            jax.ShapeDtypeStruct(view.shape, F32),
        ],
        [remote, own_sens, taper, weights, target, v, far, part, row, hot, spread]
        + [edge, crossed, back]
        + list(bases),
        [
            pltpu.VMEM((window, observers), F32),
            pltpu.VMEM((planes, comps, rows, LANES), F32),
            pltpu.SemaphoreType.DMA((chunks * planes,)),
        ],
        nbytes=12 * 2**20,
        out_specs=[VMEM, HBM],
    )
    updated = (
        updated.reshape(comps, planes, tiles, sectors, LANES)
        .transpose(0, 1, 3, 2, 4)
        .reshape(adjoint_state.shape)
    )
    return sens, updated


def solution(mesh):
    return jax.shard_map(
        body,
        mesh=mesh,
        in_specs=(
            P(None, ("stream", "azim")),
            P(("stream", "azim"), None, None),
            P(None, ("stream", "azim")),
            P(),
            P(),
            P(),
            P(("stream", "azim")),
            P(),
            P(None, "stream", "azim", None),
            P(),
            P(),
        ),
        out_specs=(P(None, "azim"), P(None, "stream", "azim", None)),
        check_vma=False,
    )
```

```python
import jax
import jax.numpy as jnp
import numpy as np
from jax import lax
from jax.experimental import pallas as pl
from jax.experimental.pallas import tpu as pltpu
from jax.sharding import PartitionSpec as P

NVAR = 5
NODE = 4
LANES = 128
F32 = jnp.float32
BF16 = jnp.bfloat16
MESH_AXES = ("stream", "azim")
VMEM = pl.BlockSpec(memory_space=pltpu.VMEM)
HBM = pl.BlockSpec(memory_space=pl.ANY)


def vmem(shape, dtype):
    return pltpu.VMEM(shape, dtype)


def in_hbm(x):
    return pltpu.with_memory_space_constraint(x, pltpu.HBM)


def call(kernel, ins, outs, args, scratch=(), mib=16, flops=0, nbytes=0, out_specs=None, aliases=None):
    return pl.pallas_call(
        kernel,
        in_specs=ins,
        out_specs=out_specs or [VMEM] * len(outs),
        out_shape=outs,
        scratch_shapes=list(scratch),
        input_output_aliases=aliases or {},
        compiler_params=pltpu.CompilerParams(vmem_limit_bytes=mib * 2**20),
        cost_estimate=pl.CostEstimate(flops=flops, bytes_accessed=nbytes, transcendentals=0),
    )(*args)


def core_of():
    return lax.rem(lax.axis_index("stream"), 2)


def mine_is_top():
    return core_of() == lax.rem(lax.axis_index("azim"), 2)


def quotient(x, n):
    return x >> (n.bit_length() - 1) if n & (n - 1) == 0 else x // n


def remainder(x, n):
    return x & (n - 1) if n & (n - 1) == 0 else x % n


def split(x):
    high = x.astype(BF16)
    return high, (x - high.astype(F32)).astype(BF16)


def project(delayed, radiation):
    return lax.dot_general(
        delayed, radiation, (((1,), (1,)), ((), ())), preferred_element_type=F32
    )


def started(pairs, sems):
    copies = [
        pltpu.make_async_copy(source, target, sems.at[n])
        for n, (source, target) in enumerate(pairs)
    ]
    for copy in copies:
        copy.start()
    return copies


def start_kernel(sectors, signal_hbm, weights_hbm, radiation_hbm, state_hbm, *refs):
    send_ref, delayed_ref, far_ref, near_ref, state_ref, weights_ref, *refs = refs
    swap_ref, mine_ref, second_ref, signal_ref, rows_ref, sems = refs
    comps, planes, rows, lanes = state_ref.shape
    tiles = rows // sectors
    block = tiles * lanes
    group = NODE * NODE
    faces = NVAR * group
    half = far_ref.shape[0]
    chunk = half // 2
    core = core_of()
    far = pl.multiple_of((1 - core) * half, half)
    near = pl.multiple_of(core * half, half)
    pairs = [(signal_hbm, signal_ref), (weights_hbm, weights_ref)]
    for first in (0, chunk):
        pairs.append(
            (radiation_hbm.at[pl.ds(far + first, chunk)], far_ref.at[pl.ds(first, chunk)])
        )
    quarter = comps // NODE
    for first in range(0, comps, quarter):
        part = pl.ds(first, quarter)
        pairs.append((state_hbm.at[part], state_ref.at[part]))
    ready = len(pairs)
    pairs.append((radiation_hbm.at[pl.ds(near, half)], near_ref))
    copies = started(pairs, sems)
    copies[0].wait()
    copies[1].wait()
    blocks = weights_ref.shape[0]
    width = signal_ref.shape[1] // blocks
    for b in range(blocks):
        columns = slice(b * width, (b + 1) * width)
        delayed_ref[:, columns] = lax.dot_general(
            weights_ref[b],
            signal_ref[:, columns],
            (((0,), (0,)), ((), ())),
            preferred_element_type=F32,
        ).astype(BF16)
    copies[2].wait()
    send_ref[:, :chunk] = project(delayed_ref[...], far_ref[:chunk, :])
    copies[3].wait()
    send_ref[:, chunk:] = project(delayed_ref[...], far_ref[chunk:, :])
    for copy in copies[4:ready]:
        copy.wait()

    def gather(x, offsets, count):
        for n, offset in enumerate(offsets):
            rows_ref[n * count * rows : (n + 1) * count * rows, :] = (
                state_ref[pl.ds(offset, count), x].astype(F32).reshape(count * rows, lanes)
            )

    def picked(k):
        return rows_ref[pl.ds(k, faces, stride=rows), :].astype(BF16)

    top = mine_is_top()
    for at_top in (0, 1):
        mine_here = top if at_top else jnp.logical_not(top)
        offset = at_top * (NODE - 1) * NODE
        a = at_top * (sectors - 1)
        for x in range(planes):
            gather(x, [n * group + offset for n in range(NVAR * NODE)], NODE)
            for j in range(tiles):
                columns = slice(x * block + j * lanes, x * block + (j + 1) * lanes)
                value = picked(j * sectors + a)

                @pl.when(mine_here)
                def _():
                    mine_ref[:, columns] = value

                @pl.when(jnp.logical_not(mine_here))
                def _():
                    swap_ref[:faces, columns] = value

    def plane_face(at_top, put):
        x = at_top * (planes - 1)
        first = at_top * ((NODE - 1) * group)
        gather(x, [v * NODE * group + first for v in range(NVAR)], group)
        for k in range(rows):
            j, a = divmod(k, sectors)
            first_lane = (a * tiles + j) * lanes
            put(slice(first_lane, first_lane + lanes), picked(k))

    def put_swap(columns, value):
        swap_ref[faces:, columns] = value

    def put_second(columns, value):
        second_ref[:, columns] = value

    plane_face(1 - core, put_swap)
    if second_ref.shape[0] == faces:
        plane_face(core, put_second)
    else:
        second_ref[...] = jnp.zeros(second_ref.shape, BF16)
    for copy in copies[ready:]:
        copy.wait()


def near_kernel(delayed_ref, near_ref, own_ref):
    own_ref[...] = project(delayed_ref[...], near_ref[...])


def join_kernel(own_ref, received_ref, mine_ref, swapped_ref, low_ref, pay_ref):
    faces = mine_ref.shape[0]
    low_ref[...] = (own_ref[...] + received_ref[...]).astype(BF16)
    pay_ref[:faces, :] = mine_ref[...]
    pay_ref[faces:, :] = swapped_ref[:faces, :]


def prepare_kernel(
    sectors,
    state_ref,
    weights_ref,
    target_hbm,
    observer_hbm,
    samples_hbm,
    host_hbm,
    profile_hbm,
    volume_hbm,
    lift_hbm,
    flat_ref,
    op_ref,
    edge_ref,
    v_ref,
    hot_ref,
    row_ref,
    spread_ref,
    target_ref,
    observer_ref,
    plane_ref,
    samples_ref,
    host_ref,
    profile_ref,
    volume_ref,
    lift_ref,
    sems,
):
    copies = started(
        (
            (volume_hbm, volume_ref),
            (lift_hbm, lift_ref),
            (samples_hbm, samples_ref),
            (host_hbm, host_ref),
            (profile_hbm, profile_ref),
            (observer_hbm, observer_ref),
            (target_hbm, target_ref),
        ),
        sems,
    )
    comps, planes, rows, lanes = state_ref.shape
    tiles = rows // sectors
    width = sectors * tiles * lanes
    group = NODE * NODE
    faces = NVAR * group
    for x in range(planes):
        plane_ref[x] = state_ref[:, x].astype(F32).reshape(comps * rows, lanes)
        for k in range(rows):
            j, a = divmod(k, sectors)
            first = x * width + (a * tiles + j) * lanes
            flat_ref[:, first : first + lanes] = plane_ref[
                x, pl.ds(k, comps, stride=rows), :
            ].astype(BF16)
    for copy in copies:
        copy.wait()
    op_ref[:, :comps] = volume_ref[...]
    op_ref[:, comps : comps + 2 * faces] = lift_ref[:, : 2 * faces]
    face = lax.broadcasted_iota(jnp.int32, (2 * faces, comps), 0)
    comp = lax.broadcasted_iota(jnp.int32, (2 * faces, comps), 1)
    upper = (face < faces).astype(jnp.int32) * (NODE - 1)
    row = jnp.where(face < faces, face, face - faces)
    sector_at = quotient(row, NODE) * group + remainder(row, NODE) + upper * NODE
    radial_at = row * NODE + upper
    first = comps + 2 * faces
    for at, start in ((sector_at, 2 * faces), (radial_at, 4 * faces)):
        place = (comp == at).astype(F32).astype(BF16)
        op_ref[:, first : first + comps] = jnp.dot(
            lift_ref[:, start : start + 2 * faces], place, preferred_element_type=F32
        ).astype(BF16)
        first += comps
    edge_ref[:, :faces] = lift_ref[:, 2 * faces : 3 * faces]
    edge_ref[:, LANES : LANES + faces] = lift_ref[:, 3 * faces : 4 * faces]

    blocks, window, _ = weights_ref.shape
    samples = jnp.concatenate([samples_ref[...]] * blocks, axis=1)
    owner = lax.broadcasted_iota(jnp.int32, (blocks, blocks * window), 0)
    entry = lax.broadcasted_iota(jnp.int32, (blocks, blocks * window), 1)
    chosen = jnp.where(owner == quotient(entry, window), samples, 0.0)
    stacked = weights_ref[...].reshape(blocks * window, window)
    v_ref[...] = sum(
        jnp.dot(part, stacked, preferred_element_type=F32) for part in split(chosen)
    )
    points = hot_ref.shape[1]
    within = lax.broadcasted_iota(jnp.int32, (lanes, points), 0)
    host = host_ref[...]
    hot_ref[...] = (within == remainder(host, lanes)).astype(F32).astype(BF16)
    row_ref[...] = (
        quotient(host, rows * lanes) * rows
        + remainder(quotient(host, lanes), tiles) * sectors
        + remainder(quotient(host, lanes * tiles), sectors)
    )

    line = lax.broadcasted_iota(jnp.int32, (comps, comps), 0)
    cross = lax.broadcasted_iota(jnp.int32, (comps, comps), 1)
    diagonal = jnp.where(line == cross, profile_ref[...].reshape(1, comps), 0.0)
    ones = jnp.ones((comps, lanes), BF16)
    high, low = split(diagonal)
    lowest = (diagonal - high.astype(F32) - low.astype(F32)).astype(BF16)
    column = sum(
        jnp.dot(part, ones, preferred_element_type=F32) for part in (high, low, lowest)
    )
    for k in range(rows):
        spread_ref[pl.ds(k, comps, stride=rows), :] = column


def planes_kernel(
    first_plane,
    planes,
    sectors,
    flat_ref,
    op_ref,
    swapped_ref,
    second_ref,
    *refs,
):
    out_refs = refs[:-1]
    stack_ref = refs[-1]
    comps = flat_ref.shape[0]
    width = flat_ref.shape[1] // planes
    group = NODE * NODE
    faces = NVAR * group
    block = width // sectors
    tiles = block // LANES
    rows = sectors * tiles
    comp = lax.broadcasted_iota(jnp.int32, (comps, block), 0)
    lane = lax.broadcasted_iota(jnp.int32, (comps, block), 1)
    q = remainder(quotient(comp, NODE), NODE)
    w = remainder(comp, NODE)
    q_top = (q == NODE - 1).astype(F32).astype(BF16)
    q_low = (q == 0).astype(F32).astype(BF16)
    w_top = ((w == NODE - 1) & (lane > 0)).astype(F32).astype(BF16)
    w_low = ((w == 0) & (lane < block - 1)).astype(F32).astype(BF16)
    odd = core_of() == 1

    def second(v):
        if second_ref.shape[0] == faces:
            return second_ref[v * group : (v + 1) * group, :]
        return jnp.zeros((group, width), BF16)

    def first(v):
        return swapped_ref[faces + v * group : faces + (v + 1) * group, :]

    for n, out_ref in enumerate(out_refs):
        x = first_plane + n
        here = x * width
        own = flat_ref[:, here : here + width]
        stack_ref[n, :comps, :] = own
        for v in range(NVAR):
            low_row = v * NODE * group
            top_row = low_row + (NODE - 1) * group
            at = comps + v * group
            if x > 0:
                value = flat_ref[top_row : top_row + group, here - width : here]
            else:
                value = jnp.where(odd, first(v), second(v))
            stack_ref[n, at : at + group, :] = value
            at += faces
            if x < planes - 1:
                value = flat_ref[low_row : low_row + group, here + width : here + 2 * width]
            else:
                value = jnp.where(odd, second(v), first(v))
            stack_ref[n, at : at + group, :] = value
        mix = comps + 2 * faces
        for a in range(sectors):
            at = a * block
            columns = slice(at, at + block)
            part = flat_ref[:, here + at : here + at + block]
            sector = None
            if a > 0:
                sector = q_top * flat_ref[:, here + at - block : here + at]
            if a < sectors - 1:
                right = q_low * flat_ref[:, here + at + block : here + at + 2 * block]
                sector = right if sector is None else sector + right
            if sector is None:
                sector = jnp.zeros((comps, block), BF16)
            stack_ref[n, mix : mix + comps, columns] = sector
            stack_ref[n, mix + comps :, columns] = w_top * pltpu.roll(
                part, 1, 1
            ) + w_low * pltpu.roll(part, block - 1, 1)
        result = jnp.dot(op_ref[...], stack_ref[n], preferred_element_type=F32)
        for k in range(rows):
            j, a = divmod(k, sectors)
            at = (a * tiles + j) * LANES
            out_ref[pl.ds(k, comps, stride=rows), :] = result[:, at : at + LANES] + own[
                :, at : at + LANES
            ].astype(F32)


def strength_part(v_ref, sens, radiation):
    blocks = v_ref.shape[0]
    points = radiation.shape[1]
    v_high, v_low = split(v_ref[...])
    s_high, s_low = split(sens)
    combined = jnp.dot(
        jnp.concatenate([v_high, v_low, v_high], axis=1),
        jnp.concatenate([s_high, s_high, s_low], axis=0),
        preferred_element_type=F32,
    )
    both = jnp.concatenate(split(combined), axis=0)
    product = jnp.dot(both, radiation, preferred_element_type=F32)
    product = product[:blocks] + product[blocks:]
    block = lax.broadcasted_iota(jnp.int32, (blocks, points), 0)
    point = lax.broadcasted_iota(jnp.int32, (blocks, points), 1)
    chosen = block == quotient(point, points // blocks)
    return jnp.sum(jnp.where(chosen, product, 0.0), axis=0, keepdims=True)


def sensitivity(sums, half, taper_ref, weights_ref, target_ref):
    width = sums.shape[1]
    columns = pl.ds(pl.multiple_of(half * width, width), width)
    return weights_ref[:, columns] * taper_ref[...] * (sums - target_ref[:, columns])


def own_kernel(sums_ref, taper_ref, weights_ref, target_ref, v_ref, radiation_ref, part_ref, sens_ref):
    sens = sensitivity(sums_ref[...], core_of(), taper_ref, weights_ref, target_ref)
    sens_ref[...] = sens
    part_ref[...] = strength_part(v_ref, sens, radiation_ref[...])


def final_kernel(
    sectors,
    chunks,
    other_ref,
    own_sens_ref,
    taper_ref,
    weights_ref,
    target_ref,
    v_ref,
    far_ref,
    part_ref,
    row_ref,
    hot_ref,
    spread_ref,
    edge_ref,
    crossed_ref,
    back_ref,
    *rest,
):
    planes = len(rest) - 5
    base_refs = rest[:planes]
    sens_ref, out_hbm, all_ref, buffer_ref, sems = rest[planes:]
    comps, _, rows, lanes = out_hbm.shape
    tiles = rows // sectors
    block = tiles * lanes
    other_core = 1 - core_of()
    half = far_ref.shape[0]
    start = pl.multiple_of(other_core * half, half)
    sens = sensitivity(other_ref[...], other_core, taper_ref, weights_ref, target_ref)
    strength = part_ref[...] + strength_part(v_ref, sens, far_ref[...])
    at = lax.broadcasted_iota(jnp.int32, (planes * rows, strength.shape[1]), 0)
    placed = jnp.where(at == row_ref[...], strength, 0.0)
    gathered = lax.dot_general(
        jnp.concatenate(split(placed), axis=0),
        hot_ref[...],
        (((1,), (1,)), ((), ())),
        preferred_element_type=F32,
    )
    source = gathered[: planes * rows] + gathered[planes * rows :]
    faces = crossed_ref.shape[0] // 2
    top = mine_is_top()
    crossed = crossed_ref[:faces, :]
    back = back_ref[faces:, :]
    halos = (jnp.where(top, back, crossed), jnp.where(top, crossed, back))
    chunk = comps // chunks
    def output_copy(n, x):
        part = pl.ds(pl.multiple_of(n * chunk, chunk), chunk)
        return pltpu.make_async_copy(
            buffer_ref.at[x, part], out_hbm.at[part, x], sems.at[n * planes + x]
        )

    def write(n, carry):
        part = pl.ds(pl.multiple_of(n * chunk, chunk), chunk)
        lines = pl.ds(pl.multiple_of(n * chunk * rows, chunk * rows), chunk * rows)
        spread = spread_ref[lines, :].reshape(chunk, rows, lanes)
        for x in range(planes):
            buffer_ref[x, part] = (
                base_refs[x][lines, :].reshape(chunk, rows, lanes)
                + spread * source[x * rows : (x + 1) * rows][None]
            )
        for side, a in ((0, 0), (1, sectors - 1)):
            term = jnp.dot(
                edge_ref[part, side * LANES : side * LANES + faces],
                halos[side],
                preferred_element_type=F32,
            )
            for x in range(planes):
                flat_ref = buffer_ref.at[x].reshape(comps * rows, lanes)
                for j in range(tiles):
                    place = pl.ds(n * chunk * rows + j * sectors + a, chunk, stride=rows)
                    column = x * block + j * lanes
                    flat_ref[place, :] = flat_ref[place, :] + term[:, column : column + lanes]
        for x in range(planes):
            output_copy(n, x).start()
        return carry

    lax.fori_loop(0, chunks, write, 0)

    all_ref[:, pl.ds(start, half)] = sens
    all_ref[:, pl.ds(pl.multiple_of((1 - other_core) * half, half), half)] = own_sens_ref[...]
    count = sens_ref.shape[1]
    first = lax.axis_index("azim") * count
    aligned = pl.multiple_of((first // LANES) * LANES, LANES)
    window = all_ref[:, pl.ds(aligned, LANES)]
    turned = pltpu.roll(window, lax.rem(LANES - (first - aligned), LANES), 1)
    sens_ref[...] = turned[:, :count]

    def finish(n, carry):
        for x in range(planes):
            output_copy(n, x).wait()
        return carry

    lax.fori_loop(0, chunks, finish, 0)


def exchange(value, mask, devices):
    return lax.ppermute(value, MESH_AXES, [(i, i ^ mask) for i in range(devices)])


def body(
    surface_signal,
    retarded_weights,
    radiation_weights,
    target_signal,
    observer_weights,
    sample_weights,
    host_element,
    source_profile,
    adjoint_state,
    volume_operator,
    lift_operator,
):
    streams = lax.axis_size("stream")
    around = lax.axis_size("azim")
    devices = streams * around
    window, points = surface_signal.shape
    observers = radiation_weights.shape[0]
    half = observers // 2
    blocks = retarded_weights.shape[0]
    comps, planes, sectors, radial = adjoint_state.shape
    tiles = radial // LANES
    rows = sectors * tiles
    width = sectors * radial
    faces = NVAR * NODE * NODE
    barrier = lax.optimization_barrier
    depth = 3 * comps + 2 * faces

    view = (
        adjoint_state.reshape(comps, planes, sectors, tiles, LANES)
        .transpose(0, 1, 3, 2, 4)
        .reshape(comps, planes, rows, LANES)
    )
    small = [
        target_signal,
        observer_weights.reshape(1, observers),
        sample_weights.reshape(1, window),
        host_element.reshape(1, points),
        source_profile,
        volume_operator,
        lift_operator,
    ]
    large = [surface_signal, retarded_weights, radiation_weights, view]
    send, delayed, far, near, state, retarded, swap, mine, second = call(
        lambda *refs: start_kernel(sectors, *refs),
        [HBM] * len(large),
        [
            vmem((window, half), F32),
            vmem((window, points), BF16),
            vmem((half, points), BF16),
            vmem((half, points), BF16),
            vmem(view.shape, BF16),
            vmem(retarded_weights.shape, BF16),
            vmem((2 * faces, width), BF16),
            vmem((faces, planes * radial), BF16),
            vmem((faces if streams > 2 else 16, width), BF16),
        ],
        [in_hbm(x) for x in large],
        [
            pltpu.VMEM((window, points), BF16),
            pltpu.VMEM((faces * rows, LANES), F32),
            pltpu.SemaphoreType.DMA((5 + NODE,)),
        ],
    )
    received = exchange(send, around, devices)
    swapped = exchange(swap, around, devices)
    own = call(near_kernel, [VMEM] * 2, [vmem((window, half), F32)], [delayed, near])[0]
    low, pay = call(
        join_kernel,
        [VMEM] * 4,
        [vmem((window, half), BF16), vmem((2 * faces, planes * radial), BF16)],
        [own, received, mine, swapped],
    )
    low, pay, state = barrier((low, pay, state))

    bits = [1 << n for n in range((around - 1).bit_length())]
    bits += [around << n for n in range(1, (streams - 1).bit_length())]
    stages = []
    for first in range(0, len(bits), 2):
        pair = bits[first : first + 2]
        stages.append(pair + ([pair[0] | pair[1]] if len(pair) == 2 else []))

    inner = [(i, i ^ 1) for i in range(around)]
    outer = [(i, (i + 1 if i % 2 else i - 1) % around) for i in range(around)]
    pairs = []
    for s in range(streams):
        pairs += [(s * around + i, s * around + j) for i, j in (outer if s % 2 else inner)]
    crossed = lax.ppermute(pay, MESH_AXES, pairs)
    parts = [exchange(low, mask, devices) for mask in stages[0]]
    if streams > 2:
        links = [(s, s + 1) for s in range(1, streams - 1, 2)]
        second = lax.ppermute(second, "stream", links + [(b, a) for a, b in links])
    flat, operator, edge, v, hot, row, spread, target, weights = call(
        lambda *refs: prepare_kernel(sectors, *refs),
        [VMEM] * 2 + [HBM] * len(small),
        [
            vmem((comps, planes * width), BF16),
            vmem((comps, depth), BF16),
            vmem((comps, 2 * LANES), BF16),
            vmem((blocks, window), F32),
            vmem((LANES, points), BF16),
            vmem((1, points), jnp.int32),
            vmem((comps * rows, LANES), F32),
            vmem(target_signal.shape, F32),
            vmem((1, observers), F32),
        ],
        [state, retarded] + [in_hbm(x) for x in small],
        [pltpu.VMEM((planes, comps * rows, LANES), F32)]
        + [pltpu.VMEM(x.shape, x.dtype) for x in small[2:]]
        + [pltpu.SemaphoreType.DMA((len(small),))],
        nbytes=12 * 2**20,
    )

    def combine(low, parts):
        total = low.astype(F32) + parts[0].astype(F32)
        if len(parts) == 3:
            total = total + (parts[1].astype(F32) + parts[2].astype(F32))
        return total

    parts, flat = barrier((parts, flat))
    sums = combine(low, parts)
    low = sums.astype(BF16)

    def run_planes(first, count):
        return call(
            lambda *refs: planes_kernel(first, planes, sectors, *refs),
            [VMEM] * 4,
            [vmem((comps * rows, LANES), F32)] * count,
            [flat, operator, swapped, second],
            [pltpu.VMEM((count, depth, width), BF16)],
            flops=2 * comps * depth * width * count,
            nbytes=count * 4 * 2**20,
        )

    bases = []
    for masks in stages[1:]:
        parts = [exchange(low, mask, devices) for mask in masks]
        if not bases:
            bases = list(run_planes(0, planes // 2)) + list(run_planes(planes // 2, planes // 2))
            parts, bases = barrier((parts, bases))
        sums = combine(low, parts)
        low = sums.astype(BF16)

    remote = exchange(sums, around, devices)
    crossed, bases = barrier((crossed, bases))
    back = exchange(crossed, around, devices)
    taper = np.arange(window, dtype=np.float64)
    taper = (0.5 - 0.5 * np.cos(2.0 * np.pi * (taper + 0.5) / window)).astype(np.float32)
    taper = jnp.asarray(taper).reshape(window, 1)
    part, own_sens = call(
        own_kernel,
        [VMEM] * 6,
        [vmem((1, points), F32), vmem((window, half), F32)],
        [sums, taper, weights, target, v, near],
        flops=2 * 2 * blocks * half * points,
        nbytes=half * points * 2,
    )
    chunks = 5
    sens, updated = call(
        lambda *refs: final_kernel(sectors, chunks, *refs),
        [VMEM] * (14 + planes),
        [
            jax.ShapeDtypeStruct((window, observers // around), F32),
            jax.ShapeDtypeStruct(view.shape, F32),
        ],
        [remote, own_sens, taper, weights, target, v, far, part, row, hot, spread]
        + [edge, crossed, back]
        + list(bases),
        [
            pltpu.VMEM((window, observers), F32),
            pltpu.VMEM((planes, comps, rows, LANES), F32),
            pltpu.SemaphoreType.DMA((chunks * planes,)),
        ],
        nbytes=12 * 2**20,
        out_specs=[VMEM, HBM],
    )
    updated = (
        updated.reshape(comps, planes, tiles, sectors, LANES)
        .transpose(0, 1, 3, 2, 4)
        .reshape(adjoint_state.shape)
    )
    return sens, updated


def solution(mesh):
    return jax.shard_map(
        body,
        mesh=mesh,
        in_specs=(
            P(None, ("stream", "azim")),
            P(("stream", "azim"), None, None),
            P(None, ("stream", "azim")),
            P(),
            P(),
            P(),
            P(("stream", "azim")),
            P(),
            P(None, "stream", "azim", None),
            P(),
            P(),
        ),
        out_specs=(P(None, "azim"), P(None, "stream", "azim", None)),
        check_vma=False,
    )
```

```python
import jax
import jax.numpy as jnp
import numpy as np
from jax import lax
from jax.experimental import pallas as pl
from jax.experimental.pallas import tpu as pltpu
from jax.sharding import PartitionSpec as P

NVAR = 5
NODE = 4
LANES = 128
F32 = jnp.float32
BF16 = jnp.bfloat16
MESH_AXES = ("stream", "azim")
VMEM = pl.BlockSpec(memory_space=pltpu.VMEM)
HBM = pl.BlockSpec(memory_space=pl.ANY)


def vmem(shape, dtype):
    return pltpu.VMEM(shape, dtype)


def in_hbm(x):
    return pltpu.with_memory_space_constraint(x, pltpu.HBM)


def call(kernel, ins, outs, args, scratch=(), mib=16, flops=0, nbytes=0, out_specs=None, aliases=None):
    return pl.pallas_call(
        kernel,
        in_specs=ins,
        out_specs=out_specs or [VMEM] * len(outs),
        out_shape=outs,
        scratch_shapes=list(scratch),
        input_output_aliases=aliases or {},
        compiler_params=pltpu.CompilerParams(vmem_limit_bytes=mib * 2**20),
        cost_estimate=pl.CostEstimate(flops=flops, bytes_accessed=nbytes, transcendentals=0),
    )(*args)


def core_of():
    return lax.rem(lax.axis_index("stream"), 2)


def mine_is_top():
    return core_of() == lax.rem(lax.axis_index("azim"), 2)


def quotient(x, n):
    return x >> (n.bit_length() - 1) if n & (n - 1) == 0 else x // n


def remainder(x, n):
    return x & (n - 1) if n & (n - 1) == 0 else x % n


def split(x):
    high = x.astype(BF16)
    return high, (x - high.astype(F32)).astype(BF16)


def project(delayed, radiation):
    return lax.dot_general(
        delayed, radiation, (((1,), (1,)), ((), ())), preferred_element_type=F32
    )


def started(pairs, sems):
    copies = [
        pltpu.make_async_copy(source, target, sems.at[n])
        for n, (source, target) in enumerate(pairs)
    ]
    for copy in copies:
        copy.start()
    return copies


def start_kernel(sectors, signal_hbm, weights_hbm, radiation_hbm, state_hbm, *refs):
    send_ref, delayed_ref, far_ref, near_ref, state_ref, weights_ref, *refs = refs
    swap_ref, mine_ref, second_ref, signal_ref, rows_ref, sems = refs
    comps, planes, rows, lanes = state_ref.shape
    tiles = rows // sectors
    block = tiles * lanes
    group = NODE * NODE
    faces = NVAR * group
    half = far_ref.shape[0]
    chunk = half // 2
    core = core_of()
    far = pl.multiple_of((1 - core) * half, half)
    near = pl.multiple_of(core * half, half)
    pairs = [(signal_hbm, signal_ref), (weights_hbm, weights_ref)]
    for first in (0, chunk):
        pairs.append(
            (radiation_hbm.at[pl.ds(far + first, chunk)], far_ref.at[pl.ds(first, chunk)])
        )
    quarter = comps // NODE
    for first in range(0, comps, quarter):
        part = pl.ds(first, quarter)
        pairs.append((state_hbm.at[part], state_ref.at[part]))
    ready = len(pairs)
    pairs.append((radiation_hbm.at[pl.ds(near, half)], near_ref))
    copies = started(pairs, sems)
    copies[0].wait()
    copies[1].wait()
    blocks = weights_ref.shape[0]
    width = signal_ref.shape[1] // blocks
    for b in range(blocks):
        columns = slice(b * width, (b + 1) * width)
        delayed_ref[:, columns] = lax.dot_general(
            weights_ref[b],
            signal_ref[:, columns],
            (((0,), (0,)), ((), ())),
            preferred_element_type=F32,
        ).astype(BF16)
    copies[2].wait()
    send_ref[:, :chunk] = project(delayed_ref[...], far_ref[:chunk, :])
    copies[3].wait()
    send_ref[:, chunk:] = project(delayed_ref[...], far_ref[chunk:, :])
    for copy in copies[4:ready]:
        copy.wait()

    def gather(x, offsets, count):
        for n, offset in enumerate(offsets):
            rows_ref[n * count * rows : (n + 1) * count * rows, :] = (
                state_ref[pl.ds(offset, count), x].astype(F32).reshape(count * rows, lanes)
            )

    def picked(k):
        return rows_ref[pl.ds(k, faces, stride=rows), :].astype(BF16)

    top = mine_is_top()
    for at_top in (0, 1):
        mine_here = top if at_top else jnp.logical_not(top)
        offset = at_top * (NODE - 1) * NODE
        a = at_top * (sectors - 1)
        for x in range(planes):
            gather(x, [n * group + offset for n in range(NVAR * NODE)], NODE)
            for j in range(tiles):
                columns = slice(x * block + j * lanes, x * block + (j + 1) * lanes)
                value = picked(j * sectors + a)

                @pl.when(mine_here)
                def _():
                    mine_ref[:, columns] = value

                @pl.when(jnp.logical_not(mine_here))
                def _():
                    swap_ref[:faces, columns] = value

    def plane_face(at_top, put):
        x = at_top * (planes - 1)
        first = at_top * ((NODE - 1) * group)
        gather(x, [v * NODE * group + first for v in range(NVAR)], group)
        for k in range(rows):
            j, a = divmod(k, sectors)
            first_lane = (a * tiles + j) * lanes
            put(slice(first_lane, first_lane + lanes), picked(k))

    def put_swap(columns, value):
        swap_ref[faces:, columns] = value

    def put_second(columns, value):
        second_ref[:, columns] = value

    plane_face(1 - core, put_swap)
    if second_ref.shape[0] == faces:
        plane_face(core, put_second)
    else:
        second_ref[...] = jnp.zeros(second_ref.shape, BF16)
    for copy in copies[ready:]:
        copy.wait()


def near_kernel(delayed_ref, near_ref, own_ref):
    own_ref[...] = project(delayed_ref[...], near_ref[...])


def join_kernel(own_ref, received_ref, mine_ref, swapped_ref, low_ref, pay_ref):
    faces = mine_ref.shape[0]
    low_ref[...] = (own_ref[...] + received_ref[...]).astype(BF16)
    pay_ref[:faces, :] = mine_ref[...]
    pay_ref[faces:, :] = swapped_ref[:faces, :]


def prepare_kernel(
    sectors,
    state_ref,
    weights_ref,
    target_hbm,
    observer_hbm,
    samples_hbm,
    host_hbm,
    profile_hbm,
    volume_hbm,
    lift_hbm,
    flat_ref,
    op_ref,
    edge_ref,
    v_ref,
    hot_ref,
    row_ref,
    spread_ref,
    target_ref,
    observer_ref,
    plane_ref,
    samples_ref,
    host_ref,
    profile_ref,
    volume_ref,
    lift_ref,
    sems,
):
    copies = started(
        (
            (volume_hbm, volume_ref),
            (lift_hbm, lift_ref),
            (samples_hbm, samples_ref),
            (host_hbm, host_ref),
            (profile_hbm, profile_ref),
            (observer_hbm, observer_ref),
            (target_hbm, target_ref),
        ),
        sems,
    )
    comps, planes, rows, lanes = state_ref.shape
    tiles = rows // sectors
    width = sectors * tiles * lanes
    group = NODE * NODE
    faces = NVAR * group
    for x in range(planes):
        plane_ref[x] = state_ref[:, x].astype(F32).reshape(comps * rows, lanes)
        for k in range(rows):
            j, a = divmod(k, sectors)
            first = x * width + (a * tiles + j) * lanes
            flat_ref[:, first : first + lanes] = plane_ref[
                x, pl.ds(k, comps, stride=rows), :
            ].astype(BF16)
    for copy in copies:
        copy.wait()
    op_ref[:, :comps] = volume_ref[...]
    op_ref[:, comps : comps + 2 * faces] = lift_ref[:, : 2 * faces]
    face = lax.broadcasted_iota(jnp.int32, (2 * faces, comps), 0)
    comp = lax.broadcasted_iota(jnp.int32, (2 * faces, comps), 1)
    upper = (face < faces).astype(jnp.int32) * (NODE - 1)
    row = jnp.where(face < faces, face, face - faces)
    sector_at = quotient(row, NODE) * group + remainder(row, NODE) + upper * NODE
    radial_at = row * NODE + upper
    first = comps + 2 * faces
    for at, start in ((sector_at, 2 * faces), (radial_at, 4 * faces)):
        place = (comp == at).astype(F32).astype(BF16)
        op_ref[:, first : first + comps] = jnp.dot(
            lift_ref[:, start : start + 2 * faces], place, preferred_element_type=F32
        ).astype(BF16)
        first += comps
    edge_ref[:, :faces] = lift_ref[:, 2 * faces : 3 * faces]
    edge_ref[:, LANES : LANES + faces] = lift_ref[:, 3 * faces : 4 * faces]

    blocks, window, _ = weights_ref.shape
    samples = jnp.concatenate([samples_ref[...]] * blocks, axis=1)
    owner = lax.broadcasted_iota(jnp.int32, (blocks, blocks * window), 0)
    entry = lax.broadcasted_iota(jnp.int32, (blocks, blocks * window), 1)
    chosen = jnp.where(owner == quotient(entry, window), samples, 0.0)
    stacked = weights_ref[...].reshape(blocks * window, window)
    v_ref[...] = sum(
        jnp.dot(part, stacked, preferred_element_type=F32) for part in split(chosen)
    )
    points = hot_ref.shape[1]
    within = lax.broadcasted_iota(jnp.int32, (lanes, points), 0)
    host = host_ref[...]
    hot_ref[...] = (within == remainder(host, lanes)).astype(F32).astype(BF16)
    row_ref[...] = (
        quotient(host, rows * lanes) * rows
        + remainder(quotient(host, lanes), tiles) * sectors
        + remainder(quotient(host, lanes * tiles), sectors)
    )

    line = lax.broadcasted_iota(jnp.int32, (comps, comps), 0)
    cross = lax.broadcasted_iota(jnp.int32, (comps, comps), 1)
    diagonal = jnp.where(line == cross, profile_ref[...].reshape(1, comps), 0.0)
    ones = jnp.ones((comps, lanes), BF16)
    high, low = split(diagonal)
    lowest = (diagonal - high.astype(F32) - low.astype(F32)).astype(BF16)
    column = sum(
        jnp.dot(part, ones, preferred_element_type=F32) for part in (high, low, lowest)
    )
    for k in range(rows):
        spread_ref[pl.ds(k, comps, stride=rows), :] = column


def planes_kernel(
    first_plane,
    planes,
    sectors,
    flat_ref,
    op_ref,
    swapped_ref,
    second_ref,
    *refs,
):
    out_refs = refs[:-1]
    stack_ref = refs[-1]
    comps = flat_ref.shape[0]
    width = flat_ref.shape[1] // planes
    group = NODE * NODE
    faces = NVAR * group
    block = width // sectors
    tiles = block // LANES
    rows = sectors * tiles
    comp = lax.broadcasted_iota(jnp.int32, (comps, block), 0)
    lane = lax.broadcasted_iota(jnp.int32, (comps, block), 1)
    q = remainder(quotient(comp, NODE), NODE)
    w = remainder(comp, NODE)
    q_top = (q == NODE - 1).astype(F32).astype(BF16)
    q_low = (q == 0).astype(F32).astype(BF16)
    w_top = ((w == NODE - 1) & (lane > 0)).astype(F32).astype(BF16)
    w_low = ((w == 0) & (lane < block - 1)).astype(F32).astype(BF16)
    odd = core_of() == 1

    def second(v):
        if second_ref.shape[0] == faces:
            return second_ref[v * group : (v + 1) * group, :]
        return jnp.zeros((group, width), BF16)

    def first(v):
        return swapped_ref[faces + v * group : faces + (v + 1) * group, :]

    for n, out_ref in enumerate(out_refs):
        x = first_plane + n
        here = x * width
        own = flat_ref[:, here : here + width]
        stack_ref[n, :comps, :] = own
        for v in range(NVAR):
            low_row = v * NODE * group
            top_row = low_row + (NODE - 1) * group
            at = comps + v * group
            if x > 0:
                value = flat_ref[top_row : top_row + group, here - width : here]
            else:
                value = jnp.where(odd, first(v), second(v))
            stack_ref[n, at : at + group, :] = value
            at += faces
            if x < planes - 1:
                value = flat_ref[low_row : low_row + group, here + width : here + 2 * width]
            else:
                value = jnp.where(odd, second(v), first(v))
            stack_ref[n, at : at + group, :] = value
        mix = comps + 2 * faces
        for a in range(sectors):
            at = a * block
            columns = slice(at, at + block)
            part = flat_ref[:, here + at : here + at + block]
            sector = None
            if a > 0:
                sector = q_top * flat_ref[:, here + at - block : here + at]
            if a < sectors - 1:
                right = q_low * flat_ref[:, here + at + block : here + at + 2 * block]
                sector = right if sector is None else sector + right
            if sector is None:
                sector = jnp.zeros((comps, block), BF16)
            stack_ref[n, mix : mix + comps, columns] = sector
            stack_ref[n, mix + comps :, columns] = w_top * pltpu.roll(
                part, 1, 1
            ) + w_low * pltpu.roll(part, block - 1, 1)
        result = jnp.dot(op_ref[...], stack_ref[n], preferred_element_type=F32)
        for k in range(rows):
            j, a = divmod(k, sectors)
            at = (a * tiles + j) * LANES
            out_ref[pl.ds(k, comps, stride=rows), :] = result[:, at : at + LANES] + own[
                :, at : at + LANES
            ].astype(F32)


def strength_part(v_ref, sens, radiation):
    blocks = v_ref.shape[0]
    points = radiation.shape[1]
    v_high, v_low = split(v_ref[...])
    s_high, s_low = split(sens)
    combined = jnp.dot(
        jnp.concatenate([v_high, v_low, v_high], axis=1),
        jnp.concatenate([s_high, s_high, s_low], axis=0),
        preferred_element_type=F32,
    )
    both = jnp.concatenate(split(combined), axis=0)
    product = jnp.dot(both, radiation, preferred_element_type=F32)
    product = product[:blocks] + product[blocks:]
    block = lax.broadcasted_iota(jnp.int32, (blocks, points), 0)
    point = lax.broadcasted_iota(jnp.int32, (blocks, points), 1)
    chosen = block == quotient(point, points // blocks)
    return jnp.sum(jnp.where(chosen, product, 0.0), axis=0, keepdims=True)


def sensitivity(sums, half, taper_ref, weights_ref, target_ref):
    width = sums.shape[1]
    columns = pl.ds(pl.multiple_of(half * width, width), width)
    return weights_ref[:, columns] * taper_ref[...] * (sums - target_ref[:, columns])


def own_kernel(sums_ref, taper_ref, weights_ref, target_ref, v_ref, radiation_ref, part_ref, sens_ref):
    sens = sensitivity(sums_ref[...], core_of(), taper_ref, weights_ref, target_ref)
    sens_ref[...] = sens
    part_ref[...] = strength_part(v_ref, sens, radiation_ref[...])


def final_kernel(
    sectors,
    chunks,
    other_ref,
    own_sens_ref,
    taper_ref,
    weights_ref,
    target_ref,
    v_ref,
    far_ref,
    part_ref,
    row_ref,
    hot_ref,
    spread_ref,
    edge_ref,
    crossed_ref,
    back_ref,
    *rest,
):
    planes = len(rest) - 6
    base_refs = rest[:planes]
    sens_hbm, out_hbm, sens_ref, all_ref, buffer_ref, sems = rest[planes:]
    comps, _, rows, lanes = out_hbm.shape
    tiles = rows // sectors
    block = tiles * lanes
    other_core = 1 - core_of()
    half = far_ref.shape[0]
    start = pl.multiple_of(other_core * half, half)
    sens = sensitivity(other_ref[...], other_core, taper_ref, weights_ref, target_ref)
    strength = part_ref[...] + strength_part(v_ref, sens, far_ref[...])
    at = lax.broadcasted_iota(jnp.int32, (planes * rows, strength.shape[1]), 0)
    placed = jnp.where(at == row_ref[...], strength, 0.0)
    gathered = lax.dot_general(
        jnp.concatenate(split(placed), axis=0),
        hot_ref[...],
        (((1,), (1,)), ((), ())),
        preferred_element_type=F32,
    )
    source = gathered[: planes * rows] + gathered[planes * rows :]
    faces = crossed_ref.shape[0] // 2
    top = mine_is_top()
    crossed = crossed_ref[:faces, :]
    back = back_ref[faces:, :]
    halos = (jnp.where(top, back, crossed), jnp.where(top, crossed, back))
    chunk = comps // chunks
    def output_copy(n, x):
        part = pl.ds(pl.multiple_of(n * chunk, chunk), chunk)
        return pltpu.make_async_copy(
            buffer_ref.at[x, part], out_hbm.at[part, x], sems.at[n * planes + x]
        )

    def write(n, carry):
        part = pl.ds(pl.multiple_of(n * chunk, chunk), chunk)
        lines = pl.ds(pl.multiple_of(n * chunk * rows, chunk * rows), chunk * rows)
        spread = spread_ref[lines, :].reshape(chunk, rows, lanes)
        for x in range(planes):
            buffer_ref[x, part] = (
                base_refs[x][lines, :].reshape(chunk, rows, lanes)
                + spread * source[x * rows : (x + 1) * rows][None]
            )
        for side, a in ((0, 0), (1, sectors - 1)):
            term = jnp.dot(
                edge_ref[part, side * LANES : side * LANES + faces],
                halos[side],
                preferred_element_type=F32,
            )
            for x in range(planes):
                flat_ref = buffer_ref.at[x].reshape(comps * rows, lanes)
                for j in range(tiles):
                    place = pl.ds(n * chunk * rows + j * sectors + a, chunk, stride=rows)
                    column = x * block + j * lanes
                    flat_ref[place, :] = flat_ref[place, :] + term[:, column : column + lanes]
        for x in range(planes):
            output_copy(n, x).start()
        return carry

    lax.fori_loop(0, chunks, write, 0)

    all_ref[:, pl.ds(start, half)] = sens
    all_ref[:, pl.ds(pl.multiple_of((1 - other_core) * half, half), half)] = own_sens_ref[...]
    count = sens_ref.shape[1]
    first = lax.axis_index("azim") * count
    aligned = pl.multiple_of((first // LANES) * LANES, LANES)
    window = all_ref[:, pl.ds(aligned, LANES)]
    turned = pltpu.roll(window, lax.rem(LANES - (first - aligned), LANES), 1)
    sens_ref[...] = turned[:, :count]
    sens_copy = pltpu.make_async_copy(sens_ref, sens_hbm, sems.at[chunks * planes])
    sens_copy.start()

    def finish(n, carry):
        for x in range(planes):
            output_copy(n, x).wait()
        return carry

    lax.fori_loop(0, chunks, finish, 0)
    sens_copy.wait()


def exchange(value, mask, devices):
    return lax.ppermute(value, MESH_AXES, [(i, i ^ mask) for i in range(devices)])


def body(
    surface_signal,
    retarded_weights,
    radiation_weights,
    target_signal,
    observer_weights,
    sample_weights,
    host_element,
    source_profile,
    adjoint_state,
    volume_operator,
    lift_operator,
):
    streams = lax.axis_size("stream")
    around = lax.axis_size("azim")
    devices = streams * around
    window, points = surface_signal.shape
    observers = radiation_weights.shape[0]
    half = observers // 2
    blocks = retarded_weights.shape[0]
    comps, planes, sectors, radial = adjoint_state.shape
    tiles = radial // LANES
    rows = sectors * tiles
    width = sectors * radial
    faces = NVAR * NODE * NODE
    barrier = lax.optimization_barrier
    depth = 3 * comps + 2 * faces

    view = (
        adjoint_state.reshape(comps, planes, sectors, tiles, LANES)
        .transpose(0, 1, 3, 2, 4)
        .reshape(comps, planes, rows, LANES)
    )
    small = [
        target_signal,
        observer_weights.reshape(1, observers),
        sample_weights.reshape(1, window),
        host_element.reshape(1, points),
        source_profile,
        volume_operator,
        lift_operator,
    ]
    large = [surface_signal, retarded_weights, radiation_weights, view]
    send, delayed, far, near, state, retarded, swap, mine, second = call(
        lambda *refs: start_kernel(sectors, *refs),
        [HBM] * len(large),
        [
            vmem((window, half), F32),
            vmem((window, points), BF16),
            vmem((half, points), BF16),
            vmem((half, points), BF16),
            vmem(view.shape, BF16),
            vmem(retarded_weights.shape, BF16),
            vmem((2 * faces, width), BF16),
            vmem((faces, planes * radial), BF16),
            vmem((faces if streams > 2 else 16, width), BF16),
        ],
        [in_hbm(x) for x in large],
        [
            pltpu.VMEM((window, points), BF16),
            pltpu.VMEM((faces * rows, LANES), F32),
            pltpu.SemaphoreType.DMA((5 + NODE,)),
        ],
    )
    received = exchange(send, around, devices)
    swapped = exchange(swap, around, devices)
    own = call(near_kernel, [VMEM] * 2, [vmem((window, half), F32)], [delayed, near])[0]
    low, pay = call(
        join_kernel,
        [VMEM] * 4,
        [vmem((window, half), BF16), vmem((2 * faces, planes * radial), BF16)],
        [own, received, mine, swapped],
    )
    low, pay, state = barrier((low, pay, state))

    bits = [1 << n for n in range((around - 1).bit_length())]
    bits += [around << n for n in range(1, (streams - 1).bit_length())]
    stages = []
    for first in range(0, len(bits), 2):
        pair = bits[first : first + 2]
        stages.append(pair + ([pair[0] | pair[1]] if len(pair) == 2 else []))

    inner = [(i, i ^ 1) for i in range(around)]
    outer = [(i, (i + 1 if i % 2 else i - 1) % around) for i in range(around)]
    pairs = []
    for s in range(streams):
        pairs += [(s * around + i, s * around + j) for i, j in (outer if s % 2 else inner)]
    crossed = lax.ppermute(pay, MESH_AXES, pairs)
    parts = [exchange(low, mask, devices) for mask in stages[0]]
    if streams > 2:
        links = [(s, s + 1) for s in range(1, streams - 1, 2)]
        second = lax.ppermute(second, "stream", links + [(b, a) for a, b in links])
    flat, operator, edge, v, hot, row, spread, target, weights = call(
        lambda *refs: prepare_kernel(sectors, *refs),
        [VMEM] * 2 + [HBM] * len(small),
        [
            vmem((comps, planes * width), BF16),
            vmem((comps, depth), BF16),
            vmem((comps, 2 * LANES), BF16),
            vmem((blocks, window), F32),
            vmem((LANES, points), BF16),
            vmem((1, points), jnp.int32),
            vmem((comps * rows, LANES), F32),
            vmem(target_signal.shape, F32),
            vmem((1, observers), F32),
        ],
        [state, retarded] + [in_hbm(x) for x in small],
        [pltpu.VMEM((planes, comps * rows, LANES), F32)]
        + [pltpu.VMEM(x.shape, x.dtype) for x in small[2:]]
        + [pltpu.SemaphoreType.DMA((len(small),))],
        nbytes=12 * 2**20,
    )

    def combine(low, parts):
        total = low.astype(F32) + parts[0].astype(F32)
        if len(parts) == 3:
            total = total + (parts[1].astype(F32) + parts[2].astype(F32))
        return total

    parts, flat = barrier((parts, flat))
    sums = combine(low, parts)
    low = sums.astype(BF16)

    def run_planes(first, count):
        return call(
            lambda *refs: planes_kernel(first, planes, sectors, *refs),
            [VMEM] * 4,
            [vmem((comps * rows, LANES), F32)] * count,
            [flat, operator, swapped, second],
            [pltpu.VMEM((count, depth, width), BF16)],
            flops=2 * comps * depth * width * count,
            nbytes=count * 4 * 2**20,
        )

    bases = []
    for masks in stages[1:]:
        parts = [exchange(low, mask, devices) for mask in masks]
        if not bases:
            bases = list(run_planes(0, planes // 2)) + list(run_planes(planes // 2, planes // 2))
            parts, bases = barrier((parts, bases))
        sums = combine(low, parts)
        low = sums.astype(BF16)

    remote = exchange(sums, around, devices)
    crossed, bases = barrier((crossed, bases))
    back = exchange(crossed, around, devices)
    taper = np.arange(window, dtype=np.float64)
    taper = (0.5 - 0.5 * np.cos(2.0 * np.pi * (taper + 0.5) / window)).astype(np.float32)
    taper = jnp.asarray(taper).reshape(window, 1)
    part, own_sens = call(
        own_kernel,
        [VMEM] * 6,
        [vmem((1, points), F32), vmem((window, half), F32)],
        [sums, taper, weights, target, v, near],
        flops=2 * 2 * blocks * half * points,
        nbytes=half * points * 2,
    )
    chunks = 5
    sens, updated = call(
        lambda *refs: final_kernel(sectors, chunks, *refs),
        [VMEM] * (14 + planes),
        [
            jax.ShapeDtypeStruct((window, observers // around), F32),
            jax.ShapeDtypeStruct(view.shape, F32),
        ],
        [remote, own_sens, taper, weights, target, v, far, part, row, hot, spread]
        + [edge, crossed, back]
        + list(bases),
        [
            pltpu.VMEM((window, observers // around), F32),
            pltpu.VMEM((window, observers), F32),
            pltpu.VMEM((planes, comps, rows, LANES), F32),
            pltpu.SemaphoreType.DMA((chunks * planes + 1,)),
        ],
        nbytes=12 * 2**20,
        out_specs=[HBM, HBM],
    )
    updated = (
        updated.reshape(comps, planes, tiles, sectors, LANES)
        .transpose(0, 1, 3, 2, 4)
        .reshape(adjoint_state.shape)
    )
    return sens, updated


def solution(mesh):
    return jax.shard_map(
        body,
        mesh=mesh,
        in_specs=(
            P(None, ("stream", "azim")),
            P(("stream", "azim"), None, None),
            P(None, ("stream", "azim")),
            P(),
            P(),
            P(),
            P(("stream", "azim")),
            P(),
            P(None, "stream", "azim", None),
            P(),
            P(),
        ),
        out_specs=(P(None, "azim"), P(None, "stream", "azim", None)),
        check_vma=False,
    )
```

```python
import jax
import jax.numpy as jnp
import numpy as np
from jax import lax
from jax.experimental import pallas as pl
from jax.experimental.pallas import tpu as pltpu
from jax.sharding import PartitionSpec as P

NVAR = 5
NODE = 4
LANES = 128
F32 = jnp.float32
BF16 = jnp.bfloat16
MESH_AXES = ("stream", "azim")
VMEM = pl.BlockSpec(memory_space=pltpu.VMEM)
HBM = pl.BlockSpec(memory_space=pl.ANY)


def vmem(shape, dtype):
    return pltpu.VMEM(shape, dtype)


def in_hbm(x):
    return pltpu.with_memory_space_constraint(x, pltpu.HBM)


def call(kernel, ins, outs, args, scratch=(), mib=16, flops=0, nbytes=0, out_specs=None, aliases=None):
    return pl.pallas_call(
        kernel,
        in_specs=ins,
        out_specs=out_specs or [VMEM] * len(outs),
        out_shape=outs,
        scratch_shapes=list(scratch),
        input_output_aliases=aliases or {},
        compiler_params=pltpu.CompilerParams(vmem_limit_bytes=mib * 2**20),
        cost_estimate=pl.CostEstimate(flops=flops, bytes_accessed=nbytes, transcendentals=0),
    )(*args)


def core_of():
    return lax.rem(lax.axis_index("stream"), 2)


def mine_is_top():
    return core_of() == lax.rem(lax.axis_index("azim"), 2)


def quotient(x, n):
    return x >> (n.bit_length() - 1) if n & (n - 1) == 0 else x // n


def remainder(x, n):
    return x & (n - 1) if n & (n - 1) == 0 else x % n


def split(x):
    high = x.astype(BF16)
    return high, (x - high.astype(F32)).astype(BF16)


def project(delayed, radiation):
    return lax.dot_general(
        delayed, radiation, (((1,), (1,)), ((), ())), preferred_element_type=F32
    )


def started(pairs, sems):
    copies = [
        pltpu.make_async_copy(source, target, sems.at[n])
        for n, (source, target) in enumerate(pairs)
    ]
    for copy in copies:
        copy.start()
    return copies


def start_kernel(sectors, signal_hbm, weights_hbm, radiation_hbm, state_hbm, *refs):
    send_ref, delayed_ref, far_ref, near_ref, state_ref, weights_ref, *refs = refs
    swap_ref, mine_ref, second_ref, signal_ref, rows_ref, sems = refs
    comps, planes, rows, lanes = state_ref.shape
    tiles = rows // sectors
    block = tiles * lanes
    group = NODE * NODE
    faces = NVAR * group
    half = far_ref.shape[0]
    chunk = half // 2
    core = core_of()
    far = pl.multiple_of((1 - core) * half, half)
    near = pl.multiple_of(core * half, half)
    pairs = [(signal_hbm, signal_ref), (weights_hbm, weights_ref)]
    for first in (0, chunk):
        pairs.append(
            (radiation_hbm.at[pl.ds(far + first, chunk)], far_ref.at[pl.ds(first, chunk)])
        )
    quarter = comps // NODE
    for first in range(0, comps, quarter):
        part = pl.ds(first, quarter)
        pairs.append((state_hbm.at[part], state_ref.at[part]))
    ready = len(pairs)
    pairs.append((radiation_hbm.at[pl.ds(near, half)], near_ref))
    copies = started(pairs, sems)
    copies[0].wait()
    copies[1].wait()
    blocks = weights_ref.shape[0]
    width = signal_ref.shape[1] // blocks
    for b in range(blocks):
        columns = slice(b * width, (b + 1) * width)
        delayed_ref[:, columns] = lax.dot_general(
            weights_ref[b],
            signal_ref[:, columns],
            (((0,), (0,)), ((), ())),
            preferred_element_type=F32,
        ).astype(BF16)
    copies[2].wait()
    send_ref[:, :chunk] = project(delayed_ref[...], far_ref[:chunk, :])
    copies[3].wait()
    send_ref[:, chunk:] = project(delayed_ref[...], far_ref[chunk:, :])
    for copy in copies[4:ready]:
        copy.wait()

    def gather(x, offsets, count):
        for n, offset in enumerate(offsets):
            rows_ref[n * count * rows : (n + 1) * count * rows, :] = (
                state_ref[pl.ds(offset, count), x].astype(F32).reshape(count * rows, lanes)
            )

    def picked(k):
        return rows_ref[pl.ds(k, faces, stride=rows), :].astype(BF16)

    top = mine_is_top()
    for at_top in (0, 1):
        mine_here = top if at_top else jnp.logical_not(top)
        offset = at_top * (NODE - 1) * NODE
        a = at_top * (sectors - 1)
        for x in range(planes):
            gather(x, [n * group + offset for n in range(NVAR * NODE)], NODE)
            for j in range(tiles):
                columns = slice(x * block + j * lanes, x * block + (j + 1) * lanes)
                value = picked(j * sectors + a)

                @pl.when(mine_here)
                def _():
                    mine_ref[:, columns] = value

                @pl.when(jnp.logical_not(mine_here))
                def _():
                    swap_ref[:faces, columns] = value

    def plane_face(at_top, put):
        x = at_top * (planes - 1)
        first = at_top * ((NODE - 1) * group)
        gather(x, [v * NODE * group + first for v in range(NVAR)], group)
        for k in range(rows):
            j, a = divmod(k, sectors)
            first_lane = (a * tiles + j) * lanes
            put(slice(first_lane, first_lane + lanes), picked(k))

    def put_swap(columns, value):
        swap_ref[faces:, columns] = value

    def put_second(columns, value):
        second_ref[:, columns] = value

    plane_face(1 - core, put_swap)
    if second_ref.shape[0] == faces:
        plane_face(core, put_second)
    else:
        second_ref[...] = jnp.zeros(second_ref.shape, BF16)
    for copy in copies[ready:]:
        copy.wait()


def near_kernel(delayed_ref, near_ref, own_ref):
    own_ref[...] = project(delayed_ref[...], near_ref[...])


def join_kernel(own_ref, received_ref, mine_ref, swapped_ref, low_ref, pay_ref):
    faces = mine_ref.shape[0]
    low_ref[...] = (own_ref[...] + received_ref[...]).astype(BF16)
    pay_ref[:faces, :] = mine_ref[...]
    pay_ref[faces:, :] = swapped_ref[:faces, :]


def prepare_kernel(
    sectors,
    state_ref,
    weights_ref,
    target_hbm,
    observer_hbm,
    samples_hbm,
    host_hbm,
    profile_hbm,
    volume_hbm,
    lift_hbm,
    flat_ref,
    op_ref,
    edge_ref,
    v_ref,
    hot_ref,
    row_ref,
    spread_ref,
    target_ref,
    observer_ref,
    plane_ref,
    samples_ref,
    host_ref,
    profile_ref,
    volume_ref,
    lift_ref,
    sems,
):
    copies = started(
        (
            (volume_hbm, volume_ref),
            (lift_hbm, lift_ref),
            (samples_hbm, samples_ref),
            (host_hbm, host_ref),
            (profile_hbm, profile_ref),
            (observer_hbm, observer_ref),
            (target_hbm, target_ref),
        ),
        sems,
    )
    comps, planes, rows, lanes = state_ref.shape
    tiles = rows // sectors
    width = sectors * tiles * lanes
    group = NODE * NODE
    faces = NVAR * group
    for x in range(planes):
        plane_ref[x] = state_ref[:, x].astype(F32).reshape(comps * rows, lanes)
        for k in range(rows):
            j, a = divmod(k, sectors)
            first = x * width + (a * tiles + j) * lanes
            flat_ref[:, first : first + lanes] = plane_ref[
                x, pl.ds(k, comps, stride=rows), :
            ].astype(BF16)
    for copy in copies:
        copy.wait()
    op_ref[:, :comps] = volume_ref[...]
    op_ref[:, comps : comps + 2 * faces] = lift_ref[:, : 2 * faces]
    face = lax.broadcasted_iota(jnp.int32, (2 * faces, comps), 0)
    comp = lax.broadcasted_iota(jnp.int32, (2 * faces, comps), 1)
    upper = (face < faces).astype(jnp.int32) * (NODE - 1)
    row = jnp.where(face < faces, face, face - faces)
    sector_at = quotient(row, NODE) * group + remainder(row, NODE) + upper * NODE
    radial_at = row * NODE + upper
    first = comps + 2 * faces
    for at, start in ((sector_at, 2 * faces), (radial_at, 4 * faces)):
        place = (comp == at).astype(F32).astype(BF16)
        op_ref[:, first : first + comps] = jnp.dot(
            lift_ref[:, start : start + 2 * faces], place, preferred_element_type=F32
        ).astype(BF16)
        first += comps
    edge_ref[:, :faces] = lift_ref[:, 2 * faces : 3 * faces]
    edge_ref[:, LANES : LANES + faces] = lift_ref[:, 3 * faces : 4 * faces]

    blocks, window, _ = weights_ref.shape
    samples = jnp.concatenate([samples_ref[...]] * blocks, axis=1)
    owner = lax.broadcasted_iota(jnp.int32, (blocks, blocks * window), 0)
    entry = lax.broadcasted_iota(jnp.int32, (blocks, blocks * window), 1)
    chosen = jnp.where(owner == quotient(entry, window), samples, 0.0)
    stacked = weights_ref[...].reshape(blocks * window, window)
    v_ref[...] = sum(
        jnp.dot(part, stacked, preferred_element_type=F32) for part in split(chosen)
    )
    points = hot_ref.shape[0]
    within = lax.broadcasted_iota(jnp.int32, (lanes, points), 0)
    host = host_ref[...]
    hot_ref[...] = jnp.transpose((within == remainder(host, lanes)).astype(F32)).astype(BF16)
    row_ref[...] = (
        quotient(host, rows * lanes) * rows
        + remainder(quotient(host, lanes), tiles) * sectors
        + remainder(quotient(host, lanes * tiles), sectors)
    )

    line = lax.broadcasted_iota(jnp.int32, (comps, comps), 0)
    cross = lax.broadcasted_iota(jnp.int32, (comps, comps), 1)
    diagonal = jnp.where(line == cross, profile_ref[...].reshape(1, comps), 0.0)
    ones = jnp.ones((comps, lanes), BF16)
    high, low = split(diagonal)
    lowest = (diagonal - high.astype(F32) - low.astype(F32)).astype(BF16)
    column = sum(
        jnp.dot(part, ones, preferred_element_type=F32) for part in (high, low, lowest)
    )
    for k in range(rows):
        spread_ref[pl.ds(k, comps, stride=rows), :] = column


def planes_kernel(
    first_plane,
    planes,
    sectors,
    flat_ref,
    op_ref,
    swapped_ref,
    second_ref,
    *refs,
):
    out_refs = refs[:-1]
    stack_ref = refs[-1]
    comps = flat_ref.shape[0]
    width = flat_ref.shape[1] // planes
    group = NODE * NODE
    faces = NVAR * group
    block = width // sectors
    tiles = block // LANES
    rows = sectors * tiles
    comp = lax.broadcasted_iota(jnp.int32, (comps, block), 0)
    lane = lax.broadcasted_iota(jnp.int32, (comps, block), 1)
    q = remainder(quotient(comp, NODE), NODE)
    w = remainder(comp, NODE)
    q_top = (q == NODE - 1).astype(F32).astype(BF16)
    q_low = (q == 0).astype(F32).astype(BF16)
    w_top = ((w == NODE - 1) & (lane > 0)).astype(F32).astype(BF16)
    w_low = ((w == 0) & (lane < block - 1)).astype(F32).astype(BF16)
    odd = core_of() == 1

    def second(v):
        if second_ref.shape[0] == faces:
            return second_ref[v * group : (v + 1) * group, :]
        return jnp.zeros((group, width), BF16)

    def first(v):
        return swapped_ref[faces + v * group : faces + (v + 1) * group, :]

    for n, out_ref in enumerate(out_refs):
        x = first_plane + n
        here = x * width
        own = flat_ref[:, here : here + width]
        stack_ref[n, :comps, :] = own
        for v in range(NVAR):
            low_row = v * NODE * group
            top_row = low_row + (NODE - 1) * group
            at = comps + v * group
            if x > 0:
                value = flat_ref[top_row : top_row + group, here - width : here]
            else:
                value = jnp.where(odd, first(v), second(v))
            stack_ref[n, at : at + group, :] = value
            at += faces
            if x < planes - 1:
                value = flat_ref[low_row : low_row + group, here + width : here + 2 * width]
            else:
                value = jnp.where(odd, second(v), first(v))
            stack_ref[n, at : at + group, :] = value
        mix = comps + 2 * faces
        for a in range(sectors):
            at = a * block
            columns = slice(at, at + block)
            part = flat_ref[:, here + at : here + at + block]
            sector = None
            if a > 0:
                sector = q_top * flat_ref[:, here + at - block : here + at]
            if a < sectors - 1:
                right = q_low * flat_ref[:, here + at + block : here + at + 2 * block]
                sector = right if sector is None else sector + right
            if sector is None:
                sector = jnp.zeros((comps, block), BF16)
            stack_ref[n, mix : mix + comps, columns] = sector
            stack_ref[n, mix + comps :, columns] = w_top * pltpu.roll(
                part, 1, 1
            ) + w_low * pltpu.roll(part, block - 1, 1)
        result = jnp.dot(op_ref[...], stack_ref[n], preferred_element_type=F32)
        for k in range(rows):
            j, a = divmod(k, sectors)
            at = (a * tiles + j) * LANES
            out_ref[pl.ds(k, comps, stride=rows), :] = result[:, at : at + LANES] + own[
                :, at : at + LANES
            ].astype(F32)


def strength_part(v_ref, sens, radiation):
    blocks = v_ref.shape[0]
    points = radiation.shape[1]
    v_high, v_low = split(v_ref[...])
    s_high, s_low = split(sens)
    combined = jnp.dot(
        jnp.concatenate([v_high, v_low, v_high], axis=1),
        jnp.concatenate([s_high, s_high, s_low], axis=0),
        preferred_element_type=F32,
    )
    both = jnp.concatenate(split(combined), axis=0)
    product = jnp.dot(both, radiation, preferred_element_type=F32)
    product = product[:blocks] + product[blocks:]
    block = lax.broadcasted_iota(jnp.int32, (blocks, points), 0)
    point = lax.broadcasted_iota(jnp.int32, (blocks, points), 1)
    chosen = block == quotient(point, points // blocks)
    return jnp.sum(jnp.where(chosen, product, 0.0), axis=0, keepdims=True)


def sensitivity(sums, half, taper_ref, weights_ref, target_ref):
    width = sums.shape[1]
    columns = pl.ds(pl.multiple_of(half * width, width), width)
    return weights_ref[:, columns] * taper_ref[...] * (sums - target_ref[:, columns])


def own_kernel(sums_ref, taper_ref, weights_ref, target_ref, v_ref, radiation_ref, part_ref, sens_ref):
    sens = sensitivity(sums_ref[...], core_of(), taper_ref, weights_ref, target_ref)
    sens_ref[...] = sens
    part_ref[...] = strength_part(v_ref, sens, radiation_ref[...])


def final_kernel(
    sectors,
    chunks,
    other_ref,
    own_sens_ref,
    taper_ref,
    weights_ref,
    target_ref,
    v_ref,
    far_ref,
    part_ref,
    row_ref,
    hot_ref,
    spread_ref,
    edge_ref,
    crossed_ref,
    back_ref,
    *rest,
):
    planes = len(rest) - 6
    base_refs = rest[:planes]
    sens_hbm, out_hbm, sens_ref, all_ref, buffer_ref, sems = rest[planes:]
    comps, _, rows, lanes = out_hbm.shape
    tiles = rows // sectors
    block = tiles * lanes
    other_core = 1 - core_of()
    half = far_ref.shape[0]
    start = pl.multiple_of(other_core * half, half)
    sens = sensitivity(other_ref[...], other_core, taper_ref, weights_ref, target_ref)
    strength = part_ref[...] + strength_part(v_ref, sens, far_ref[...])
    at = lax.broadcasted_iota(jnp.int32, (planes * rows, strength.shape[1]), 0)
    placed = jnp.where(at == row_ref[...], strength, 0.0)
    gathered = lax.dot_general(
        jnp.concatenate(split(placed), axis=0),
        hot_ref[...],
        (((1,), (0,)), ((), ())),
        preferred_element_type=F32,
    )
    source = gathered[: planes * rows] + gathered[planes * rows :]
    faces = crossed_ref.shape[0] // 2
    top = mine_is_top()
    crossed = crossed_ref[:faces, :]
    back = back_ref[faces:, :]
    halos = (jnp.where(top, back, crossed), jnp.where(top, crossed, back))
    chunk = comps // chunks
    def output_copy(n, x):
        part = pl.ds(pl.multiple_of(n * chunk, chunk), chunk)
        return pltpu.make_async_copy(
            buffer_ref.at[x, part], out_hbm.at[part, x], sems.at[n * planes + x]
        )

    def write(n, carry):
        part = pl.ds(pl.multiple_of(n * chunk, chunk), chunk)
        lines = pl.ds(pl.multiple_of(n * chunk * rows, chunk * rows), chunk * rows)
        spread = spread_ref[lines, :].reshape(chunk, rows, lanes)
        for x in range(planes):
            buffer_ref[x, part] = (
                base_refs[x][lines, :].reshape(chunk, rows, lanes)
                + spread * source[x * rows : (x + 1) * rows][None]
            )
        for side, a in ((0, 0), (1, sectors - 1)):
            term = jnp.dot(
                edge_ref[part, side * LANES : side * LANES + faces],
                halos[side],
                preferred_element_type=F32,
            )
            for x in range(planes):
                flat_ref = buffer_ref.at[x].reshape(comps * rows, lanes)
                for j in range(tiles):
                    place = pl.ds(n * chunk * rows + j * sectors + a, chunk, stride=rows)
                    column = x * block + j * lanes
                    flat_ref[place, :] = flat_ref[place, :] + term[:, column : column + lanes]
        for x in range(planes):
            output_copy(n, x).start()
        return carry

    lax.fori_loop(0, chunks, write, 0)

    all_ref[:, pl.ds(start, half)] = sens
    all_ref[:, pl.ds(pl.multiple_of((1 - other_core) * half, half), half)] = own_sens_ref[...]
    count = sens_ref.shape[1]
    first = lax.axis_index("azim") * count
    aligned = pl.multiple_of((first // LANES) * LANES, LANES)
    window = all_ref[:, pl.ds(aligned, LANES)]
    turned = pltpu.roll(window, lax.rem(LANES - (first - aligned), LANES), 1)
    sens_ref[...] = turned[:, :count]
    sens_copy = pltpu.make_async_copy(sens_ref, sens_hbm, sems.at[chunks * planes])
    sens_copy.start()

    def finish(n, carry):
        for x in range(planes):
            output_copy(n, x).wait()
        return carry

    lax.fori_loop(0, chunks, finish, 0)
    sens_copy.wait()


def exchange(value, mask, devices):
    return lax.ppermute(value, MESH_AXES, [(i, i ^ mask) for i in range(devices)])


def body(
    surface_signal,
    retarded_weights,
    radiation_weights,
    target_signal,
    observer_weights,
    sample_weights,
    host_element,
    source_profile,
    adjoint_state,
    volume_operator,
    lift_operator,
):
    streams = lax.axis_size("stream")
    around = lax.axis_size("azim")
    devices = streams * around
    window, points = surface_signal.shape
    observers = radiation_weights.shape[0]
    half = observers // 2
    blocks = retarded_weights.shape[0]
    comps, planes, sectors, radial = adjoint_state.shape
    tiles = radial // LANES
    rows = sectors * tiles
    width = sectors * radial
    faces = NVAR * NODE * NODE
    barrier = lax.optimization_barrier
    depth = 3 * comps + 2 * faces

    view = (
        adjoint_state.reshape(comps, planes, sectors, tiles, LANES)
        .transpose(0, 1, 3, 2, 4)
        .reshape(comps, planes, rows, LANES)
    )
    small = [
        target_signal,
        observer_weights.reshape(1, observers),
        sample_weights.reshape(1, window),
        host_element.reshape(1, points),
        source_profile,
        volume_operator,
        lift_operator,
    ]
    large = [surface_signal, retarded_weights, radiation_weights, view]
    send, delayed, far, near, state, retarded, swap, mine, second = call(
        lambda *refs: start_kernel(sectors, *refs),
        [HBM] * len(large),
        [
            vmem((window, half), F32),
            vmem((window, points), BF16),
            vmem((half, points), BF16),
            vmem((half, points), BF16),
            vmem(view.shape, BF16),
            vmem(retarded_weights.shape, BF16),
            vmem((2 * faces, width), BF16),
            vmem((faces, planes * radial), BF16),
            vmem((faces if streams > 2 else 16, width), BF16),
        ],
        [in_hbm(x) for x in large],
        [
            pltpu.VMEM((window, points), BF16),
            pltpu.VMEM((faces * rows, LANES), F32),
            pltpu.SemaphoreType.DMA((5 + NODE,)),
        ],
    )
    received = exchange(send, around, devices)
    swapped = exchange(swap, around, devices)
    own = call(near_kernel, [VMEM] * 2, [vmem((window, half), F32)], [delayed, near])[0]
    low, pay = call(
        join_kernel,
        [VMEM] * 4,
        [vmem((window, half), BF16), vmem((2 * faces, planes * radial), BF16)],
        [own, received, mine, swapped],
    )
    low, pay, state = barrier((low, pay, state))

    bits = [1 << n for n in range((around - 1).bit_length())]
    bits += [around << n for n in range(1, (streams - 1).bit_length())]
    stages = []
    for first in range(0, len(bits), 2):
        pair = bits[first : first + 2]
        stages.append(pair + ([pair[0] | pair[1]] if len(pair) == 2 else []))

    inner = [(i, i ^ 1) for i in range(around)]
    outer = [(i, (i + 1 if i % 2 else i - 1) % around) for i in range(around)]
    pairs = []
    for s in range(streams):
        pairs += [(s * around + i, s * around + j) for i, j in (outer if s % 2 else inner)]
    crossed = lax.ppermute(pay, MESH_AXES, pairs)
    parts = [exchange(low, mask, devices) for mask in stages[0]]
    if streams > 2:
        links = [(s, s + 1) for s in range(1, streams - 1, 2)]
        second = lax.ppermute(second, "stream", links + [(b, a) for a, b in links])
    flat, operator, edge, v, hot, row, spread, target, weights = call(
        lambda *refs: prepare_kernel(sectors, *refs),
        [VMEM] * 2 + [HBM] * len(small),
        [
            vmem((comps, planes * width), BF16),
            vmem((comps, depth), BF16),
            vmem((comps, 2 * LANES), BF16),
            vmem((blocks, window), F32),
            vmem((points, LANES), BF16),
            vmem((1, points), jnp.int32),
            vmem((comps * rows, LANES), F32),
            vmem(target_signal.shape, F32),
            vmem((1, observers), F32),
        ],
        [state, retarded] + [in_hbm(x) for x in small],
        [pltpu.VMEM((planes, comps * rows, LANES), F32)]
        + [pltpu.VMEM(x.shape, x.dtype) for x in small[2:]]
        + [pltpu.SemaphoreType.DMA((len(small),))],
        nbytes=12 * 2**20,
    )

    def combine(low, parts):
        total = low.astype(F32) + parts[0].astype(F32)
        if len(parts) == 3:
            total = total + (parts[1].astype(F32) + parts[2].astype(F32))
        return total

    parts, flat = barrier((parts, flat))
    sums = combine(low, parts)
    low = sums.astype(BF16)

    def run_planes(first, count):
        return call(
            lambda *refs: planes_kernel(first, planes, sectors, *refs),
            [VMEM] * 4,
            [vmem((comps * rows, LANES), F32)] * count,
            [flat, operator, swapped, second],
            [pltpu.VMEM((count, depth, width), BF16)],
            flops=2 * comps * depth * width * count,
            nbytes=count * 4 * 2**20,
        )

    bases = []
    for masks in stages[1:]:
        parts = [exchange(low, mask, devices) for mask in masks]
        if not bases:
            bases = list(run_planes(0, planes // 2)) + list(run_planes(planes // 2, planes // 2))
            parts, bases = barrier((parts, bases))
        sums = combine(low, parts)
        low = sums.astype(BF16)

    remote = exchange(sums, around, devices)
    crossed, bases = barrier((crossed, bases))
    back = exchange(crossed, around, devices)
    taper = np.arange(window, dtype=np.float64)
    taper = (0.5 - 0.5 * np.cos(2.0 * np.pi * (taper + 0.5) / window)).astype(np.float32)
    taper = jnp.asarray(taper).reshape(window, 1)
    part, own_sens = call(
        own_kernel,
        [VMEM] * 6,
        [vmem((1, points), F32), vmem((window, half), F32)],
        [sums, taper, weights, target, v, near],
        flops=2 * 2 * blocks * half * points,
        nbytes=half * points * 2,
    )
    chunks = 5
    sens, updated = call(
        lambda *refs: final_kernel(sectors, chunks, *refs),
        [VMEM] * (14 + planes),
        [
            jax.ShapeDtypeStruct((window, observers // around), F32),
            jax.ShapeDtypeStruct(view.shape, F32),
        ],
        [remote, own_sens, taper, weights, target, v, far, part, row, hot, spread]
        + [edge, crossed, back]
        + list(bases),
        [
            pltpu.VMEM((window, observers // around), F32),
            pltpu.VMEM((window, observers), F32),
            pltpu.VMEM((planes, comps, rows, LANES), F32),
            pltpu.SemaphoreType.DMA((chunks * planes + 1,)),
        ],
        nbytes=12 * 2**20,
        out_specs=[HBM, HBM],
    )
    updated = (
        updated.reshape(comps, planes, tiles, sectors, LANES)
        .transpose(0, 1, 3, 2, 4)
        .reshape(adjoint_state.shape)
    )
    return sens, updated


def solution(mesh):
    return jax.shard_map(
        body,
        mesh=mesh,
        in_specs=(
            P(None, ("stream", "azim")),
            P(("stream", "azim"), None, None),
            P(None, ("stream", "azim")),
            P(),
            P(),
            P(),
            P(("stream", "azim")),
            P(),
            P(None, "stream", "azim", None),
            P(),
            P(),
        ),
        out_specs=(P(None, "azim"), P(None, "stream", "azim", None)),
        check_vma=False,
    )
```

```python
import jax
import jax.numpy as jnp
import numpy as np
from jax import lax
from jax.experimental import pallas as pl
from jax.experimental.pallas import tpu as pltpu
from jax.sharding import PartitionSpec as P

NVAR = 5
NODE = 4
LANES = 128
F32 = jnp.float32
BF16 = jnp.bfloat16
MESH_AXES = ("stream", "azim")
VMEM = pl.BlockSpec(memory_space=pltpu.VMEM)
HBM = pl.BlockSpec(memory_space=pl.ANY)


def vmem(shape, dtype):
    return pltpu.VMEM(shape, dtype)


def in_hbm(x):
    return pltpu.with_memory_space_constraint(x, pltpu.HBM)


def call(kernel, ins, outs, args, scratch=(), mib=16, flops=0, nbytes=0, out_specs=None, aliases=None):
    return pl.pallas_call(
        kernel,
        in_specs=ins,
        out_specs=out_specs or [VMEM] * len(outs),
        out_shape=outs,
        scratch_shapes=list(scratch),
        input_output_aliases=aliases or {},
        compiler_params=pltpu.CompilerParams(vmem_limit_bytes=mib * 2**20),
        cost_estimate=pl.CostEstimate(flops=flops, bytes_accessed=nbytes, transcendentals=0),
    )(*args)


def core_of():
    return lax.rem(lax.axis_index("stream"), 2)


def mine_is_top():
    return core_of() == lax.rem(lax.axis_index("azim"), 2)


def quotient(x, n):
    return x >> (n.bit_length() - 1) if n & (n - 1) == 0 else x // n


def remainder(x, n):
    return x & (n - 1) if n & (n - 1) == 0 else x % n


def split(x):
    high = x.astype(BF16)
    return high, (x - high.astype(F32)).astype(BF16)


def project(delayed, radiation):
    return lax.dot_general(
        delayed, radiation, (((1,), (1,)), ((), ())), preferred_element_type=F32
    )


def started(pairs, sems):
    copies = [
        pltpu.make_async_copy(source, target, sems.at[n])
        for n, (source, target) in enumerate(pairs)
    ]
    for copy in copies:
        copy.start()
    return copies


def start_kernel(sectors, signal_hbm, weights_hbm, radiation_hbm, state_hbm, *refs):
    send_ref, delayed_ref, far_ref, near_ref, state_ref, weights_ref, *refs = refs
    swap_ref, mine_ref, second_ref, signal_ref, rows_ref, sems = refs
    comps, planes, rows, lanes = state_ref.shape
    tiles = rows // sectors
    block = tiles * lanes
    group = NODE * NODE
    faces = NVAR * group
    half = far_ref.shape[0]
    chunk = half // 2
    core = core_of()
    far = pl.multiple_of((1 - core) * half, half)
    near = pl.multiple_of(core * half, half)
    pairs = [(signal_hbm, signal_ref), (weights_hbm, weights_ref)]
    for first in (0, chunk):
        pairs.append(
            (radiation_hbm.at[pl.ds(far + first, chunk)], far_ref.at[pl.ds(first, chunk)])
        )
    quarter = comps // NODE
    for first in range(0, comps, quarter):
        part = pl.ds(first, quarter)
        pairs.append((state_hbm.at[part], state_ref.at[part]))
    ready = len(pairs)
    pairs.append((radiation_hbm.at[pl.ds(near, half)], near_ref))
    copies = started(pairs, sems)
    copies[0].wait()
    copies[1].wait()
    blocks = weights_ref.shape[0]
    width = signal_ref.shape[1] // blocks
    for b in range(blocks):
        columns = slice(b * width, (b + 1) * width)
        delayed_ref[:, columns] = lax.dot_general(
            weights_ref[b],
            signal_ref[:, columns],
            (((0,), (0,)), ((), ())),
            preferred_element_type=F32,
        ).astype(BF16)
    copies[2].wait()
    send_ref[:, :chunk] = project(delayed_ref[...], far_ref[:chunk, :])
    copies[3].wait()
    send_ref[:, chunk:] = project(delayed_ref[...], far_ref[chunk:, :])
    for copy in copies[4:ready]:
        copy.wait()

    def gather(x, offsets, count):
        for n, offset in enumerate(offsets):
            rows_ref[n * count * rows : (n + 1) * count * rows, :] = (
                state_ref[pl.ds(offset, count), x].astype(F32).reshape(count * rows, lanes)
            )

    def picked(k):
        return rows_ref[pl.ds(k, faces, stride=rows), :].astype(BF16)

    top = mine_is_top()
    for x in range(planes):
        sides = []
        for at_top in (0, 1):
            offset = at_top * (NODE - 1) * NODE
            gather(x, [n * group + offset for n in range(NVAR * NODE)], NODE)
            first = at_top * (sectors - 1)
            sides.append([picked(j * sectors + first) for j in range(tiles)])
        for j in range(tiles):
            columns = slice(x * block + j * lanes, x * block + (j + 1) * lanes)
            low, high = sides[0][j], sides[1][j]
            mine_ref[:, columns] = jnp.where(top, high, low)
            swap_ref[:faces, columns] = jnp.where(top, low, high)

    def plane_face(at_top, put):
        x = at_top * (planes - 1)
        first = at_top * ((NODE - 1) * group)
        gather(x, [v * NODE * group + first for v in range(NVAR)], group)
        for k in range(rows):
            j, a = divmod(k, sectors)
            first_lane = (a * tiles + j) * lanes
            put(slice(first_lane, first_lane + lanes), picked(k))

    def put_swap(columns, value):
        swap_ref[faces:, columns] = value

    def put_second(columns, value):
        second_ref[:, columns] = value

    plane_face(1 - core, put_swap)
    if second_ref.shape[0] == faces:
        plane_face(core, put_second)
    else:
        second_ref[...] = jnp.zeros(second_ref.shape, BF16)
    for copy in copies[ready:]:
        copy.wait()


def near_kernel(delayed_ref, near_ref, own_ref):
    own_ref[...] = project(delayed_ref[...], near_ref[...])


def join_kernel(own_ref, received_ref, mine_ref, swapped_ref, low_ref, pay_ref):
    faces = mine_ref.shape[0]
    low_ref[...] = (own_ref[...] + received_ref[...]).astype(BF16)
    pay_ref[:faces, :] = mine_ref[...]
    pay_ref[faces:, :] = swapped_ref[:faces, :]


def prepare_kernel(
    sectors,
    state_ref,
    weights_ref,
    target_hbm,
    observer_hbm,
    samples_hbm,
    host_hbm,
    profile_hbm,
    volume_hbm,
    lift_hbm,
    flat_ref,
    op_ref,
    edge_ref,
    v_ref,
    hot_ref,
    row_ref,
    spread_ref,
    target_ref,
    observer_ref,
    plane_ref,
    samples_ref,
    host_ref,
    profile_ref,
    volume_ref,
    lift_ref,
    sems,
):
    copies = started(
        (
            (volume_hbm, volume_ref),
            (lift_hbm, lift_ref),
            (samples_hbm, samples_ref),
            (host_hbm, host_ref),
            (profile_hbm, profile_ref),
            (observer_hbm, observer_ref),
            (target_hbm, target_ref),
        ),
        sems,
    )
    comps, planes, rows, lanes = state_ref.shape
    tiles = rows // sectors
    width = sectors * tiles * lanes
    group = NODE * NODE
    faces = NVAR * group
    for x in range(planes):
        plane_ref[x] = state_ref[:, x].astype(F32).reshape(comps * rows, lanes)
        for k in range(rows):
            j, a = divmod(k, sectors)
            first = x * width + (a * tiles + j) * lanes
            flat_ref[:, first : first + lanes] = plane_ref[
                x, pl.ds(k, comps, stride=rows), :
            ].astype(BF16)
    for copy in copies:
        copy.wait()
    op_ref[:, :comps] = volume_ref[...]
    op_ref[:, comps : comps + 2 * faces] = lift_ref[:, : 2 * faces]
    face = lax.broadcasted_iota(jnp.int32, (2 * faces, comps), 0)
    comp = lax.broadcasted_iota(jnp.int32, (2 * faces, comps), 1)
    upper = (face < faces).astype(jnp.int32) * (NODE - 1)
    row = jnp.where(face < faces, face, face - faces)
    sector_at = quotient(row, NODE) * group + remainder(row, NODE) + upper * NODE
    radial_at = row * NODE + upper
    first = comps + 2 * faces
    for at, start in ((sector_at, 2 * faces), (radial_at, 4 * faces)):
        place = (comp == at).astype(F32).astype(BF16)
        op_ref[:, first : first + comps] = jnp.dot(
            lift_ref[:, start : start + 2 * faces], place, preferred_element_type=F32
        ).astype(BF16)
        first += comps
    edge_ref[:, :faces] = lift_ref[:, 2 * faces : 3 * faces]
    edge_ref[:, LANES : LANES + faces] = lift_ref[:, 3 * faces : 4 * faces]

    blocks, window, _ = weights_ref.shape
    samples = jnp.concatenate([samples_ref[...]] * blocks, axis=1)
    owner = lax.broadcasted_iota(jnp.int32, (blocks, blocks * window), 0)
    entry = lax.broadcasted_iota(jnp.int32, (blocks, blocks * window), 1)
    chosen = jnp.where(owner == quotient(entry, window), samples, 0.0)
    stacked = weights_ref[...].reshape(blocks * window, window)
    v_ref[...] = sum(
        jnp.dot(part, stacked, preferred_element_type=F32) for part in split(chosen)
    )
    points = hot_ref.shape[0]
    within = lax.broadcasted_iota(jnp.int32, (lanes, points), 0)
    host = host_ref[...]
    hot_ref[...] = jnp.transpose((within == remainder(host, lanes)).astype(F32)).astype(BF16)
    row_ref[...] = (
        quotient(host, rows * lanes) * rows
        + remainder(quotient(host, lanes), tiles) * sectors
        + remainder(quotient(host, lanes * tiles), sectors)
    )

    line = lax.broadcasted_iota(jnp.int32, (comps, comps), 0)
    cross = lax.broadcasted_iota(jnp.int32, (comps, comps), 1)
    diagonal = jnp.where(line == cross, profile_ref[...].reshape(1, comps), 0.0)
    ones = jnp.ones((comps, lanes), BF16)
    high, low = split(diagonal)
    lowest = (diagonal - high.astype(F32) - low.astype(F32)).astype(BF16)
    column = sum(
        jnp.dot(part, ones, preferred_element_type=F32) for part in (high, low, lowest)
    )
    for k in range(rows):
        spread_ref[pl.ds(k, comps, stride=rows), :] = column


def planes_kernel(
    first_plane,
    planes,
    sectors,
    flat_ref,
    op_ref,
    swapped_ref,
    second_ref,
    *refs,
):
    out_refs = refs[:-1]
    stack_ref = refs[-1]
    comps = flat_ref.shape[0]
    width = flat_ref.shape[1] // planes
    group = NODE * NODE
    faces = NVAR * group
    block = width // sectors
    tiles = block // LANES
    rows = sectors * tiles
    comp = lax.broadcasted_iota(jnp.int32, (comps, block), 0)
    lane = lax.broadcasted_iota(jnp.int32, (comps, block), 1)
    q = remainder(quotient(comp, NODE), NODE)
    w = remainder(comp, NODE)
    q_top = (q == NODE - 1).astype(F32).astype(BF16)
    q_low = (q == 0).astype(F32).astype(BF16)
    w_top = ((w == NODE - 1) & (lane > 0)).astype(F32).astype(BF16)
    w_low = ((w == 0) & (lane < block - 1)).astype(F32).astype(BF16)
    odd = core_of() == 1

    def second(v):
        if second_ref.shape[0] == faces:
            return second_ref[v * group : (v + 1) * group, :]
        return jnp.zeros((group, width), BF16)

    def first(v):
        return swapped_ref[faces + v * group : faces + (v + 1) * group, :]

    for n, out_ref in enumerate(out_refs):
        x = first_plane + n
        here = x * width
        own = flat_ref[:, here : here + width]
        stack_ref[n, :comps, :] = own
        for v in range(NVAR):
            low_row = v * NODE * group
            top_row = low_row + (NODE - 1) * group
            at = comps + v * group
            if x > 0:
                value = flat_ref[top_row : top_row + group, here - width : here]
            else:
                value = jnp.where(odd, first(v), second(v))
            stack_ref[n, at : at + group, :] = value
            at += faces
            if x < planes - 1:
                value = flat_ref[low_row : low_row + group, here + width : here + 2 * width]
            else:
                value = jnp.where(odd, second(v), first(v))
            stack_ref[n, at : at + group, :] = value
        mix = comps + 2 * faces
        for a in range(sectors):
            at = a * block
            columns = slice(at, at + block)
            part = flat_ref[:, here + at : here + at + block]
            sector = None
            if a > 0:
                sector = q_top * flat_ref[:, here + at - block : here + at]
            if a < sectors - 1:
                right = q_low * flat_ref[:, here + at + block : here + at + 2 * block]
                sector = right if sector is None else sector + right
            if sector is None:
                sector = jnp.zeros((comps, block), BF16)
            stack_ref[n, mix : mix + comps, columns] = sector
            stack_ref[n, mix + comps :, columns] = w_top * pltpu.roll(
                part, 1, 1
            ) + w_low * pltpu.roll(part, block - 1, 1)
        result = jnp.dot(op_ref[...], stack_ref[n], preferred_element_type=F32)
        for k in range(rows):
            j, a = divmod(k, sectors)
            at = (a * tiles + j) * LANES
            out_ref[pl.ds(k, comps, stride=rows), :] = result[:, at : at + LANES] + own[
                :, at : at + LANES
            ].astype(F32)


def strength_part(v_ref, sens, radiation):
    blocks = v_ref.shape[0]
    points = radiation.shape[1]
    v_high, v_low = split(v_ref[...])
    s_high, s_low = split(sens)
    combined = jnp.dot(
        jnp.concatenate([v_high, v_low, v_high], axis=1),
        jnp.concatenate([s_high, s_high, s_low], axis=0),
        preferred_element_type=F32,
    )
    both = jnp.concatenate(split(combined), axis=0)
    product = jnp.dot(both, radiation, preferred_element_type=F32)
    product = product[:blocks] + product[blocks:]
    block = lax.broadcasted_iota(jnp.int32, (blocks, points), 0)
    point = lax.broadcasted_iota(jnp.int32, (blocks, points), 1)
    chosen = block == quotient(point, points // blocks)
    return jnp.sum(jnp.where(chosen, product, 0.0), axis=0, keepdims=True)


def sensitivity(sums, half, taper_ref, weights_ref, target_ref):
    width = sums.shape[1]
    columns = pl.ds(pl.multiple_of(half * width, width), width)
    return weights_ref[:, columns] * taper_ref[...] * (sums - target_ref[:, columns])


def own_kernel(sums_ref, taper_ref, weights_ref, target_ref, v_ref, radiation_ref, part_ref, sens_ref):
    sens = sensitivity(sums_ref[...], core_of(), taper_ref, weights_ref, target_ref)
    sens_ref[...] = sens
    part_ref[...] = strength_part(v_ref, sens, radiation_ref[...])


def final_kernel(
    sectors,
    chunks,
    other_ref,
    own_sens_ref,
    taper_ref,
    weights_ref,
    target_ref,
    v_ref,
    far_ref,
    part_ref,
    row_ref,
    hot_ref,
    spread_ref,
    edge_ref,
    crossed_ref,
    back_ref,
    *rest,
):
    planes = len(rest) - 6
    base_refs = rest[:planes]
    sens_hbm, out_hbm, sens_ref, all_ref, buffer_ref, sems = rest[planes:]
    comps, _, rows, lanes = out_hbm.shape
    tiles = rows // sectors
    block = tiles * lanes
    other_core = 1 - core_of()
    half = far_ref.shape[0]
    start = pl.multiple_of(other_core * half, half)
    sens = sensitivity(other_ref[...], other_core, taper_ref, weights_ref, target_ref)
    strength = part_ref[...] + strength_part(v_ref, sens, far_ref[...])
    at = lax.broadcasted_iota(jnp.int32, (planes * rows, strength.shape[1]), 0)
    placed = jnp.where(at == row_ref[...], strength, 0.0)
    gathered = lax.dot_general(
        jnp.concatenate(split(placed), axis=0),
        hot_ref[...],
        (((1,), (0,)), ((), ())),
        preferred_element_type=F32,
    )
    source = gathered[: planes * rows] + gathered[planes * rows :]
    faces = crossed_ref.shape[0] // 2
    top = mine_is_top()
    crossed = crossed_ref[:faces, :]
    back = back_ref[faces:, :]
    halos = (jnp.where(top, back, crossed), jnp.where(top, crossed, back))
    chunk = comps // chunks
    def output_copy(n, x):
        part = pl.ds(pl.multiple_of(n * chunk, chunk), chunk)
        return pltpu.make_async_copy(
            buffer_ref.at[x, part], out_hbm.at[part, x], sems.at[n * planes + x]
        )

    def write(n, carry):
        part = pl.ds(pl.multiple_of(n * chunk, chunk), chunk)
        lines = pl.ds(pl.multiple_of(n * chunk * rows, chunk * rows), chunk * rows)
        spread = spread_ref[lines, :].reshape(chunk, rows, lanes)
        for x in range(planes):
            buffer_ref[x, part] = (
                base_refs[x][lines, :].reshape(chunk, rows, lanes)
                + spread * source[x * rows : (x + 1) * rows][None]
            )
        for side, a in ((0, 0), (1, sectors - 1)):
            term = jnp.dot(
                edge_ref[part, side * LANES : side * LANES + faces],
                halos[side],
                preferred_element_type=F32,
            )
            for x in range(planes):
                flat_ref = buffer_ref.at[x].reshape(comps * rows, lanes)
                for j in range(tiles):
                    place = pl.ds(n * chunk * rows + j * sectors + a, chunk, stride=rows)
                    column = x * block + j * lanes
                    flat_ref[place, :] = flat_ref[place, :] + term[:, column : column + lanes]
        for x in range(planes):
            output_copy(n, x).start()
        return carry

    lax.fori_loop(0, chunks, write, 0)

    all_ref[:, pl.ds(start, half)] = sens
    all_ref[:, pl.ds(pl.multiple_of((1 - other_core) * half, half), half)] = own_sens_ref[...]
    count = sens_ref.shape[1]
    first = lax.axis_index("azim") * count
    aligned = pl.multiple_of((first // LANES) * LANES, LANES)
    window = all_ref[:, pl.ds(aligned, LANES)]
    turned = pltpu.roll(window, lax.rem(LANES - (first - aligned), LANES), 1)
    sens_ref[...] = turned[:, :count]
    sens_copy = pltpu.make_async_copy(sens_ref, sens_hbm, sems.at[chunks * planes])
    sens_copy.start()

    def finish(n, carry):
        for x in range(planes):
            output_copy(n, x).wait()
        return carry

    lax.fori_loop(0, chunks, finish, 0)
    sens_copy.wait()


def exchange(value, mask, devices):
    return lax.ppermute(value, MESH_AXES, [(i, i ^ mask) for i in range(devices)])


def body(
    surface_signal,
    retarded_weights,
    radiation_weights,
    target_signal,
    observer_weights,
    sample_weights,
    host_element,
    source_profile,
    adjoint_state,
    volume_operator,
    lift_operator,
):
    streams = lax.axis_size("stream")
    around = lax.axis_size("azim")
    devices = streams * around
    window, points = surface_signal.shape
    observers = radiation_weights.shape[0]
    half = observers // 2
    blocks = retarded_weights.shape[0]
    comps, planes, sectors, radial = adjoint_state.shape
    tiles = radial // LANES
    rows = sectors * tiles
    width = sectors * radial
    faces = NVAR * NODE * NODE
    barrier = lax.optimization_barrier
    depth = 3 * comps + 2 * faces

    view = (
        adjoint_state.reshape(comps, planes, sectors, tiles, LANES)
        .transpose(0, 1, 3, 2, 4)
        .reshape(comps, planes, rows, LANES)
    )
    small = [
        target_signal,
        observer_weights.reshape(1, observers),
        sample_weights.reshape(1, window),
        host_element.reshape(1, points),
        source_profile,
        volume_operator,
        lift_operator,
    ]
    large = [surface_signal, retarded_weights, radiation_weights, view]
    send, delayed, far, near, state, retarded, swap, mine, second = call(
        lambda *refs: start_kernel(sectors, *refs),
        [HBM] * len(large),
        [
            vmem((window, half), F32),
            vmem((window, points), BF16),
            vmem((half, points), BF16),
            vmem((half, points), BF16),
            vmem(view.shape, BF16),
            vmem(retarded_weights.shape, BF16),
            vmem((2 * faces, width), BF16),
            vmem((faces, planes * radial), BF16),
            vmem((faces if streams > 2 else 16, width), BF16),
        ],
        [in_hbm(x) for x in large],
        [
            pltpu.VMEM((window, points), BF16),
            pltpu.VMEM((faces * rows, LANES), F32),
            pltpu.SemaphoreType.DMA((5 + NODE,)),
        ],
    )
    received = exchange(send, around, devices)
    swapped = exchange(swap, around, devices)
    own = call(near_kernel, [VMEM] * 2, [vmem((window, half), F32)], [delayed, near])[0]
    low, pay = call(
        join_kernel,
        [VMEM] * 4,
        [vmem((window, half), BF16), vmem((2 * faces, planes * radial), BF16)],
        [own, received, mine, swapped],
    )
    low, pay, state = barrier((low, pay, state))

    bits = [1 << n for n in range((around - 1).bit_length())]
    bits += [around << n for n in range(1, (streams - 1).bit_length())]
    stages = []
    for first in range(0, len(bits), 2):
        pair = bits[first : first + 2]
        stages.append(pair + ([pair[0] | pair[1]] if len(pair) == 2 else []))

    inner = [(i, i ^ 1) for i in range(around)]
    outer = [(i, (i + 1 if i % 2 else i - 1) % around) for i in range(around)]
    pairs = []
    for s in range(streams):
        pairs += [(s * around + i, s * around + j) for i, j in (outer if s % 2 else inner)]
    crossed = lax.ppermute(pay, MESH_AXES, pairs)
    parts = [exchange(low, mask, devices) for mask in stages[0]]
    if streams > 2:
        links = [(s, s + 1) for s in range(1, streams - 1, 2)]
        second = lax.ppermute(second, "stream", links + [(b, a) for a, b in links])
    flat, operator, edge, v, hot, row, spread, target, weights = call(
        lambda *refs: prepare_kernel(sectors, *refs),
        [VMEM] * 2 + [HBM] * len(small),
        [
            vmem((comps, planes * width), BF16),
            vmem((comps, depth), BF16),
            vmem((comps, 2 * LANES), BF16),
            vmem((blocks, window), F32),
            vmem((points, LANES), BF16),
            vmem((1, points), jnp.int32),
            vmem((comps * rows, LANES), F32),
            vmem(target_signal.shape, F32),
            vmem((1, observers), F32),
        ],
        [state, retarded] + [in_hbm(x) for x in small],
        [pltpu.VMEM((planes, comps * rows, LANES), F32)]
        + [pltpu.VMEM(x.shape, x.dtype) for x in small[2:]]
        + [pltpu.SemaphoreType.DMA((len(small),))],
        nbytes=12 * 2**20,
    )

    def combine(low, parts):
        total = low.astype(F32) + parts[0].astype(F32)
        if len(parts) == 3:
            total = total + (parts[1].astype(F32) + parts[2].astype(F32))
        return total

    parts, flat = barrier((parts, flat))
    sums = combine(low, parts)
    low = sums.astype(BF16)

    def run_planes(first, count):
        return call(
            lambda *refs: planes_kernel(first, planes, sectors, *refs),
            [VMEM] * 4,
            [vmem((comps * rows, LANES), F32)] * count,
            [flat, operator, swapped, second],
            [pltpu.VMEM((count, depth, width), BF16)],
            flops=2 * comps * depth * width * count,
            nbytes=count * 4 * 2**20,
        )

    bases = []
    for masks in stages[1:]:
        parts = [exchange(low, mask, devices) for mask in masks]
        if not bases:
            bases = list(run_planes(0, planes // 2)) + list(run_planes(planes // 2, planes // 2))
            parts, bases = barrier((parts, bases))
        sums = combine(low, parts)
        low = sums.astype(BF16)

    remote = exchange(sums, around, devices)
    crossed, bases = barrier((crossed, bases))
    back = exchange(crossed, around, devices)
    taper = np.arange(window, dtype=np.float64)
    taper = (0.5 - 0.5 * np.cos(2.0 * np.pi * (taper + 0.5) / window)).astype(np.float32)
    taper = jnp.asarray(taper).reshape(window, 1)
    part, own_sens = call(
        own_kernel,
        [VMEM] * 6,
        [vmem((1, points), F32), vmem((window, half), F32)],
        [sums, taper, weights, target, v, near],
        flops=2 * 2 * blocks * half * points,
        nbytes=half * points * 2,
    )
    chunks = 5
    sens, updated = call(
        lambda *refs: final_kernel(sectors, chunks, *refs),
        [VMEM] * (14 + planes),
        [
            jax.ShapeDtypeStruct((window, observers // around), F32),
            jax.ShapeDtypeStruct(view.shape, F32),
        ],
        [remote, own_sens, taper, weights, target, v, far, part, row, hot, spread]
        + [edge, crossed, back]
        + list(bases),
        [
            pltpu.VMEM((window, observers // around), F32),
            pltpu.VMEM((window, observers), F32),
            pltpu.VMEM((planes, comps, rows, LANES), F32),
            pltpu.SemaphoreType.DMA((chunks * planes + 1,)),
        ],
        nbytes=12 * 2**20,
        out_specs=[HBM, HBM],
    )
    updated = (
        updated.reshape(comps, planes, tiles, sectors, LANES)
        .transpose(0, 1, 3, 2, 4)
        .reshape(adjoint_state.shape)
    )
    return sens, updated


def solution(mesh):
    return jax.shard_map(
        body,
        mesh=mesh,
        in_specs=(
            P(None, ("stream", "azim")),
            P(("stream", "azim"), None, None),
            P(None, ("stream", "azim")),
            P(),
            P(),
            P(),
            P(("stream", "azim")),
            P(),
            P(None, "stream", "azim", None),
            P(),
            P(),
        ),
        out_specs=(P(None, "azim"), P(None, "stream", "azim", None)),
        check_vma=False,
    )
```
